32 devices in a mesh: dp: 16 (over z, y, x), tp: 2 (over core).
Axes of the slice: x: 2, y: 2, z: 4, core: 2. Of those that a mesh axis runs over, the one named last changes fastest.
Arguments:
- inputs: bfloat16 [76800, 512], P(('dp', 'tp')), may hold values from -6 to 6
- page_of: int32 [76800], P('dp'), may hold values from 0 to 3071, as said below
- rel_index: int32 [100, 100], replicated, may hold values from 0 to 360, as said below
- w_qkv: bfloat16 [3, 512, 512], P(None, None, 'tp'), may hold values from -0.25 to 0.25
- qv_bias: float32 [2, 512], P(None, 'tp'), may hold values from -1.5 to 1.5
- w_proj: bfloat16 [512, 512], P('tp'), may hold values from -1 to 1
- w_fc1: bfloat16 [512, 2048], P(None, 'tp'), may hold values from -0.25 to 0.25
- fc1_bias: float32 [2048], P('tp'), may hold values from -1.5 to 1.5
- w_fc2: bfloat16 [2048, 512], P('tp'), may hold values from -0.125 to 0.125
- out_biases: float32 [2, 512], replicated, may hold values from -1.5 to 1.5
- norm_gains: float32 [2, 512], replicated, may hold values from 0.1 to 1.9
- norm_biases: float32 [2, 512], replicated, may hold values from -1.5 to 1.5
- bias_table: float32 [361, 16], P(None, 'tp'), may hold values from -3 to 3
- out_grad: bfloat16 [76800, 512], P(('dp', 'tp')), may hold values from -6 to 6
Outputs:
- block_out: bfloat16 [76800, 512], P(('dp', 'tp'))
- grad_in: bfloat16 [76800, 512], P(('dp', 'tp'))
- g_qkv: float32 [3, 512, 512], P(None, None, 'tp')
- g_qv_bias: float32 [2, 512], P(None, 'tp')
- g_proj: float32 [512, 512], P('tp')
- g_fc1: float32 [512, 2048], P(None, 'tp')
- g_fc1_bias: float32 [2048], P('tp')
- g_fc2: float32 [2048, 512], P('tp')
- g_out_biases: float32 [2, 512], replicated
- g_norm_gains: float32 [2, 512], replicated
- g_norm_biases: float32 [2, 512], replicated
- g_table: float32 [361, 16], P(None, 'tp')
The draws below stay inside these ranges and needn't reach their ends.
Inputs may be any that keep to these rules, and one draw needn't show every extreme that they name: `page_of`: within each window (100 consecutive patches, row-major), the regions are the rectangles cut by one row boundary and one column boundary; no two windows share a region. `rel_index`: entry [i, j] depends only on the offset of position i from position j within a window, each of the 361 offsets with its own table row.
All inputs are finite; a program needn't handle non-finite values.
Results may differ from the reference program's by a relative error of at most 0.015.
Values may be sent and summed in bfloat16 or wider, within the bound.
No kernel may reach another device: no remote copies, remote signals or barrier semaphores. Data moves between devices by JAX's collectives and lax.ppermute only.
A program may use at most 256 MiB of HBM per device.

```python
import jax
import jax.numpy as jnp
from jax import lax

D = 512
HEADS = 16
FF = 2048
WS = 10
HEAD = 32
TOKENS = 76800
TAB = 361


def draw_page_of(key, part):
    key = jax.random.fold_in(key, 11)
    windows_all = TOKENS // (WS * WS)
    cuts = jax.random.randint(key, (windows_all, 2), 0, WS)
    position = jnp.arange(WS * WS, dtype=jnp.int32)
    row_side = (position[None, :] // WS >= cuts[:, 0:1]).astype(jnp.int32)
    col_side = (position[None, :] % WS >= cuts[:, 1:2]).astype(jnp.int32)
    base_id = 4 * jnp.arange(windows_all, dtype=jnp.int32)[:, None]
    return (base_id + 2 * row_side + col_side).reshape(-1)


def draw_rel_index(key, part):
    key = jax.random.fold_in(key, 23)
    span_size = 2 * WS - 1
    position = jnp.arange(WS * WS, dtype=jnp.int32)
    row_off = position[:, None] // WS - position[None, :] // WS + WS - 1
    col_off = position[:, None] % WS - position[None, :] % WS + WS - 1
    relabel = jax.random.permutation(key, span_size * span_size).astype(jnp.int32)
    return relabel[row_off * span_size + col_off]


def steps_of(key, shape, cuts, least, largest):
    gain, own = 1.0, jax.random.fold_in(key, 6)
    for dim, parts in cuts:
        draws = jnp.exp(jax.random.uniform(jax.random.fold_in(own, dim), (parts,), jnp.float32, least / len(cuts), largest / len(cuts)))
        gain = gain * jnp.repeat(draws, shape[dim] // parts).reshape([-1 if axis == dim else 1 for axis in range(len(shape))])
    return gain


def normal_values(stream_key, shape, width, reach, split=(), kind=jnp.bfloat16):
    values = jax.random.normal(stream_key, shape, jnp.float32) * width
    if len(split) > 0:
        values = steps_of(stream_key, shape, split, -0.22, 0.18) * values
    return jnp.clip(values, min=-reach, max=reach).astype(kind)


def setup_inputs(seed: int = 0) -> dict:
    streams_of = jax.random.split(jax.random.key(seed), 15)
    inputs = normal_values(streams_of[0], (TOKENS, D), 1.0, 6.0, ((0, 32),))
    page_of = draw_page_of(jax.random.fold_in(streams_of[14], 71), 0)
    rel_index = draw_rel_index(jax.random.fold_in(streams_of[14], 71), 0)
    w_qkv = normal_values(streams_of[3], (3, D, D), D ** -0.5, 0.25, ((2, 2),))
    qv_bias = normal_values(streams_of[4], (2, D), 0.3, 1.5, ((1, 2),), jnp.float32)
    w_proj = normal_values(streams_of[5], (D, D), (D // 16) ** -0.5, 1.0, ((0, 2),))
    w_fc1 = normal_values(streams_of[6], (D, FF), D ** -0.5, 0.25, ((1, 2),))
    fc1_bias = normal_values(streams_of[7], (FF,), 0.3, 1.5, ((0, 2),), jnp.float32)
    w_fc2 = normal_values(streams_of[8], (FF, D), FF ** -0.5, 0.125, ((0, 2),))
    out_biases = normal_values(streams_of[9], (2, D), 0.3, 1.5, (), jnp.float32)
    norm_gains = jnp.clip(1.0 + 0.18 * jax.random.normal(streams_of[10], (2, D), jnp.float32), 0.1, 1.9)
    norm_biases = normal_values(streams_of[11], (2, D), 0.3, 1.5, (), jnp.float32)
    bias_table = normal_values(streams_of[12], (TAB, HEADS), 1.0, 3.0, ((1, 2),), jnp.float32)
    out_grad = normal_values(streams_of[13], (TOKENS, D), 1.0, 6.0, ((0, 32),))
    return dict(inputs=inputs, page_of=page_of, rel_index=rel_index, w_qkv=w_qkv, qv_bias=qv_bias, w_proj=w_proj, w_fc1=w_fc1, fc1_bias=fc1_bias, w_fc2=w_fc2, out_biases=out_biases, norm_gains=norm_gains, norm_biases=norm_biases, bias_table=bias_table, out_grad=out_grad)


@jax.custom_vjp
def low(v):
    return lax.optimization_barrier(v.astype(jnp.bfloat16)).astype(jnp.float32)

@jax.custom_vjp
def low_back(v):
    return v

def low_keep(v):
    return (low(v), None)

def low_pass(kept, grad):
    return (grad,)

def back_keep(v):
    return (v, None)

def back_low(kept, grad):
    return (low(grad),)
low.defvjp(low_keep, low_pass)
low_back.defvjp(back_keep, back_low)
EPS = 1e-05
HIGH = lax.Precision.HIGHEST

def layer_norm(values_in, gain_row, shift_row):
    row_mean = lax.optimization_barrier(jnp.mean(values_in, axis=-1, keepdims=True))
    centered = values_in - row_mean
    variance = lax.optimization_barrier(jnp.mean(centered * centered, axis=-1, keepdims=True))
    return centered * lax.rsqrt(variance + EPS) * gain_row + shift_row

def matmul(left, right):
    return jnp.dot(left, right, precision=HIGH)

def forward(params, inputs, pages, rel_index):
    w_qkv, qv_bias, w_proj, w_fc1, fc1_bias, w_fc2, out_biases, norm_gains, norm_biases, bias_table = params
    windows_here = inputs.shape[0] // (WS * WS)
    normed = low(layer_norm(inputs, norm_gains[0], norm_biases[0]))
    query = low(low_back(matmul(normed, w_qkv[0]) + qv_bias[0]))
    keys = low(low_back(matmul(normed, w_qkv[1])))
    values = low(low_back(matmul(normed, w_qkv[2]) + qv_bias[1]))
    split_shape = (windows_here, WS * WS, HEADS, HEAD)
    query = query.reshape(split_shape)
    keys = keys.reshape(split_shape)
    values = values.reshape(split_shape)
    table_bias = jnp.transpose(bias_table[rel_index], (2, 0, 1))
    scores = jnp.einsum('wqhd,wkhd->whqk', query, keys, precision=HIGH) * HEAD ** (-0.5) + table_bias[None]
    scores = low_back(scores)
    page_rows = pages.reshape(windows_here, WS * WS)
    same_page = page_rows[:, :, None] == page_rows[:, None, :]
    scores = jnp.where(same_page[:, None], scores, -1e+30)
    weights_p = low(jax.nn.softmax(scores, axis=-1))
    attended = jnp.einsum('whqk,wkhd->wqhd', weights_p, values, precision=HIGH).reshape(-1, D)
    attended = low(low_back(attended))
    mixed = inputs + low_back(matmul(attended, w_proj)) + out_biases[0]
    normed2 = low(layer_norm(mixed, norm_gains[1], norm_biases[1]))
    hidden = low_back(matmul(normed2, w_fc1) + fc1_bias)
    active = low(jax.nn.gelu(hidden, approximate=False))
    return mixed + low_back(matmul(active, w_fc2)) + out_biases[1]

def reference(inputs, page_of, rel_index, w_qkv, qv_bias, w_proj, w_fc1, fc1_bias, w_fc2, out_biases, norm_gains, norm_biases, bias_table, out_grad):
    params = (w_qkv.astype(jnp.float32), qv_bias, w_proj.astype(jnp.float32), w_fc1.astype(jnp.float32), fc1_bias, w_fc2.astype(jnp.float32), out_biases, norm_gains, norm_biases, bias_table)
    block_rows = 8 * WS * WS
    steps_all = TOKENS // block_rows
    input_blocks = inputs.astype(jnp.float32).reshape(steps_all, block_rows, D)
    page_blocks = page_of.reshape(steps_all, block_rows)
    grad_blocks = out_grad.astype(jnp.float32).reshape(steps_all, block_rows, D)

    def one_block(running, block_item):
        input_block, page_block, grad_block = block_item
        out_block, pull_back = jax.vjp(lambda param_set, input_set: forward(param_set, input_set, page_block, rel_index), params, input_block)
        param_grads, input_grads = pull_back(grad_block)
        running = jax.tree.map(jnp.add, running, param_grads)
        return (running, (out_block.astype(jnp.bfloat16), input_grads.astype(jnp.bfloat16)))
    start_sums = jax.tree.map(jnp.zeros_like, params)
    sums_all, (out_all, grad_all) = lax.scan(one_block, start_sums, (input_blocks, page_blocks, grad_blocks))
    return (out_all.reshape(TOKENS, D), grad_all.reshape(TOKENS, D), sums_all[0], sums_all[1], sums_all[2], sums_all[3], sums_all[4], sums_all[5], sums_all[6], sums_all[7], sums_all[8], sums_all[9])
```

```python
import functools

import jax
import jax.numpy as jnp
from jax import lax
from jax.experimental import pallas as pl
from jax.experimental.pallas import tpu as pltpu
from jax.sharding import PartitionSpec as P

HEAD = 32
EPS = 1e-05
WIN = 100
KEYS = 104
LANES = 128
SLAB = 256
GROUP = 4
ROWS = GROUP * WIN
LOG2E = 1.4426950408889634
NEG = -1e30
BF = jnp.bfloat16
F32 = jnp.float32
NT = (((1,), (1,)), ((), ()))
TN = (((0,), (0,)), ((), ()))


def dot(a, b):
    return jnp.dot(a, b, preferred_element_type=F32)


def dot_nt(a, b):
    return lax.dot_general(a, b, NT, preferred_element_type=F32)


def dot_tn(a, b):
    return lax.dot_general(a, b, TN, preferred_element_type=F32)


def norm_parts(v):
    mean = jnp.mean(v, axis=-1, keepdims=True)
    centered = v - mean
    var = jnp.mean(centered * centered, axis=-1, keepdims=True)
    r = lax.rsqrt(var + EPS)
    return centered * r, r


def fold_rows(v):
    rows, cols = v.shape
    return jnp.sum(v.reshape(rows // 8, 8, cols), axis=0)


def lane_mask(rows, test):
    lane = lax.broadcasted_iota(jnp.int32, (rows, SLAB), 1)
    return jnp.where(test(lane), 1.0, 0.0).astype(BF)


def attn_fwd_body(
    x_ref, page_ref, wa_ref, wb_ref, qva_ref, qvb_ref, bias_ref, pa_ref, pb_ref, ob_ref, gain_ref, shift_ref,
    mixed_ref, att_ref, n_ref, qkv_ref, p_ref,
    scr, att_scr,
):
    scale = (HEAD ** -0.5) * LOG2E

    @pl.when(pl.program_id(0) == 0)
    def _():
        scr[ROWS:, :] = jnp.zeros((scr.shape[0] - ROWS, scr.shape[1]), F32)

    x = x_ref[...].astype(F32)
    n, _ = norm_parts(x)
    n = (n * gain_ref[0:1] + shift_ref[0:1]).astype(BF)
    n_ref[...] = n
    for s, (w_ref, b_ref) in enumerate(((wa_ref, qva_ref), (wb_ref, qvb_ref))):
        lo = s * SLAB
        scr[:ROWS, lo : lo + SLAB] = dot(n, w_ref[0]) + b_ref[0:1]
        scr[:ROWS, 512 + lo : 512 + lo + SLAB] = dot(n, w_ref[1])
        scr[:ROWS, 1024 + lo : 1024 + lo + SLAB] = dot(n, w_ref[2]) + b_ref[1:2]
    for w in range(GROUP):
        qkv_ref[w] = scr[w * WIN : w * WIN + LANES, :].astype(BF)

    even = lane_mask(LANES, lambda c: (c // HEAD) % 2 == 0)
    odd = lane_mask(LANES, lambda c: (c // HEAD) % 2 == 1)
    low = lane_mask(KEYS, lambda c: c % 128 < 64)[:, :128]
    high = lane_mask(KEYS, lambda c: c % 128 >= 64)[:, :128]
    query_lane = lax.broadcasted_iota(jnp.int32, (1, SLAB), 1) % LANES
    valid = jnp.where(query_lane < WIN, 1.0, 0.0)
    first_head = lax.broadcasted_iota(jnp.int32, (2 * HEAD, LANES), 0) < HEAD

    def window(w, carry):
        pages = jnp.broadcast_to(page_ref[w], (LANES, LANES))
        mask = jnp.where(pages == pages.T, 0.0, NEG)[:KEYS]
        mask = jnp.concatenate([mask, mask], axis=1)
        for s in range(2):
            lo = s * SLAB
            q = qkv_ref[w, :, lo : lo + SLAB]
            k = qkv_ref[w, :KEYS, 512 + lo : 512 + lo + SLAB]
            v = qkv_ref[w, :, 1024 + lo : 1024 + lo + SLAB]
            q2 = jnp.concatenate([q * even, q * odd], axis=0)
            v_t = v.T
            outs = []
            for p in range(4):
                g = p // 2
                kp = k[:, 128 * g : 128 * g + 128] * (low if p % 2 == 0 else high)
                st = dot_nt(kp, q2[:, 128 * g : 128 * g + 128])
                st = st * scale + bias_ref[4 * s + p] + mask
                peak = jnp.max(st, axis=0, keepdims=True)
                e = jnp.exp2(st - peak)
                total = jnp.sum(e, axis=0, keepdims=True)
                pt = (e * (valid / total)).astype(BF)
                p_ref[w, 4 * s + p] = pt
                ot = dot(v_t[64 * p : 64 * p + 64, :KEYS], pt)
                outs.append(jnp.where(first_head, ot[:, :LANES], ot[:, LANES:]))
            att_scr[w, :, lo : lo + SLAB] = jnp.concatenate(outs, axis=0).T
        return carry

    lax.fori_loop(0, GROUP, window, 0)
    for w in range(GROUP):
        scr[w * WIN : w * WIN + WIN, :512] = att_scr[w, :WIN, :]
    att = scr[:ROWS, :512].astype(BF)
    att_ref[...] = att
    mixed_ref[...] = x + ob_ref[0:1] + dot(att[:, :SLAB], pa_ref[...]) + dot(att[:, SLAB:], pb_ref[...])


def gelu_parts(h):
    e = jnp.exp2(h * h * (-0.5 * LOG2E))
    t = 1.0 / (1.0 + (0.3275911 * 0.7071067811865476) * jnp.abs(h))
    poly = t * (
        0.5 * 0.254829592
        + t * (0.5 * -0.284496736 + t * (0.5 * 1.421413741 + t * (0.5 * -1.453152027 + t * (0.5 * 1.061405429))))
    )
    tail = poly * e
    phi = jnp.where(h >= 0, 1.0 - tail, tail)
    return phi, e * 0.3989422804014327


def ffn_body(
    mixed_ref, go_ref, att_ref, w1a_ref, w1b_ref, w2a_ref, w2b_ref, b1a_ref, b1b_ref, ob_ref, gain_ref, shift_ref,
    out_ref, gm_ref, gml_ref, g1_ref, g2_ref, gp_ref, gb1_ref, gs_ref,
    acc1, acc2, accp, accb, accs,
):
    step = pl.program_id(0)

    @pl.when(step == 0)
    def _():
        acc1[...] = jnp.zeros_like(acc1)
        acc2[...] = jnp.zeros_like(acc2)
        accp[...] = jnp.zeros_like(accp)
        accb[...] = jnp.zeros_like(accb)
        accs[...] = jnp.zeros_like(accs)

    mixed = mixed_ref[...]
    nh, r = norm_parts(mixed)
    n2 = (nh * gain_ref[1:2] + shift_ref[1:2]).astype(BF)
    go = go_ref[...]
    y = mixed + ob_ref[1:2]
    gn = jnp.zeros_like(mixed)
    for c in range(4):
        w1_ref, w2_ref, b1_ref = (w1a_ref, w2a_ref, b1a_ref) if c < 2 else (w1b_ref, w2b_ref, b1b_ref)
        col = slice(512 * (c % 2), 512 * (c % 2) + 512)
        full = slice(512 * c, 512 * c + 512)
        h = dot(n2, w1_ref[:, col]) + b1_ref[0:1, col]
        ga = dot_nt(go, w2_ref[col, :])
        phi, density = gelu_parts(h)
        act = (h * phi).astype(BF)
        ghf = ga * (phi + h * density)
        gh = ghf.astype(BF)
        y += dot(act, w2_ref[col, :])
        gn += dot_nt(gh, w1_ref[:, col])
        acc2[full, :] += dot_tn(act, go)
        acc1[:, full] += dot_tn(n2, gh)
        accb[:, full] += fold_rows(ghf)
    out_ref[...] = y.astype(BF)
    gof = go.astype(F32)
    e = gn * gain_ref[1:2]
    gm = gof + r * (
        e - jnp.mean(e, axis=-1, keepdims=True) - nh * jnp.mean(e * nh, axis=-1, keepdims=True)
    )
    gm_ref[...] = gm
    gml = gm.astype(BF)
    gml_ref[...] = gml
    accp[...] += dot_tn(att_ref[...], gml)
    accs[0] += fold_rows(gm)
    accs[1] += fold_rows(gof)
    accs[2] += fold_rows(gn * nh)
    accs[3] += fold_rows(gn)

    @pl.when(step == pl.num_programs(0) - 1)
    def _():
        g1_ref[...] = acc1[...].astype(BF)
        g2_ref[...] = acc2[...].astype(BF)
        gp_ref[...] = accp[...].astype(BF)
        gb1_ref[...] = accb[...]
        gs_ref[...] = accs[...]


def attn_bwd_body(
    x_ref, n_ref, gm_ref, gml_ref, qkv_ref, p_ref, wa_ref, wb_ref, pa_ref, pb_ref, gain_ref,
    gin_ref, gqkv_ref, gt_ref, gqv_ref, gs_ref,
    scr, dpad, acc, acct, accb, accs,
):
    step = pl.program_id(0)
    scale = HEAD ** -0.5

    @pl.when(step == 0)
    def _():
        scr[ROWS:, :] = jnp.zeros((scr.shape[0] - ROWS, scr.shape[1]), F32)
        acc[...] = jnp.zeros_like(acc)
        acct[...] = jnp.zeros_like(acct)
        accb[...] = jnp.zeros_like(accb)
        accs[...] = jnp.zeros_like(accs)

    gml = gml_ref[...]
    scr[:ROWS, :SLAB] = dot_nt(gml, pa_ref[...])
    scr[:ROWS, SLAB : 2 * SLAB] = dot_nt(gml, pb_ref[...])
    row = lax.broadcasted_iota(jnp.int32, (LANES, 512), 0)
    for w in range(GROUP):
        dpad[w, :, :512] = jnp.where(row < WIN, scr[w * WIN : w * WIN + LANES, :512], 0.0)

    even = lane_mask(LANES, lambda c: (c // HEAD) % 2 == 0)
    odd = lane_mask(LANES, lambda c: (c // HEAD) % 2 == 1)
    low = lane_mask(KEYS, lambda c: c % 128 < 64)[:, :128]
    high = lane_mask(KEYS, lambda c: c % 128 >= 64)[:, :128]
    first_head = lax.broadcasted_iota(jnp.int32, (2 * HEAD, LANES), 0) < HEAD
    first_pair = lax.broadcasted_iota(jnp.int32, (KEYS, 128), 1) < 64

    def window(w, carry):
        for s in range(2):
            lo = s * SLAB
            q = qkv_ref[w, :, lo : lo + SLAB]
            k = qkv_ref[w, :, 512 + lo : 512 + lo + SLAB]
            v = qkv_ref[w, :KEYS, 1024 + lo : 1024 + lo + SLAB]
            do = dpad[w, :, lo : lo + SLAB].astype(BF)
            q2 = jnp.concatenate([q * even, q * odd], axis=0)
            d2 = jnp.concatenate([do * even, do * odd], axis=0)
            k_t = k.T
            outs, dks, dvs = [], [], []
            for p in range(4):
                g = p // 2
                cols = slice(128 * g, 128 * g + 128)
                vp = v[:, cols] * (low if p % 2 == 0 else high)
                dp = dot_nt(vp, d2[:, cols])
                pt = p_ref[w, 4 * s + p]
                ptf = pt.astype(F32)
                centre = jnp.sum(dp * ptf, axis=0, keepdims=True)
                ds = ptf * (dp - centre)
                acct[4 * s + p] += ds
                ds = ds.astype(BF)
                qt = dot(k_t[64 * p : 64 * p + 64, :KEYS], ds)
                outs.append(jnp.where(first_head, qt[:, :LANES], qt[:, LANES:]))
                dks.append(dot(ds, q2[:, cols]))
                dvs.append(dot(pt, d2[:, cols]))
            dpad[w, :, lo : lo + SLAB] = jnp.concatenate(outs, axis=0).T * scale
            for g in range(2):
                cols = slice(512 + lo + 128 * g, 512 + lo + 128 * g + 128)
                dpad[w, :KEYS, cols] = jnp.where(first_pair, dks[2 * g], dks[2 * g + 1]) * scale
                cols = slice(1024 + lo + 128 * g, 1024 + lo + 128 * g + 128)
                dpad[w, :KEYS, cols] = jnp.where(first_pair, dvs[2 * g], dvs[2 * g + 1])
        return carry

    lax.fori_loop(0, GROUP, window, 0)
    for w in range(GROUP):
        scr[w * WIN : w * WIN + WIN, :] = dpad[w, :WIN, :]
    accb[0] += fold_rows(scr[:ROWS, :512])
    accb[1] += fold_rows(scr[:ROWS, 1024:])
    n = n_ref[...]
    gn = jnp.zeros((ROWS, 512), F32)
    for i in range(3):
        for s, w_ref in enumerate((wa_ref, wb_ref)):
            cols = slice(512 * i + SLAB * s, 512 * i + SLAB * s + SLAB)
            d = scr[:ROWS, cols].astype(BF)
            acc[2 * i + s] += dot_tn(n, d)
            gn += dot_nt(d, w_ref[i])
    nh, r = norm_parts(x_ref[...].astype(F32))
    e = gn * gain_ref[0:1]
    gin = gm_ref[...] + r * (
        e - jnp.mean(e, axis=-1, keepdims=True) - nh * jnp.mean(e * nh, axis=-1, keepdims=True)
    )
    gin_ref[...] = gin.astype(BF)
    accs[0] += fold_rows(gn * nh)
    accs[1] += fold_rows(gn)

    @pl.when(step == pl.num_programs(0) - 1)
    def _():
        for i in range(3):
            for s in range(2):
                gqkv_ref[s, i] = acc[2 * i + s].astype(BF)
        gt_ref[...] = acct[...]
        gqv_ref[...] = accb[...]
        gs_ref[...] = accs[...]


def shaped(shape, dtype):
    return jax.ShapeDtypeStruct(shape, dtype)


def whole(shape):
    return pl.BlockSpec(shape, lambda i: (0,) * len(shape))


def by_rows(*shape):
    return pl.BlockSpec((ROWS,) + shape, lambda i: (i,) + (0,) * len(shape))


def by_windows(*shape):
    return pl.BlockSpec((GROUP,) + shape, lambda i: (i,) + (0,) * len(shape))


PARAMS = pltpu.CompilerParams(vmem_limit_bytes=60 << 20, dimension_semantics=("arbitrary",))


def attn_fwd(x, pages, wa, wb, qva, qvb, bias, pa, pb, ob, gain, shift):
    rows = x.shape[0]
    windows = rows // WIN
    return pl.pallas_call(
        attn_fwd_body,
        name="attn_fwd",
        grid=(rows // ROWS,),
        in_specs=[by_rows(512), by_windows(1, LANES)] + [whole(a.shape) for a in (wa, wb, qva, qvb, bias, pa, pb, ob, gain, shift)],
        out_specs=[by_rows(512), by_rows(512), by_rows(512), by_windows(LANES, 1536), by_windows(8, KEYS, SLAB)],
        out_shape=[
            shaped((rows, 512), F32),
            shaped((rows, 512), BF),
            shaped((rows, 512), BF),
            shaped((windows, LANES, 1536), BF),
            shaped((windows, 8, KEYS, SLAB), BF),
        ],
        scratch_shapes=[pltpu.VMEM((ROWS + 32, 1536), F32), pltpu.VMEM((GROUP, LANES, 512), F32)],
        compiler_params=PARAMS,
    )(x, pages, wa, wb, qva, qvb, bias, pa, pb, ob, gain, shift)


def ffn(mixed, go, att, w1a, w1b, w2a, w2b, b1a, b1b, ob, gain, shift):
    rows = mixed.shape[0]
    small = [w1a, w1b, w2a, w2b, b1a, b1b, ob, gain, shift]
    return pl.pallas_call(
        ffn_body,
        name="feed_forward",
        grid=(rows // ROWS,),
        in_specs=[by_rows(512)] * 3 + [whole(a.shape) for a in small],
        out_specs=[by_rows(512)] * 3
        + [whole((512, 2048)), whole((2048, 512)), whole((512, 512)), whole((8, 2048)), whole((4, 8, 512))],
        out_shape=[
            shaped((rows, 512), BF),
            shaped((rows, 512), F32),
            shaped((rows, 512), BF),
            shaped((512, 2048), BF),
            shaped((2048, 512), BF),
            shaped((512, 512), BF),
            shaped((8, 2048), F32),
            shaped((4, 8, 512), F32),
        ],
        scratch_shapes=[
            pltpu.VMEM((512, 2048), F32),
            pltpu.VMEM((2048, 512), F32),
            pltpu.VMEM((512, 512), F32),
            pltpu.VMEM((8, 2048), F32),
            pltpu.VMEM((4, 8, 512), F32),
        ],
        compiler_params=PARAMS,
    )(mixed, go, att, *small)


def attn_bwd(x, n, gm, gml, qkv, probs, wa, wb, pa, pb, gain):
    rows = x.shape[0]
    return pl.pallas_call(
        attn_bwd_body,
        name="attn_bwd",
        grid=(rows // ROWS,),
        in_specs=[by_rows(512)] * 4
        + [by_windows(LANES, 1536), by_windows(8, KEYS, SLAB)]
        + [whole(a.shape) for a in (wa, wb, pa, pb, gain)],
        out_specs=[
            by_rows(512),
            whole((2, 3, 512, SLAB)),
            whole((8, KEYS, SLAB)),
            whole((2, 8, 512)),
            whole((2, 8, 512)),
        ],
        out_shape=[
            shaped((rows, 512), BF),
            shaped((2, 3, 512, SLAB), BF),
            shaped((8, KEYS, SLAB), F32),
            shaped((2, 8, 512), F32),
            shaped((2, 8, 512), F32),
        ],
        scratch_shapes=[
            pltpu.VMEM((ROWS + 32, 1536), F32),
            pltpu.VMEM((GROUP, LANES, 1536), F32),
            pltpu.VMEM((6, 512, SLAB), F32),
            pltpu.VMEM((8, KEYS, SLAB), F32),
            pltpu.VMEM((2, 8, 512), F32),
            pltpu.VMEM((2, 8, 512), F32),
        ],
        compiler_params=PARAMS,
    )(x, n, gm, gml, qkv, probs, wa, wb, pa, pb, gain)


def expand_table(rel_index, table):
    heads = table.shape[1]
    slots = jnp.arange(table.shape[0], dtype=jnp.int32)
    onehot = (rel_index.T.reshape(-1)[:, None] == slots[None, :]).astype(F32)
    bias = jnp.dot(onehot, table * LOG2E, precision=lax.Precision.HIGHEST)
    bias = bias.reshape(WIN, WIN, heads).transpose(2, 0, 1)
    bias = jnp.pad(bias, ((0, 0), (0, KEYS - WIN), (0, LANES - WIN)))
    return bias.reshape(heads // 2, 2, KEYS, LANES).transpose(0, 2, 1, 3).reshape(heads // 2, KEYS, SLAB)


def table_grad(rel_index, gt):
    pairs = gt.shape[0]
    g = gt.reshape(pairs, KEYS, 2, LANES)[:, :WIN, :, :WIN].transpose(0, 2, 1, 3).reshape(2 * pairs, WIN * WIN)
    slots = jnp.arange(361, dtype=jnp.int32)
    onehot = (rel_index.T.reshape(-1)[:, None] == slots[None, :]).astype(F32)
    return jnp.einsum("pt,hp->th", onehot, g, precision=lax.Precision.HIGHEST)


SWAP = [(0, 1), (1, 0)]


def dp_exchanges(size):
    bit = 1
    while bit < size:
        yield [(i, i ^ bit) for i in range(size)]
        bit *= 2


def all_sum(v, size, over_tp):
    if over_tp:
        v = v + lax.ppermute(v, "tp", SWAP)
    for perm in dp_exchanges(size):
        v = v + lax.ppermute(v, "dp", perm)
    return v


def local_block(x, pages, rel_index, wa, wb, qva, qvb, pa, pb, w1a, w1b, b1a, b1b, w2a, w2b, ob, gain, shift, ta, tb, go):
    bias = expand_table(rel_index, jnp.concatenate([ta, tb], axis=1))
    mixed, att, n, qkv, probs = attn_fwd(x, pages, wa, wb, qva, qvb, bias, pa, pb, ob, gain, shift)
    out, gm, gml, g1, g2, gp, gb1, gs2 = ffn(mixed, go, att, w1a, w1b, w2a, w2b, b1a, b1b, ob, gain, shift)
    gin, gqkv, gt, gqv, gs1 = attn_bwd(x, n, gm, gml, qkv, probs, wa, wb, pa, pb, gain)
    g_table = table_grad(rel_index, gt)
    return out, gin, g1, g2, gp, gqkv, gb1.sum(0), gs2.sum(1), gqv.sum(1), gs1.sum(1), g_table


def per_device(
    dp_size, inputs, page_of, rel_index, w_qkv, qv_bias, w_proj, w_fc1, fc1_bias, w_fc2, out_biases, norm_gains,
    norm_biases, bias_table, out_grad,
):
    me = lax.axis_index("tp")
    windows = inputs.shape[0] // WIN
    swap = lambda v: lax.ppermute(v, "tp", SWAP)
    pages = lax.dynamic_slice_in_dim(page_of.reshape(2 * windows, WIN), me * windows, windows, 0)
    pages = jnp.pad(pages.astype(F32), ((0, 0), (0, LANES - WIN)), constant_values=-1.0)[:, None, :]
    res = local_block(
        inputs, pages, rel_index, w_qkv, swap(w_qkv), qv_bias, swap(qv_bias), w_proj, swap(w_proj),
        w_fc1, swap(w_fc1), fc1_bias[None], swap(fc1_bias)[None], w_fc2, swap(w_fc2), out_biases, norm_gains,
        norm_biases, bias_table, swap(bias_table), out_grad,
    )
    out, gin, g1, g2, gp, gqkv, gb1, gs2, gqv, gs1, g_table = res
    add = lambda mine, other: all_sum(mine + swap(other), dp_size, False).astype(F32)
    g_qkv = add(gqkv[0], gqkv[1])
    g_proj = add(gp[:SLAB], gp[SLAB:])
    g_fc1 = add(g1[:, :1024], g1[:, 1024:])
    g_fc2 = add(g2[:1024], g2[1024:])
    g_fc1_bias = add(gb1[:1024], gb1[1024:])
    g_qv_bias = add(gqv[:, :SLAB], gqv[:, SLAB:])
    g_tab = add(g_table[:, :8], g_table[:, 8:])
    shared = all_sum(jnp.concatenate([gs2, gs1]), dp_size, True)
    g_out_biases = shared[0:2]
    g_gains = jnp.stack([shared[4], shared[2]])
    g_shifts = jnp.stack([shared[5], shared[3]])
    return out, gin, g_qkv, g_qv_bias, g_proj, g_fc1, g_fc1_bias, g_fc2, g_out_biases, g_gains, g_shifts, g_tab


def solution(mesh):
    rows = P(("dp", "tp"), None)
    placed = (
        rows, P("dp"), P(), P(None, None, "tp"), P(None, "tp"), P("tp", None), P(None, "tp"), P("tp"),
        P("tp", None), P(), P(), P(), P(None, "tp"), rows,
    )
    results = (
        rows, rows, P(None, None, "tp"), P(None, "tp"), P("tp", None), P(None, "tp"), P("tp"), P("tp", None),
        P(), P(), P(), P(None, "tp"),
    )
    return jax.shard_map(
        functools.partial(per_device, mesh.shape["dp"]), mesh=mesh, in_specs=placed, out_specs=results, check_vma=False
    )
```

```python
import functools

import jax
import jax.numpy as jnp
from jax import lax
from jax.experimental import pallas as pl
from jax.experimental.pallas import tpu as pltpu
from jax.sharding import PartitionSpec as P

HEAD = 32
EPS = 1e-05
WIN = 100
KEYS = 104
LANES = 128
SLAB = 256
GROUP = 4
ROWS = GROUP * WIN
DENSE = 480
CHUNK = 256
LOG2E = 1.4426950408889634
NEG = -1e30
BF = jnp.bfloat16
F32 = jnp.float32
NT = (((1,), (1,)), ((), ()))
TN = (((0,), (0,)), ((), ()))


def dot(a, b):
    return jnp.dot(a, b, preferred_element_type=F32)


def dot_nt(a, b):
    return lax.dot_general(a, b, NT, preferred_element_type=F32)


def dot_tn(a, b):
    return lax.dot_general(a, b, TN, preferred_element_type=F32)


def norm_parts(v):
    mean = jnp.mean(v, axis=-1, keepdims=True)
    centered = v - mean
    var = jnp.mean(centered * centered, axis=-1, keepdims=True)
    r = lax.rsqrt(var + EPS)
    return centered * r, r


def fold_rows(v):
    rows, cols = v.shape
    return jnp.sum(v.reshape(rows // 8, 8, cols), axis=0)


def lane_mask(rows, test):
    lane = lax.broadcasted_iota(jnp.int32, (rows, SLAB), 1)
    return jnp.where(test(lane), 1.0, 0.0).astype(BF)


def attn_fwd_body(
    x_ref, page_ref, wa_ref, wb_ref, qva_ref, qvb_ref, bias_ref, pa_ref, pb_ref, ob_ref, gain_ref, shift_ref,
    mixed_ref, att_ref, n_ref, qkv_ref, p_ref,
    scr, att_scr,
):
    scale = (HEAD ** -0.5) * LOG2E

    @pl.when(pl.program_id(0) == 0)
    def _():
        scr[ROWS:, :] = jnp.zeros((scr.shape[0] - ROWS, scr.shape[1]), F32)

    x = x_ref[...].astype(F32)
    n, _ = norm_parts(x)
    n = (n * gain_ref[0:1] + shift_ref[0:1]).astype(BF)
    n_ref[...] = n
    for s, (w_ref, b_ref) in enumerate(((wa_ref, qva_ref), (wb_ref, qvb_ref))):
        lo = s * SLAB
        scr[:ROWS, lo : lo + SLAB] = dot(n, w_ref[0]) + b_ref[0:1]
        scr[:ROWS, 512 + lo : 512 + lo + SLAB] = dot(n, w_ref[1])
        scr[:ROWS, 1024 + lo : 1024 + lo + SLAB] = dot(n, w_ref[2]) + b_ref[1:2]
    for w in range(GROUP):
        qkv_ref[w] = scr[w * WIN : w * WIN + LANES, :].astype(BF)

    even = lane_mask(LANES, lambda c: (c // HEAD) % 2 == 0)
    odd = lane_mask(LANES, lambda c: (c // HEAD) % 2 == 1)
    low = lane_mask(KEYS, lambda c: c % 128 < 64)[:, :128]
    high = lane_mask(KEYS, lambda c: c % 128 >= 64)[:, :128]
    query_lane = lax.broadcasted_iota(jnp.int32, (1, SLAB), 1) % LANES
    valid = jnp.where(query_lane < WIN, 1.0, 0.0)
    first_head = lax.broadcasted_iota(jnp.int32, (2 * HEAD, LANES), 0) < HEAD

    for w in range(GROUP):
        pages = jnp.broadcast_to(page_ref[w], (LANES, LANES))
        mask = jnp.where(pages == pages.T, 0.0, NEG)[:KEYS]
        mask = jnp.concatenate([mask, mask], axis=1)
        scores, v_ts = [], []
        for s in range(2):
            lo = s * SLAB
            q = qkv_ref[w, :, lo : lo + SLAB]
            k = qkv_ref[w, :KEYS, 512 + lo : 512 + lo + SLAB]
            v_ts.append(qkv_ref[w, :, 1024 + lo : 1024 + lo + SLAB].T)
            q2 = jnp.concatenate([q * even, q * odd], axis=0)
            for p in range(4):
                cols = slice(128 * (p // 2), 128 * (p // 2) + 128)
                scores.append(dot_nt(k[:, cols] * (low if p % 2 == 0 else high), q2[:, cols]))
        for s in range(2):
            outs = []
            for p in range(4):
                st = scores[4 * s + p] * scale + bias_ref[4 * s + p] + mask
                e = jnp.exp2(st - jnp.max(st, axis=0, keepdims=True))
                pt = (e * (valid / jnp.sum(e, axis=0, keepdims=True))).astype(BF)
                p_ref[w, 4 * s + p] = pt
                ot = dot(v_ts[s][64 * p : 64 * p + 64, :KEYS], pt)
                outs.append(jnp.where(first_head, ot[:, :LANES], ot[:, LANES:]))
            att_scr[w, :, s * SLAB : s * SLAB + SLAB] = jnp.concatenate(outs, axis=0).T

    for w in range(GROUP):
        scr[w * WIN : w * WIN + WIN, :512] = att_scr[w, :WIN, :]
    att = scr[:ROWS, :512].astype(BF)
    att_ref[...] = att
    mixed_ref[...] = x + ob_ref[0:1] + dot(att[:, :SLAB], pa_ref[...]) + dot(att[:, SLAB:], pb_ref[...])


def gelu_parts(h):
    phi = 0.5 + 0.5 * lax.erf(h * 0.7071067811865476)
    return phi, jnp.exp2(h * h * (-0.5 * LOG2E)) * 0.3989422804014327


def ffn_body(
    mixed_ref, go_ref, att_ref, w1a_ref, w1b_ref, w2a_ref, w2b_ref, b1a_ref, b1b_ref, pa_ref, pb_ref, gain_ref, shift_ref,
    act_ref, gm_ref, do_ref, gf_ref, gb1_ref, gs_ref,
    acc1, acc2, accp, accb, accs,
):
    step = pl.program_id(0)

    @pl.when(step == 0)
    def _():
        acc1[...] = jnp.zeros_like(acc1)
        acc2[...] = jnp.zeros_like(acc2)
        accp[...] = jnp.zeros_like(accp)
        accb[...] = jnp.zeros_like(accb)
        accs[...] = jnp.zeros_like(accs)

    mixed = mixed_ref[...]
    nh, r = norm_parts(mixed)
    n2 = (nh * gain_ref[1:2] + shift_ref[1:2]).astype(BF)
    go = go_ref[...]
    gn = jnp.zeros_like(mixed)
    per_half = 1024 // CHUNK

    def weights(c):
        col = slice(CHUNK * (c % per_half), CHUNK * (c % per_half) + CHUNK)
        return ((w1a_ref, w2a_ref, b1a_ref) if c < per_half else (w1b_ref, w2b_ref, b1b_ref)) + (col,)

    def front(c):
        w1_ref, w2_ref, b1_ref, col = weights(c)
        return dot(n2, w1_ref[:, col]) + b1_ref[0:1, col], dot_nt(go, w2_ref[col, :])

    ready = front(0)
    for c in range(2 * per_half):
        h, ga = ready
        if c + 1 < 2 * per_half:
            ready = front(c + 1)
        w1_ref, _, _, col = weights(c)
        full = slice(CHUNK * c, CHUNK * c + CHUNK)
        phi, density = gelu_parts(h)
        act = (h * phi).astype(BF)
        act_ref[:, full] = act
        ghf = ga * (phi + h * density)
        accb[:, full] += fold_rows(ghf)
        gh = ghf.astype(BF)
        gn += dot_nt(gh, w1_ref[:, col])
        acc2[full, :] += dot_tn(act, go)
        acc1[:, full] += dot_tn(n2, gh)
    gof = go.astype(F32)
    e = gn * gain_ref[1:2]
    gm = gof + r * (
        e - jnp.mean(e, axis=-1, keepdims=True) - nh * jnp.mean(e * nh, axis=-1, keepdims=True)
    )
    gm_ref[...] = gm
    gml = gm.astype(BF)
    accp[...] += dot_tn(att_ref[...], gml)
    do_ref[:, :SLAB] = dot_nt(gml, pa_ref[...]).astype(BF)
    do_ref[:, SLAB:] = dot_nt(gml, pb_ref[...]).astype(BF)
    accs[0] += fold_rows(gm)
    accs[1] += fold_rows(gof)
    accs[2] += fold_rows(gn * nh)
    accs[3] += fold_rows(gn)

    @pl.when(step == pl.num_programs(0) - 1)
    def _():
        for s in range(2):
            gf_ref[s, :1024] = acc2[1024 * s : 1024 * s + 1024, :].astype(BF)
            gf_ref[s, 1024:1536] = acc1[:, 1024 * s : 1024 * s + 512].astype(BF)
            gf_ref[s, 1536:2048] = acc1[:, 1024 * s + 512 : 1024 * s + 1024].astype(BF)
            gf_ref[s, 2048:2304] = accp[SLAB * s : SLAB * s + SLAB, :].astype(BF)
        gb1_ref[...] = jnp.sum(accb[...], axis=0, keepdims=True)
        gs_ref[...] = jnp.sum(accs[...], axis=1)


def out_body(mixed_ref, act_ref, w2a_ref, w2b_ref, ob_ref, out_ref):
    out = mixed_ref[...] + ob_ref[1:2] + dot(act_ref[:, :1024], w2a_ref[...]) + dot(act_ref[:, 1024:], w2b_ref[...])
    out_ref[...] = out.astype(BF)


def window_bwd_body(do_ref, qkv_ref, p_ref, *refs):
    d_ref, t_ref, scr = refs[-3:]
    scale = HEAD ** -0.5

    @pl.when(pl.program_id(0) == 0)
    def _():
        t_ref[...] = refs[1][...] if len(refs) > 3 else jnp.zeros_like(t_ref)
        scr[ROWS:, :512] = jnp.zeros((scr.shape[0] - ROWS, 512), F32)

    scr[:ROWS, :512] = do_ref[...].astype(F32)
    row = lax.broadcasted_iota(jnp.int32, (LANES, 512), 0)
    dos = [jnp.where(row < WIN, scr[w * WIN : w * WIN + LANES, :512], 0.0).astype(BF) for w in range(GROUP)]

    even = lane_mask(LANES, lambda c: (c // HEAD) % 2 == 0)
    odd = lane_mask(LANES, lambda c: (c // HEAD) % 2 == 1)
    low = lane_mask(KEYS, lambda c: c % 128 < 64)[:, :128]
    high = lane_mask(KEYS, lambda c: c % 128 >= 64)[:, :128]
    first_head = lax.broadcasted_iota(jnp.int32, (2 * HEAD, LANES), 0) < HEAD
    first_pair = lax.broadcasted_iota(jnp.int32, (KEYS, 128), 1) < 64
    for w in range(GROUP):
        rows = slice(w * WIN, w * WIN + WIN)
        q2s, d2s, k_ts, dps = [], [], [], []
        for s in range(2):
            lo = s * SLAB
            q = qkv_ref[w, :, lo : lo + SLAB]
            v = qkv_ref[w, :KEYS, 1024 + lo : 1024 + lo + SLAB]
            do = dos[w][:, lo : lo + SLAB]
            q2s.append(jnp.concatenate([q * even, q * odd], axis=0))
            d2s.append(jnp.concatenate([do * even, do * odd], axis=0))
            k_ts.append(qkv_ref[w, :, 512 + lo : 512 + lo + SLAB].T)
            for p in range(4):
                cols = slice(128 * (p // 2), 128 * (p // 2) + 128)
                dps.append(dot_nt(v[:, cols] * (low if p % 2 == 0 else high), d2s[s][:, cols]))
        for s in range(2):
            lo = s * SLAB
            outs, dks, dvs = [], [], []
            for p in range(4):
                cols = slice(128 * (p // 2), 128 * (p // 2) + 128)
                pt = p_ref[w, 4 * s + p]
                ptf = pt.astype(F32)
                dp = dps[4 * s + p]
                ds = ptf * (dp - jnp.sum(dp * ptf, axis=0, keepdims=True))
                t_ref[4 * s + p] += ds
                ds = ds.astype(BF)
                qt = dot(k_ts[s][64 * p : 64 * p + 64, :KEYS], ds)
                outs.append(jnp.where(first_head, qt[:, :LANES], qt[:, LANES:]))
                dks.append(dot(ds, q2s[s][:, cols]))
                dvs.append(dot(pt, d2s[s][:, cols]))
            scr[rows, lo : lo + SLAB] = (jnp.concatenate(outs, axis=0).T * scale)[:WIN]
            for g in range(2):
                cols = slice(512 + lo + 128 * g, 512 + lo + 128 * g + 128)
                scr[rows, cols] = (jnp.where(first_pair, dks[2 * g], dks[2 * g + 1]) * scale)[:WIN]
                cols = slice(1024 + lo + 128 * g, 1024 + lo + 128 * g + 128)
                scr[rows, cols] = jnp.where(first_pair, dvs[2 * g], dvs[2 * g + 1])[:WIN]
    d_ref[...] = scr[:ROWS, :].astype(BF)


def qkv_grad_body(n_ref, d_ref, gq_ref, gqv_ref, acc, accb):
    step = pl.program_id(0)

    @pl.when(step == 0)
    def _():
        acc[...] = jnp.zeros_like(acc)
        accb[...] = jnp.zeros_like(accb)

    d = d_ref[...]
    accb[0] += fold_rows(d[:, :512].astype(F32))
    accb[1] += fold_rows(d[:, 1024:].astype(F32))
    acc[...] += dot_tn(n_ref[...], d)

    @pl.when(step == pl.num_programs(0) - 1)
    def _():
        for s in range(2):
            for i in range(3):
                cols = slice(512 * i + SLAB * s, 512 * i + SLAB * s + SLAB)
                gq_ref[s, 256 * i : 256 * i + 256, :256] = acc[:256, cols].astype(BF)
                gq_ref[s, 256 * i : 256 * i + 256, 256:] = acc[256:, cols].astype(BF)
        gqv_ref[...] = jnp.sum(accb[...], axis=1)


def input_grad_body(x_ref, gm_ref, d_ref, wa_ref, wb_ref, gain_ref, gin_ref, gs_ref, accs):
    step = pl.program_id(0)

    @pl.when(step == 0)
    def _():
        accs[...] = jnp.zeros_like(accs)

    gn = jnp.zeros(gm_ref.shape, F32)
    for i in range(3):
        for s, w_ref in enumerate((wa_ref, wb_ref)):
            gn += dot_nt(d_ref[:, 512 * i + SLAB * s : 512 * i + SLAB * s + SLAB], w_ref[i])
    nh, r = norm_parts(x_ref[...].astype(F32))
    e = gn * gain_ref[0:1]
    gin = gm_ref[...] + r * (
        e - jnp.mean(e, axis=-1, keepdims=True) - nh * jnp.mean(e * nh, axis=-1, keepdims=True)
    )
    gin_ref[...] = gin.astype(BF)
    accs[0] += fold_rows(gn * nh)
    accs[1] += fold_rows(gn)

    @pl.when(step == pl.num_programs(0) - 1)
    def _():
        gs_ref[...] = jnp.sum(accs[...], axis=1)


def shaped(shape, dtype):
    return jax.ShapeDtypeStruct(shape, dtype)


def whole(shape):
    return pl.BlockSpec(shape, lambda i: (0,) * len(shape))


def by_rows(*shape, rows=ROWS):
    return pl.BlockSpec((rows,) + shape, lambda i: (i,) + (0,) * len(shape))


def dense_rows(*shape):
    return by_rows(*shape, rows=DENSE)


def by_windows(*shape):
    return pl.BlockSpec((GROUP,) + shape, lambda i: (i,) + (0,) * len(shape))


PARAMS = pltpu.CompilerParams(vmem_limit_bytes=60 << 20, dimension_semantics=("arbitrary",))


def attn_fwd(x, pages, wa, wb, qva, qvb, bias, pa, pb, ob, gain, shift):
    rows = x.shape[0]
    windows = rows // WIN
    return pl.pallas_call(
        attn_fwd_body,
        name="attn_fwd",
        grid=(rows // ROWS,),
        in_specs=[by_rows(512), by_windows(1, LANES)] + [whole(a.shape) for a in (wa, wb, qva, qvb, bias, pa, pb, ob, gain, shift)],
        out_specs=[by_rows(512), by_rows(512), by_rows(512), by_windows(LANES, 1536), by_windows(8, KEYS, SLAB)],
        out_shape=[
            shaped((rows, 512), F32),
            shaped((rows, 512), BF),
            shaped((rows, 512), BF),
            shaped((windows, LANES, 1536), BF),
            shaped((windows, 8, KEYS, SLAB), BF),
        ],
        scratch_shapes=[pltpu.VMEM((ROWS + 32, 1536), F32), pltpu.VMEM((GROUP, LANES, 512), F32)],
        compiler_params=PARAMS,
    )(x, pages, wa, wb, qva, qvb, bias, pa, pb, ob, gain, shift)


def cost(flops, moved):
    return pl.CostEstimate(flops=int(flops), bytes_accessed=int(moved), transcendentals=0)


def ffn(mixed, go, att, w1a, w1b, w2a, w2b, b1a, b1b, pa, pb, gain, shift):
    rows = mixed.shape[0]
    small = [w1a, w1b, w2a, w2b, b1a, b1b, pa, pb, gain, shift]
    return pl.pallas_call(
        ffn_body,
        name="feed_forward",
        grid=(rows // DENSE,),
        in_specs=[dense_rows(512)] * 3 + [whole(a.shape) for a in small],
        out_specs=[dense_rows(2048), dense_rows(512), dense_rows(512)]
        + [whole((2, 2304, 512)), whole((1, 2048)), whole((4, 512))],
        out_shape=[
            shaped((rows, 2048), BF),
            shaped((rows, 512), F32),
            shaped((rows, 512), BF),
            shaped((2, 2304, 512), BF),
            shaped((1, 2048), F32),
            shaped((4, 512), F32),
        ],
        scratch_shapes=[
            pltpu.VMEM((512, 2048), F32),
            pltpu.VMEM((2048, 512), F32),
            pltpu.VMEM((512, 512), F32),
            pltpu.VMEM((8, 2048), F32),
            pltpu.VMEM((4, 8, 512), F32),
        ],
        compiler_params=PARAMS,
        cost_estimate=cost(50e9, 40e6),
    )(mixed, go, att, *small)


def out_rows(mixed, act, w2a, w2b, ob):
    rows = mixed.shape[0]
    return pl.pallas_call(
        out_body,
        name="block_out",
        grid=(rows // DENSE,),
        in_specs=[dense_rows(512), dense_rows(2048)] + [whole(a.shape) for a in (w2a, w2b, ob)],
        out_specs=dense_rows(512),
        out_shape=shaped((rows, 512), BF),
        compiler_params=PARAMS,
        cost_estimate=cost(8e9, 20e6),
    )(mixed, act, w2a, w2b, ob)


def window_bwd(first, count, do, qkv, probs, *old):
    windows = qkv.shape[0]
    base = first // GROUP
    rows = lambda *shape: pl.BlockSpec((ROWS,) + shape, lambda i: (base + i,) + (0,) * len(shape))
    spec = lambda *shape: pl.BlockSpec((GROUP,) + shape, lambda i: (base + i,) + (0,) * len(shape))
    old_specs = [pl.BlockSpec(memory_space=pl.ANY), whole((8, KEYS, SLAB))] if old else []
    return pl.pallas_call(
        window_bwd_body,
        name="window_bwd",
        grid=(count // GROUP,),
        in_specs=[rows(512), spec(LANES, 1536), spec(8, KEYS, SLAB)] + old_specs,
        out_specs=[rows(1536), whole((8, KEYS, SLAB))],
        out_shape=[shaped((windows * WIN, 1536), BF), shaped((8, KEYS, SLAB), F32)],
        scratch_shapes=[pltpu.VMEM((ROWS + 32, 1536), F32)],
        input_output_aliases={3: 0, 4: 1} if old else {},
        compiler_params=PARAMS,
        cost_estimate=cost(1e9 * count, 1e6 * count),
    )(do, qkv, probs, *old)


def qkv_grad(n, d):
    rows = n.shape[0]
    return pl.pallas_call(
        qkv_grad_body,
        name="qkv_grad",
        grid=(rows // DENSE,),
        in_specs=[dense_rows(512), dense_rows(1536)],
        out_specs=[whole((2, 768, 512)), whole((2, 512))],
        out_shape=[shaped((2, 768, 512), BF), shaped((2, 512), F32)],
        scratch_shapes=[pltpu.VMEM((512, 1536), F32), pltpu.VMEM((2, 8, 512), F32)],
        compiler_params=PARAMS,
        cost_estimate=cost(9e9, 20e6),
    )(n, d)


def input_grad(x, gm, d, wa, wb, gain):
    rows = x.shape[0]
    return pl.pallas_call(
        input_grad_body,
        name="input_grad",
        grid=(rows // DENSE,),
        in_specs=[dense_rows(512), dense_rows(512), dense_rows(1536)] + [whole(a.shape) for a in (wa, wb, gain)],
        out_specs=[dense_rows(512), whole((2, 512))],
        out_shape=[shaped((rows, 512), BF), shaped((2, 512), F32)],
        scratch_shapes=[pltpu.VMEM((2, 8, 512), F32)],
        compiler_params=PARAMS,
        cost_estimate=cost(10e9, 20e6),
    )(x, gm, d, wa, wb, gain)


def expand_table(rel_index, table):
    heads = table.shape[1]
    slots = jnp.arange(table.shape[0], dtype=jnp.int32)
    onehot = (rel_index.T.reshape(-1)[:, None] == slots[None, :]).astype(F32)
    bias = jnp.dot(onehot, table * LOG2E, precision=lax.Precision.HIGHEST)
    bias = bias.reshape(WIN, WIN, heads).transpose(2, 0, 1)
    bias = jnp.pad(bias, ((0, 0), (0, KEYS - WIN), (0, LANES - WIN)))
    return bias.reshape(heads // 2, 2, KEYS, LANES).transpose(0, 2, 1, 3).reshape(heads // 2, KEYS, SLAB)


def table_grad(rel_index, gt):
    pairs = gt.shape[0]
    g = gt.reshape(pairs, KEYS, 2, LANES)[:, :WIN, :, :WIN].transpose(0, 2, 1, 3).reshape(2 * pairs, WIN * WIN)
    slots = jnp.arange(361, dtype=jnp.int32)
    onehot = (rel_index.T.reshape(-1)[:, None] == slots[None, :]).astype(F32)
    return jnp.einsum("pt,hp->th", onehot, g, precision=lax.Precision.HIGHEST)


SWAP = [(0, 1), (1, 0)]
PIECES = 3


def dp_bits(size):
    bits = []
    while 1 << len(bits) < size:
        bits.append(1 << len(bits))
    return bits


class Chain:
    def __init__(self, size, pair):
        bits = dp_bits(size)
        self.orders = (bits, bits[1:] + bits[:1])
        self.size = size
        tp, dp = lax.axis_index("tp"), lax.axis_index("dp")
        self.upper = [jnp.where(tp == 0, dp & p, dp & q) != 0 for p, q in zip(*self.orders)]
        last = len(bits) - 1
        self.steps = [("pair", None)] + [("half", k) for k in range(last)] + [("full", last)]
        self.steps += [("join", k) for k in range(last - 1, -1, -1)]
        self.own, self.out = pair
        self.late = None

    def begin(self):
        kind, k = self.steps[0]
        if kind == "pair":
            return self.out
        if kind == "half":
            half = self.own.shape[0] // 2
            up = self.upper[k].astype(jnp.int32)
            send = lax.dynamic_slice_in_dim(self.own, (1 - up) * half, half, 0)
            self.own = lax.dynamic_slice_in_dim(self.own, up * half, half, 0)
            return send
        if self.late is not None:
            return jnp.concatenate([self.own, self.late], axis=0)
        return self.own

    def move(self, send):
        kind, k = self.steps[0]
        if kind == "pair":
            return lax.ppermute(send, "tp", SWAP)
        perm = [(2 * i + t, 2 * (i ^ self.orders[t][k]) + t) for i in range(self.size) for t in range(2)]
        return lax.ppermute(send, ("dp", "tp"), perm)

    def end(self, got):
        kind, k = self.steps.pop(0)
        if kind in ("full", "join") and self.late is not None:
            rows = self.own.shape[0]
            self.late = self.late + got[rows:]
            got = got[:rows]
        if kind == "join":
            up = self.upper[k]
            self.own = jnp.concatenate([jnp.where(up, got, self.own), jnp.where(up, self.own, got)], axis=0)
        else:
            self.own = self.own + got


def advance(chains, work=None, *inputs):
    sends = [c.begin() for c in chains]
    if work is not None:
        sends, inputs = lax.optimization_barrier((sends, inputs))
    gots = [c.move(v) for c, v in zip(chains, sends)]
    result = None
    if work is not None:
        result = work(*inputs)
        gots, result = lax.optimization_barrier((gots, result))
    for c, got in zip(chains, gots):
        c.end(got)
    return result


def forward(x, pages, bias, wa, wb, qva, qvb, pa, pb, w1a, w1b, b1a, b1b, w2a, w2b, ob, gain, shift, go):
    mixed, att, n, qkv, probs = attn_fwd(x, pages, wa, wb, qva, qvb, bias, pa, pb, ob, gain, shift)
    act, gm, do, gf, gb1, gs2 = ffn(mixed, go, att, w1a, w1b, w2a, w2b, b1a, b1b, pa, pb, gain, shift)
    return mixed, n, qkv, probs, act, gm, do, gf, gb1, gs2


def attention_back(first, pieces, do, qkv, probs, *old):
    count = qkv.shape[0] // PIECES
    for i in range(first, first + pieces):
        old = window_bwd(i * count, count, do, qkv, probs, *old)
    return old


def local_block(x, pages, rel_index, wa, wb, qva, qvb, pa, pb, w1a, w1b, b1a, b1b, w2a, w2b, ob, gain, shift, ta, tb, go):
    bias = expand_table(rel_index, jnp.concatenate([ta, tb], axis=1))
    mixed, n, qkv, probs, act, gm, do, gf, gb1, gs2 = forward(
        x, pages, bias, wa, wb, qva, qvb, pa, pb, w1a, w1b, b1a, b1b, w2a, w2b, ob, gain, shift, go
    )
    d, t = attention_back(0, PIECES, do, qkv, probs)
    gq, gqv = qkv_grad(n, d)
    gin, gs1 = input_grad(x, gm, d, wa, wb, gain)
    out = out_rows(mixed, act, w2a, w2b, ob)
    g_table = table_grad(rel_index, t)
    g1 = jnp.concatenate([gf[0, 1024:1536], gf[0, 1536:2048], gf[1, 1024:1536], gf[1, 1536:2048]], axis=1)
    g2 = jnp.concatenate([gf[0, :1024], gf[1, :1024]])
    gp = jnp.concatenate([gf[0, 2048:], gf[1, 2048:]])
    return out, gin, g1, g2, gp, jax.vmap(unpack_qkv)(gq), gb1[0], gs2, gqv, gs1, g_table


def unpack_qkv(g):
    g = g.reshape(3, 256, 2, 256)
    return jnp.concatenate([g[:, :, 0], g[:, :, 1]], axis=1)


def flat_rows(v, rows):
    v = v.reshape(-1)
    return jnp.pad(v, (0, rows * 512 - v.shape[0])).reshape(rows, 512)


def per_device(
    dp_size, inputs, page_of, rel_index, w_qkv, qv_bias, w_proj, w_fc1, fc1_bias, w_fc2, out_biases, norm_gains,
    norm_biases, bias_table, out_grad,
):
    me = lax.axis_index("tp")
    windows = inputs.shape[0] // WIN
    swap = lambda v: lax.ppermute(v, "tp", SWAP)
    pages = lax.dynamic_slice_in_dim(page_of.reshape(2 * windows, WIN), me * windows, windows, 0)
    pages = jnp.pad(pages.astype(F32), ((0, 0), (0, LANES - WIN)), constant_values=-1.0)[:, None, :]
    w_qkv_b, qv_bias_b, w_proj_b, w_fc1_b, fc1_bias_b, w_fc2_b, table_b = (
        swap(v) for v in (w_qkv, qv_bias, w_proj, w_fc1, fc1_bias, w_fc2, bias_table)
    )
    bias = expand_table(rel_index, jnp.concatenate([bias_table, table_b], axis=1))
    mixed, n, qkv, probs, act, gm, do, gf, gb1, gs2 = forward(
        inputs, pages, bias, w_qkv, w_qkv_b, qv_bias, qv_bias_b, w_proj, w_proj_b, w_fc1, w_fc1_b,
        fc1_bias[None], fc1_bias_b[None], w_fc2, w_fc2_b, out_biases, norm_gains, norm_biases, out_grad,
    )
    f = Chain(dp_size, (gf[0], gf[1]))
    piece = advance([f], functools.partial(attention_back, 0, 1), do, qkv, probs)
    d, t = advance([f], functools.partial(attention_back, 1, 2), do, qkv, probs, *piece)
    gq, gqv = advance([f], qkv_grad, n, d)
    q = Chain(dp_size, (gq[0], gq[1]))
    gin, gs1 = advance([f, q], input_grad, inputs, gm, d, w_qkv, w_qkv_b, norm_gains)
    g_table = advance([f, q], functools.partial(table_grad, rel_index), t)
    small = lambda s: jnp.concatenate([
        gs2, gs1, gb1[0, 1024 * s : 1024 * s + 1024].reshape(2, 512), gqv[:, SLAB * s : SLAB * s + SLAB].reshape(1, 512),
        flat_rows(g_table[:, 8 * s : 8 * s + 8], 7),
    ]).astype(BF)
    q.late = small(0) + swap(small(1))
    out = advance([f, q], out_rows, mixed, act, w_fc2, w_fc2_b, out_biases)
    while f.steps or q.steps:
        advance([c for c in (f, q) if c.steps])
    g_f, g_q, late = f.own, q.own, q.late
    late = late.astype(F32)
    g_f = g_f.astype(F32)
    g_qkv = unpack_qkv(g_q.astype(F32))
    g_fc2 = g_f[:1024]
    g_fc1 = jnp.concatenate([g_f[1024:1536], g_f[1536:2048]], axis=1)
    g_proj = g_f[2048:]
    g_tab = late[9:].reshape(-1)[: bias_table.size].reshape(bias_table.shape)
    return (
        out, gin, g_qkv, late[8].reshape(2, SLAB), g_proj, g_fc1, late[6:8].reshape(-1), g_fc2, late[0:2],
        jnp.stack([late[4], late[2]]), jnp.stack([late[5], late[3]]), g_tab,
    )


def solution(mesh):
    rows = P(("dp", "tp"), None)
    placed = (
        rows, P("dp"), P(), P(None, None, "tp"), P(None, "tp"), P("tp", None), P(None, "tp"), P("tp"),
        P("tp", None), P(), P(), P(), P(None, "tp"), rows,
    )
    results = (
        rows, rows, P(None, None, "tp"), P(None, "tp"), P("tp", None), P(None, "tp"), P("tp"), P("tp", None),
        P(), P(), P(), P(None, "tp"),
    )
    return jax.shard_map(
        functools.partial(per_device, mesh.shape["dp"]), mesh=mesh, in_specs=placed, out_specs=results, check_vma=False
    )
```

```python
import functools

import jax
import jax.numpy as jnp
from jax import lax
from jax.experimental import pallas as pl
from jax.experimental.pallas import tpu as pltpu
from jax.sharding import PartitionSpec as P

HEAD = 32
EPS = 1e-05
WIN = 100
WS = 10
TAB = 361
KEYS = 104
LANES = 128
SLAB = 256
GROUP = 4
ROWS = GROUP * WIN
DENSE = 480
THIRD = 2
CHUNK = 256
LOG2E = 1.4426950408889634
NEG = -1e30
BF = jnp.bfloat16
F32 = jnp.float32
NT = (((1,), (1,)), ((), ()))
TN = (((0,), (0,)), ((), ()))


def dot(a, b):
    return jnp.dot(a, b, preferred_element_type=F32)


def dot_nt(a, b):
    return lax.dot_general(a, b, NT, preferred_element_type=F32)


def dot_tn(a, b):
    return lax.dot_general(a, b, TN, preferred_element_type=F32)


def norm_parts(v):
    mean = jnp.mean(v, axis=-1, keepdims=True)
    centered = v - mean
    var = jnp.mean(centered * centered, axis=-1, keepdims=True)
    r = lax.rsqrt(var + EPS)
    return centered * r, r


def fold_rows(v):
    rows, cols = v.shape
    return jnp.sum(v.reshape(rows // 8, 8, cols), axis=0)


def lane_mask(rows, test):
    lane = lax.broadcasted_iota(jnp.int32, (rows, SLAB), 1)
    return jnp.where(test(lane), 1.0, 0.0).astype(BF)


def attn_fwd_body(
    x_ref, xb_ref, page_ref, wa_ref, wb_ref, qva_ref, qvb_ref, bias_ref, pa_ref, pb_ref, ob_ref, gain_ref, shift_ref,
    n_ref, qkv_ref, mixed_ref, att_ref, p_ref,
    scr, cur, nxt, att_scr, att_rows,
):
    scale = (HEAD ** -0.5) * LOG2E

    @pl.when(pl.program_id(0) == 0)
    def _():
        scr[ROWS:, :] = jnp.zeros((scr.shape[0] - ROWS, scr.shape[1]), F32)

    def prepare():
        n, _ = norm_parts(x_ref[...].astype(F32))
        n = (n * gain_ref[0:1] + shift_ref[0:1]).astype(BF)
        n_ref[...] = n
        return n

    def project(n, i):
        for s, (w_ref, b_ref) in enumerate(((wa_ref, qva_ref), (wb_ref, qvb_ref))):
            cols = slice(512 * i + s * SLAB, 512 * i + s * SLAB + SLAB)
            out = dot(n, w_ref[i])
            scr[:ROWS, cols] = out if i == 1 else out + b_ref[i // 2 : i // 2 + 1]
        for w in range(GROUP):
            v = scr[w * WIN : w * WIN + LANES, 512 * i : 512 * i + 512].astype(BF)
            nxt[w, :, 512 * i : 512 * i + 512] = v
            qkv_ref[w, :, 512 * i : 512 * i + 512] = v

    def attend(beside):
        even = lane_mask(LANES, lambda c: (c // HEAD) % 2 == 0)
        odd = lane_mask(LANES, lambda c: (c // HEAD) % 2 == 1)
        low = lane_mask(KEYS, lambda c: c % 128 < 64)[:, :128]
        high = lane_mask(KEYS, lambda c: c % 128 >= 64)[:, :128]
        query_lane = lax.broadcasted_iota(jnp.int32, (1, SLAB), 1) % LANES
        valid = jnp.where(query_lane < WIN, 1.0, 0.0)
        first_head = lax.broadcasted_iota(jnp.int32, (2 * HEAD, LANES), 0) < HEAD
        for w in range(GROUP):
            pages = jnp.broadcast_to(page_ref[w], (LANES, LANES))
            mask = jnp.where(pages == pages.T, 0.0, NEG)[:KEYS]
            mask = jnp.concatenate([mask, mask], axis=1)
            scores, v_ts = [], []
            for s in range(2):
                lo = s * SLAB
                q = cur[w, :, lo : lo + SLAB]
                k = cur[w, :KEYS, 512 + lo : 512 + lo + SLAB]
                v_ts.append(cur[w, :, 1024 + lo : 1024 + lo + SLAB].T)
                q2 = jnp.concatenate([q * even, q * odd], axis=0)
                for p in range(4):
                    cols = slice(128 * (p // 2), 128 * (p // 2) + 128)
                    scores.append(dot_nt(k[:, cols] * (low if p % 2 == 0 else high), q2[:, cols]))
            beside(w)
            for s in range(2):
                outs = []
                for p in range(4):
                    st = scores[4 * s + p] * scale + bias_ref[4 * s + p] + mask
                    e = jnp.exp2(st - jnp.max(st, axis=0, keepdims=True))
                    pt = (e * (valid / jnp.sum(e, axis=0, keepdims=True))).astype(BF)
                    p_ref[w, 4 * s + p] = pt
                    ot = dot(v_ts[s][64 * p : 64 * p + 64, :KEYS], pt)
                    outs.append(jnp.where(first_head, ot[:, :LANES], ot[:, LANES:]))
                att_scr[w, :, s * SLAB : s * SLAB + SLAB] = jnp.concatenate(outs, axis=0).T
        for w in range(GROUP):
            att_rows[w * WIN : w * WIN + WIN, :] = att_scr[w, :WIN, :]
        att = att_rows[...].astype(BF)
        att_ref[...] = att
        mixed_ref[...] = (
            xb_ref[...].astype(F32) + ob_ref[0:1] + dot(att[:, :SLAB], pa_ref[...]) + dot(att[:, SLAB:], pb_ref[...])
        )

    step, end = pl.program_id(0), pl.num_programs(0) - 1

    @pl.when(step == 0)
    def _():
        n = prepare()
        for i in range(3):
            project(n, i)
        cur[...] = nxt[...]

    @pl.when((step > 0) & (step < end))
    def _():
        n = prepare()
        attend(lambda w: project(n, w) if w < 3 else None)
        cur[...] = nxt[...]

    @pl.when(step == end)
    def _():
        attend(lambda w: None)


def gelu_parts(h):
    phi = 0.5 + 0.5 * lax.erf(h * 0.7071067811865476)
    return phi, jnp.exp2(h * h * (-0.5 * LOG2E)) * 0.3989422804014327


def ffn_body(
    mixed_ref, go_ref, att_ref, w1a_ref, w1b_ref, w2a_ref, w2b_ref, b1a_ref, b1b_ref, pa_ref, pb_ref, gain_ref, shift_ref,
    act_ref, gm_ref, do_ref, gfa_ref, gfb_ref, gb1_ref, gs_ref,
    acc1, acc2, accp, accb, accs,
):
    step = pl.program_id(0)

    @pl.when(step == 0)
    def _():
        acc1[...] = jnp.zeros_like(acc1)
        acc2[...] = jnp.zeros_like(acc2)
        accp[...] = jnp.zeros_like(accp)
        accb[...] = jnp.zeros_like(accb)
        accs[...] = jnp.zeros_like(accs)

    mixed = mixed_ref[...]
    nh, r = norm_parts(mixed)
    n2 = (nh * gain_ref[1:2] + shift_ref[1:2]).astype(BF)
    go = go_ref[...]
    gn = jnp.zeros_like(mixed)
    per_half = 1024 // CHUNK

    def weights(c):
        col = slice(CHUNK * (c % per_half), CHUNK * (c % per_half) + CHUNK)
        return ((w1a_ref, w2a_ref, b1a_ref) if c < per_half else (w1b_ref, w2b_ref, b1b_ref)) + (col,)

    def front(c):
        w1_ref, w2_ref, b1_ref, col = weights(c)
        return dot(n2, w1_ref[:, col]) + b1_ref[0:1, col], dot_nt(go, w2_ref[col, :])

    ready = front(0)
    for c in range(2 * per_half):
        h, ga = ready
        if c + 1 < 2 * per_half:
            ready = front(c + 1)
        w1_ref, _, _, col = weights(c)
        full = slice(CHUNK * c, CHUNK * c + CHUNK)
        phi, density = gelu_parts(h)
        act = (h * phi).astype(BF)
        act_ref[:, full] = act
        ghf = ga * (phi + h * density)
        accb[:, full] += fold_rows(ghf)
        gh = ghf.astype(BF)
        gn += dot_nt(gh, w1_ref[:, col])
        acc2[full, :] += dot_tn(act, go)
        acc1[:, full] += dot_tn(n2, gh)
    gof = go.astype(F32)
    e = gn * gain_ref[1:2]
    gm = gof + r * (
        e - jnp.mean(e, axis=-1, keepdims=True) - nh * jnp.mean(e * nh, axis=-1, keepdims=True)
    )
    gm_ref[...] = gm
    gml = gm.astype(BF)
    accp[...] += dot_tn(att_ref[...], gml)
    do_ref[:, :SLAB] = dot_nt(gml, pa_ref[...]).astype(BF)
    do_ref[:, SLAB:] = dot_nt(gml, pb_ref[...]).astype(BF)
    accs[0] += fold_rows(gm)
    accs[1] += fold_rows(gof)
    accs[2] += fold_rows(gn * nh)
    accs[3] += fold_rows(gn)

    @pl.when(step == pl.num_programs(0) - 1)
    def _():
        for s, gf_ref in enumerate((gfa_ref, gfb_ref)):
            gf_ref[:1024] = acc2[1024 * s : 1024 * s + 1024, :].astype(BF)
            gf_ref[1024:1536] = acc1[:, 1024 * s : 1024 * s + 512].astype(BF)
            gf_ref[1536:2048] = acc1[:, 1024 * s + 512 : 1024 * s + 1024].astype(BF)
            gf_ref[2048:2304] = accp[SLAB * s : SLAB * s + SLAB, :].astype(BF)
        gb1_ref[...] = jnp.sum(accb[...], axis=0, keepdims=True)
        gs_ref[...] = jnp.sum(accs[...], axis=1)


def out_body(mixed_ref, act_ref, w2a_ref, w2b_ref, ob_ref, *refs):
    out_ref = refs[-1]
    out = mixed_ref[...] + ob_ref[1:2] + dot(act_ref[:, :1024], w2a_ref[...]) + dot(act_ref[:, 1024:], w2b_ref[...])
    out_ref[...] = out.astype(BF)


def attn_bwd_body(
    n_ref, do_ref, qkv_ref, p_ref, d_ref, t_ref, gqa_ref, gqb_ref, gqv_ref, scr, prev, acc, accb
):
    scale = HEAD ** -0.5
    step, end = pl.program_id(0), pl.num_programs(0) - 1

    @pl.when(step == 0)
    def _():
        scr[ROWS:, :512] = jnp.zeros((scr.shape[0] - ROWS, 512), F32)
        t_ref[...] = jnp.zeros_like(t_ref)
        prev[...] = jnp.zeros_like(prev)
        acc[...] = jnp.zeros_like(acc)
        accb[...] = jnp.zeros_like(accb)

    def weights(i):
        cols = slice(512 * i, 512 * i + 512)
        d = prev[:, cols]
        acc[:, cols] += dot_tn(n_ref[...], d)
        if i != 1:
            accb[i // 2] += fold_rows(d.astype(F32))

    def windows():
        scr[:ROWS, :512] = do_ref[...].astype(F32)
        row = lax.broadcasted_iota(jnp.int32, (LANES, 512), 0)
        dos = [jnp.where(row < WIN, scr[w * WIN : w * WIN + LANES, :512], 0.0).astype(BF) for w in range(GROUP)]
        even = lane_mask(LANES, lambda c: (c // HEAD) % 2 == 0)
        odd = lane_mask(LANES, lambda c: (c // HEAD) % 2 == 1)
        low = lane_mask(KEYS, lambda c: c % 128 < 64)[:, :128]
        high = lane_mask(KEYS, lambda c: c % 128 >= 64)[:, :128]
        first_head = lax.broadcasted_iota(jnp.int32, (2 * HEAD, LANES), 0) < HEAD
        first_pair = lax.broadcasted_iota(jnp.int32, (KEYS, 128), 1) < 64
        for w in range(GROUP):
            rows = slice(w * WIN, w * WIN + WIN)
            q2s, d2s, k_ts, dps = [], [], [], []
            for s in range(2):
                lo = s * SLAB
                q = qkv_ref[w, :, lo : lo + SLAB]
                v = qkv_ref[w, :KEYS, 1024 + lo : 1024 + lo + SLAB]
                do = dos[w][:, lo : lo + SLAB]
                q2s.append(jnp.concatenate([q * even, q * odd], axis=0))
                d2s.append(jnp.concatenate([do * even, do * odd], axis=0))
                k_ts.append(qkv_ref[w, :, 512 + lo : 512 + lo + SLAB].T)
                for p in range(4):
                    cols = slice(128 * (p // 2), 128 * (p // 2) + 128)
                    dps.append(dot_nt(v[:, cols] * (low if p % 2 == 0 else high), d2s[s][:, cols]))
            if w < 3:
                weights(w)
            for s in range(2):
                lo = s * SLAB
                outs, dks, dvs = [], [], []
                for p in range(4):
                    cols = slice(128 * (p // 2), 128 * (p // 2) + 128)
                    pt = p_ref[w, 4 * s + p]
                    ptf = pt.astype(F32)
                    dp = dps[4 * s + p]
                    ds = ptf * (dp - jnp.sum(dp * ptf, axis=0, keepdims=True))
                    t_ref[4 * s + p] += ds
                    ds = ds.astype(BF)
                    qt = dot(k_ts[s][64 * p : 64 * p + 64, :KEYS], ds)
                    outs.append(jnp.where(first_head, qt[:, :LANES], qt[:, LANES:]))
                    dks.append(dot(ds, q2s[s][:, cols]))
                    dvs.append(dot(pt, d2s[s][:, cols]))
                scr[rows, lo : lo + SLAB] = (jnp.concatenate(outs, axis=0).T * scale)[:WIN]
                for g in range(2):
                    cols = slice(512 + lo + 128 * g, 512 + lo + 128 * g + 128)
                    scr[rows, cols] = (jnp.where(first_pair, dks[2 * g], dks[2 * g + 1]) * scale)[:WIN]
                    cols = slice(1024 + lo + 128 * g, 1024 + lo + 128 * g + 128)
                    scr[rows, cols] = jnp.where(first_pair, dvs[2 * g], dvs[2 * g + 1])[:WIN]
        d = scr[:ROWS, :].astype(BF)
        d_ref[...] = d
        prev[...] = d

    @pl.when(step < end)
    def _():
        windows()

    @pl.when(step == end)
    def _():
        for i in range(3):
            weights(i)
        for s, gq_ref in enumerate((gqa_ref, gqb_ref)):
            for i in range(3):
                cols = slice(512 * i + SLAB * s, 512 * i + SLAB * s + SLAB)
                gq_ref[256 * i : 256 * i + 256, :256] = acc[:256, cols].astype(BF)
                gq_ref[256 * i : 256 * i + 256, 256:] = acc[256:, cols].astype(BF)
        gqv_ref[...] = jnp.sum(accb[...], axis=1)


def input_grad_body(x_ref, gm_ref, d_ref, wa_ref, wb_ref, gain_ref, *refs):
    gin_ref, gs_ref, accs = refs[-3:]
    step = pl.program_id(0)

    @pl.when(step == 0)
    def _():
        accs[...] = jnp.zeros_like(accs)

    gn = jnp.zeros(gm_ref.shape, F32)
    for i in range(3):
        for s, w_ref in enumerate((wa_ref, wb_ref)):
            gn += dot_nt(d_ref[:, 512 * i + SLAB * s : 512 * i + SLAB * s + SLAB], w_ref[i])
    nh, r = norm_parts(x_ref[...].astype(F32))
    e = gn * gain_ref[0:1]
    gin = gm_ref[...] + r * (
        e - jnp.mean(e, axis=-1, keepdims=True) - nh * jnp.mean(e * nh, axis=-1, keepdims=True)
    )
    gin_ref[...] = gin.astype(BF)
    accs[0] += fold_rows(gn * nh)
    accs[1] += fold_rows(gn)

    @pl.when(step == pl.num_programs(0) - 1)
    def _():
        gs_ref[...] = jnp.sum(accs[...], axis=1)


def shaped(shape, dtype):
    return jax.ShapeDtypeStruct(shape, dtype)


def whole(shape):
    return pl.BlockSpec(shape, lambda i: (0,) * len(shape))


def by_rows(*shape, rows=ROWS):
    return pl.BlockSpec((rows,) + shape, lambda i: (i,) + (0,) * len(shape))


def dense_rows(*shape):
    return by_rows(*shape, rows=DENSE)


def by_windows(*shape):
    return pl.BlockSpec((GROUP,) + shape, lambda i: (i,) + (0,) * len(shape))


PARAMS = pltpu.CompilerParams(vmem_limit_bytes=60 << 20, dimension_semantics=("arbitrary",))


def attn_fwd(x, pages, wa, wb, qva, qvb, bias, pa, pb, ob, gain, shift):
    rows = x.shape[0]
    windows = rows // WIN
    last = rows // ROWS - 1
    front = lambda *shape: pl.BlockSpec(shape, lambda i: (jnp.minimum(i, last),) + (0,) * (len(shape) - 1))
    back = lambda *shape: pl.BlockSpec(shape, lambda i: (jnp.maximum(i - 1, 0),) + (0,) * (len(shape) - 1))
    return pl.pallas_call(
        attn_fwd_body,
        name="attn_fwd",
        grid=(rows // ROWS + 1,),
        in_specs=[front(ROWS, 512), back(ROWS, 512), back(GROUP, 1, LANES)]
        + [whole(a.shape) for a in (wa, wb, qva, qvb, bias, pa, pb, ob, gain, shift)],
        out_specs=[
            front(ROWS, 512), front(GROUP, LANES, 1536), back(ROWS, 512), back(ROWS, 512),
            back(GROUP, 8, KEYS, SLAB),
        ],
        out_shape=[
            shaped((rows, 512), BF),
            shaped((windows, LANES, 1536), BF),
            shaped((rows, 512), F32),
            shaped((rows, 512), BF),
            shaped((windows, 8, KEYS, SLAB), BF),
        ],
        scratch_shapes=[
            pltpu.VMEM((ROWS + 32, 1536), F32),
            pltpu.VMEM((GROUP, LANES, 1536), BF),
            pltpu.VMEM((GROUP, LANES, 1536), BF),
            pltpu.VMEM((GROUP, LANES, 512), F32),
            pltpu.VMEM((ROWS, 512), F32),
        ],
        compiler_params=PARAMS,
    )(x, x, pages, wa, wb, qva, qvb, bias, pa, pb, ob, gain, shift)


def cost(flops, moved):
    return pl.CostEstimate(flops=int(flops), bytes_accessed=int(moved), transcendentals=0)


def ffn(mixed, go, att, w1a, w1b, w2a, w2b, b1a, b1b, pa, pb, gain, shift):
    rows = mixed.shape[0]
    small = [w1a, w1b, w2a, w2b, b1a, b1b, pa, pb, gain, shift]
    return pl.pallas_call(
        ffn_body,
        name="feed_forward",
        grid=(rows // DENSE,),
        in_specs=[dense_rows(512)] * 3 + [whole(a.shape) for a in small],
        out_specs=[dense_rows(2048), dense_rows(512), dense_rows(512)]
        + [whole((2304, 512)), whole((2304, 512)), whole((1, 2048)), whole((4, 512))],
        out_shape=[
            shaped((rows, 2048), BF),
            shaped((rows, 512), F32),
            shaped((rows, 512), BF),
            shaped((2304, 512), BF),
            shaped((2304, 512), BF),
            shaped((1, 2048), F32),
            shaped((4, 512), F32),
        ],
        scratch_shapes=[
            pltpu.VMEM((512, 2048), F32),
            pltpu.VMEM((2048, 512), F32),
            pltpu.VMEM((512, 512), F32),
            pltpu.VMEM((8, 2048), F32),
            pltpu.VMEM((4, 8, 512), F32),
        ],
        compiler_params=PARAMS,
        cost_estimate=cost(50e9, 40e6),
    )(mixed, go, att, *small)


def third_rows(part):
    return lambda *shape: pl.BlockSpec((ROWS,) + shape, lambda i: (THIRD * part + i,) + (0,) * len(shape))


def out_rows(part, mixed, act, w2a, w2b, ob, *old):
    rows = mixed.shape[0]
    spec = third_rows(part)
    return pl.pallas_call(
        out_body,
        name="block_out",
        grid=(THIRD,),
        in_specs=[spec(512), spec(2048)] + [whole(a.shape) for a in (w2a, w2b, ob)] + [pl.BlockSpec(memory_space=pl.ANY)] * len(old),
        out_specs=spec(512),
        out_shape=shaped((rows, 512), BF),
        input_output_aliases={5: 0} if old else {},
        compiler_params=PARAMS,
        cost_estimate=cost(3e9, 7e6),
    )(mixed, act, w2a, w2b, ob, *old)


def attn_bwd(n, do, qkv, probs):
    rows = n.shape[0]
    last = rows // ROWS - 1
    front = lambda *shape: pl.BlockSpec(shape, lambda i: (jnp.minimum(i, last),) + (0,) * (len(shape) - 1))
    back = lambda *shape: pl.BlockSpec(shape, lambda i: (jnp.maximum(i - 1, 0),) + (0,) * (len(shape) - 1))
    return pl.pallas_call(
        attn_bwd_body,
        name="attn_bwd",
        grid=(rows // ROWS + 1,),
        in_specs=[back(ROWS, 512), front(ROWS, 512), front(GROUP, LANES, 1536), front(GROUP, 8, KEYS, SLAB)],
        out_specs=[
            front(ROWS, 1536), whole((8, KEYS, SLAB)), whole((768, 512)), whole((768, 512)), whole((2, 512)),
        ],
        out_shape=[
            shaped((rows, 1536), BF), shaped((8, KEYS, SLAB), F32), shaped((768, 512), BF), shaped((768, 512), BF),
            shaped((2, 512), F32),
        ],
        scratch_shapes=[
            pltpu.VMEM((ROWS + 32, 1536), F32),
            pltpu.VMEM((ROWS, 1536), BF),
            pltpu.VMEM((512, 1536), F32),
            pltpu.VMEM((2, 8, 512), F32),
        ],
        compiler_params=PARAMS,
        cost_estimate=cost(30e9, 60e6),
    )(n, do, qkv, probs)


def input_grad(part, x, gm, d, wa, wb, gain, *old):
    rows = x.shape[0]
    spec = third_rows(part)
    return pl.pallas_call(
        input_grad_body,
        name="input_grad",
        grid=(THIRD,),
        in_specs=[spec(512), spec(512), spec(1536)] + [whole(a.shape) for a in (wa, wb, gain)] + [pl.BlockSpec(memory_space=pl.ANY)] * len(old),
        out_specs=[spec(512), whole((2, 512))],
        out_shape=[shaped((rows, 512), BF), shaped((2, 512), F32)],
        scratch_shapes=[pltpu.VMEM((2, 8, 512), F32)],
        input_output_aliases={6: 0} if old else {},
        compiler_params=PARAMS,
        cost_estimate=cost(3e9, 7e6),
    )(x, gm, d, wa, wb, gain, *old)


def offset_onehot(index_row):
    slot = lax.broadcasted_iota(jnp.int32, (TAB, SLAB), 0).astype(F32)
    return jnp.where(slot == index_row, 1.0, 0.0).astype(BF)


def bias_body(rel_ref, ta_ref, tb_ref, bias_ref, idx_ref, scr):
    scr[...] = jnp.zeros_like(scr)
    scr[:WIN, :WIN] = rel_ref[...].astype(F32)
    scr[...] = scr[...].T
    lane = lax.broadcasted_iota(jnp.int32, (16, SLAB), 1)
    blank = jnp.zeros((16, SLAB - LANES), F32)

    def place(row, width, at):
        piece = jnp.concatenate([scr[row : row + 16, :], blank], axis=1)
        return pltpu.roll(jnp.where(lane < width, piece, 0.0), at, 1)

    idx = place(0, WIN, WIN - WS)
    for d in range(WS - 1):
        idx += place(WS * (WS - 1 - d), WS, WS * d)
    idx = jnp.where(lane < WIN + WIN - WS, idx, -1.0)
    idx_ref[...] = idx
    table = jnp.concatenate([ta_ref[...], tb_ref[...]], axis=1) * LOG2E
    high = table.astype(BF)
    rest = table - high.astype(F32)
    mid = rest.astype(BF)
    table = jnp.concatenate([high, mid, (rest - mid.astype(F32)).astype(BF)], axis=1)
    row = lax.broadcasted_iota(jnp.int32, (16, 48), 0)
    col = lax.broadcasted_iota(jnp.int32, (16, 48), 1)
    pick = jnp.where(col % 16 == 2 * (row % 8) + row // 8, 1.0, 0.0).astype(BF)
    for jx in range(WS):
        parts = dot_tn(table, offset_onehot(idx[jx : jx + 1]))
        values = dot(pick, parts.astype(BF))
        for jy in range(WS):
            shift = WS * (WS - 1 - jy)
            moved = pltpu.roll(values, (SLAB - shift) % SLAB, 1) if shift else values
            bias_ref[:, WS * jy + jx, :LANES] = moved[:8, :LANES]
            bias_ref[:, WS * jy + jx, LANES:] = moved[8:, :LANES]
    for key in range(WIN, KEYS):
        bias_ref[:, key, :] = jnp.zeros((8, SLAB), F32)


def expand_table(rel_index, ta, tb):
    return pl.pallas_call(
        bias_body,
        name="bias",
        out_shape=[shaped((8, KEYS, SLAB), F32), shaped((16, SLAB), F32)],
        scratch_shapes=[pltpu.VMEM((LANES, LANES), F32)],
        compiler_params=pltpu.CompilerParams(vmem_limit_bytes=16 << 20),
        cost_estimate=cost(3e9, 1e6),
    )(rel_index, ta, tb)


def small_body(idx_ref, t_ref, gs2_ref, gs1a_ref, gs1b_ref, gs1c_ref, gb1_ref, gqv_ref, own_ref, other_ref, scr):
    total = jnp.zeros((32, TAB), F32)
    blank = jnp.zeros((8, SLAB - LANES), F32)
    for jx in range(WS):
        even = jnp.zeros((8, SLAB), F32)
        odd = jnp.zeros((8, SLAB), F32)
        for jy in range(WS):
            shift = WS * (WS - 1 - jy)
            even += pltpu.roll(jnp.concatenate([t_ref[:, WS * jy + jx, :LANES], blank], axis=1), shift, 1)
            odd += pltpu.roll(jnp.concatenate([t_ref[:, WS * jy + jx, LANES:], blank], axis=1), shift, 1)
        heads = jnp.concatenate([even, odd], axis=0)
        high = heads.astype(BF)
        rest = (heads - high.astype(F32)).astype(BF)
        total += dot_nt(jnp.concatenate([high, rest], axis=0), offset_onehot(idx_ref[jx : jx + 1]))
    total = total[:16] + total[16:]
    for s, out_ref in enumerate((own_ref, other_ref)):
        scr[...] = jnp.zeros_like(scr)
        scr[0:4] = gs2_ref[...]
        scr[4:6] = gs1a_ref[...] + gs1b_ref[...] + gs1c_ref[...]
        scr[6:7] = gb1_ref[:, 1024 * s : 1024 * s + 512]
        scr[7:8] = gb1_ref[:, 1024 * s + 512 : 1024 * s + 1024]
        scr[8:9, :SLAB] = gqv_ref[0:1, SLAB * s : SLAB * s + SLAB]
        scr[8:9, SLAB:] = gqv_ref[1:2, SLAB * s : SLAB * s + SLAB]
        scr[16:20, :TAB] = total[4 * s : 4 * s + 4]
        scr[20:24, :TAB] = total[8 + 4 * s : 12 + 4 * s]
        out_ref[...] = scr[...].astype(BF)


def small_sums(*args):
    return pl.pallas_call(
        small_body,
        name="small_sums",
        out_shape=[shaped((32, 512), BF), shaped((32, 512), BF)],
        scratch_shapes=[pltpu.VMEM((32, 512), F32)],
        compiler_params=pltpu.CompilerParams(vmem_limit_bytes=16 << 20),
        cost_estimate=cost(3e9, 1e6),
    )(*args)


def finish_body(q_ref, late_ref, gq_ref, gqv_ref, gob_ref, gg_ref, gh_ref, gb1_ref, gt_ref, scr):
    for i in range(3):
        q = q_ref[256 * i : 256 * i + 256, :].astype(F32)
        gq_ref[i, :256, :] = q[:, :256]
        gq_ref[i, 256:, :] = q[:, 256:]
    late = late_ref[...].astype(F32)
    gob_ref[...] = late[0:2]
    gg_ref[0:1] = late[4:5]
    gg_ref[1:2] = late[2:3]
    gh_ref[0:1] = late[5:6]
    gh_ref[1:2] = late[3:4]
    gb1_ref[:, :512] = late[6:7]
    gb1_ref[:, 512:] = late[7:8]
    gqv_ref[0:1] = late[8:9, :SLAB]
    gqv_ref[1:2] = late[8:9, SLAB:]
    scr[...] = jnp.zeros_like(scr)
    for h in range(8):
        r = 16 + 4 * (h % 2) + h // 2
        scr[h : h + 1, :] = late[r : r + 1, :]
    gt_ref[...] = scr[...].T[:TAB, :8]


def finish(q, late):
    return pl.pallas_call(
        finish_body,
        name="finish",
        out_shape=[
            shaped((3, 512, SLAB), F32), shaped((2, SLAB), F32), shaped((2, 512), F32), shaped((2, 512), F32),
            shaped((2, 512), F32), shaped((1, 1024), F32), shaped((TAB, 8), F32),
        ],
        scratch_shapes=[pltpu.VMEM((LANES, 512), F32)],
        compiler_params=pltpu.CompilerParams(vmem_limit_bytes=16 << 20),
        cost_estimate=cost(1e9, 4e6),
    )(q, late)


SWAP = [(0, 1), (1, 0)]
SPLIT = True


def dp_bits(size):
    bits = []
    while 1 << len(bits) < size:
        bits.append(1 << len(bits))
    return bits


class Chain:
    def __init__(self, size, own, orders):
        self.orders, self.size, self.own, self.late = orders, size, own, None
        tp, dp = lax.axis_index("tp"), lax.axis_index("dp")
        self.upper = [jnp.where(tp == 0, dp & p, dp & q) != 0 for p, q in zip(*orders)]
        last = len(orders[0]) - 1
        self.steps = [("half", k) for k in range(last)] + [("full", last)]
        self.steps += [("join", k) for k in range(last - 1, -1, -1)]

    def begin(self):
        kind, k = self.steps[0]
        if kind == "half":
            half = self.own.shape[0] // 2
            up = self.upper[k].astype(jnp.int32)
            send = lax.dynamic_slice_in_dim(self.own, (1 - up) * half, half, 0)
            self.own = lax.dynamic_slice_in_dim(self.own, up * half, half, 0)
            return send
        if self.late is not None:
            return jnp.concatenate([self.own, self.late], axis=0)
        return self.own

    def move(self, send):
        k = self.steps[0][1]
        perm = [(2 * i + t, 2 * (i ^ self.orders[t][k]) + t) for i in range(self.size) for t in range(2)]
        return lax.ppermute(send, ("dp", "tp"), perm)

    def end(self, got):
        kind, k = self.steps.pop(0)
        if kind in ("full", "join") and self.late is not None:
            rows = self.own.shape[0]
            self.late = self.late + got[rows:]
            got = got[:rows]
        if kind == "join":
            up = self.upper[k]
            self.own = jnp.concatenate([jnp.where(up, got, self.own), jnp.where(up, self.own, got)], axis=0)
        else:
            self.own = self.own + got


class Pair:
    def __init__(self, own, other):
        self.own, self.other = own, other

    def begin(self):
        return self.other

    def move(self, send):
        return lax.ppermute(send, "tp", SWAP)

    def end(self, got):
        self.got = got

    def total(self):
        return self.own + self.got


tie = lax.optimization_barrier


def advance(chains, work=None, *inputs):
    sends, inputs = tie(([c.begin() for c in chains], inputs))
    gots = [c.move(v) for c, v in zip(chains, sends)]
    result = None if work is None else work(*inputs)
    gots, result = tie((gots, result))
    for c, got in zip(chains, gots):
        c.end(got)
    return result


class Flight:
    def __init__(self, chains):
        self.chains, self.sends, self.gots = chains, [c.begin() for c in chains], None

    def beside(self, chains, work, *inputs):
        sends = [c.begin() for c in chains]
        self.sends, sends, inputs = tie((self.sends, sends, inputs))
        if self.gots is None:
            self.gots = [c.move(v) for c, v in zip(self.chains, self.sends)]
        gots = [c.move(v) for c, v in zip(chains, sends)]
        gots, result = tie((gots, work(*inputs)))
        self.last = (gots, result)
        for c, got in zip(chains, gots):
            c.end(got)
        return result

    def land(self):
        self.gots, _ = tie((self.gots, self.last))
        for c, got in zip(self.chains, self.gots):
            c.end(got)


class Slices:
    def __init__(self, chain, count):
        self.chain, self.send, self.gots = chain, chain.begin(), []
        rows = self.send.shape[0]
        self.cuts = [rows * i // count // 8 * 8 for i in range(count)] + [rows]

    def begin(self):
        i = len(self.gots)
        return self.send[self.cuts[i] : self.cuts[i + 1]]

    def move(self, send):
        return self.chain.move(send)

    def end(self, got):
        self.gots.append(got)
        if len(self.gots) + 1 == len(self.cuts):
            self.chain.end(jnp.concatenate(self.gots, axis=0))


def forward(x, pages, bias, wa, wb, qva, qvb, pa, pb, w1a, w1b, b1a, b1b, w2a, w2b, ob, gain, shift, go):
    n, qkv, mixed, att, probs = attn_fwd(x, pages, wa, wb, qva, qvb, bias, pa, pb, ob, gain, shift)
    act, gm, do, gfa, gfb, gb1, gs2 = ffn(mixed, go, att, w1a, w1b, w2a, w2b, b1a, b1b, pa, pb, gain, shift)
    return mixed, n, qkv, probs, act, gm, do, (gfa, gfb), gb1, gs2


def local_block(x, pages, rel_index, wa, wb, qva, qvb, pa, pb, w1a, w1b, b1a, b1b, w2a, w2b, ob, gain, shift, ta, tb, go):
    bias, idx = expand_table(rel_index, ta, tb)
    mixed, n, qkv, probs, act, gm, do, gf, gb1, gs2 = forward(
        x, pages, bias, wa, wb, qva, qvb, pa, pb, w1a, w1b, b1a, b1b, w2a, w2b, ob, gain, shift, go
    )
    d, t, gqa, gqb, gqv = attn_bwd(n, do, qkv, probs)
    gin, out, sums = (), (), []
    for i in range(3):
        *gin, part = input_grad(i, x, gm, d, wa, wb, gain, *gin)
        sums.append(part)
        out = [out_rows(i, mixed, act, w2a, w2b, ob, *out)]
    own, other = small_sums(idx, t, gs2, *sums, gb1, gqv)
    gin, out = gin[0], out[0]
    return out, gin, gf, finish(gqa, own), finish(gqb, other)


def per_device(
    dp_size, inputs, page_of, rel_index, w_qkv, qv_bias, w_proj, w_fc1, fc1_bias, w_fc2, out_biases, norm_gains,
    norm_biases, bias_table, out_grad,
):
    me = lax.axis_index("tp")
    windows = inputs.shape[0] // WIN
    swap = lambda v: lax.ppermute(v, "tp", SWAP)
    pages = lax.dynamic_slice_in_dim(page_of.reshape(2 * windows, WIN), me * windows, windows, 0)
    pages = jnp.pad(pages.astype(F32), ((0, 0), (0, LANES - WIN)), constant_values=-1.0)[:, None, :]
    w_qkv_b, qv_bias_b, w_proj_b, table_b = (swap(v) for v in (w_qkv, qv_bias, w_proj, bias_table))
    later, w_qkv_b, table_b = tie(((w_fc1, fc1_bias, w_fc2), w_qkv_b, table_b))
    w_fc1_b, fc1_bias_b, w_fc2_b = (swap(v) for v in later)
    bias, idx = expand_table(rel_index, bias_table, table_b)
    mixed, n, qkv, probs, act, gm, do, gf, gb1, gs2 = forward(
        inputs, pages, bias, w_qkv, w_qkv_b, qv_bias, qv_bias_b, w_proj, w_proj_b, w_fc1, w_fc1_b,
        fc1_bias[None], fc1_bias_b[None], w_fc2, w_fc2_b, out_biases, norm_gains, norm_biases, out_grad,
    )
    bits = dp_bits(dp_size)
    turned = bits[1:] + bits[:1]
    mid = len(bits) // 2
    deep = bits[mid:-1] + bits[:mid] + bits[-1:]
    grad = lambda i, *old: (functools.partial(input_grad, i), inputs, gm, d, w_qkv, w_qkv_b, norm_gains) + old
    rows_out = lambda i, *old: (functools.partial(out_rows, i), mixed, act, w_fc2, w_fc2_b, out_biases) + old

    pair = Pair(*gf)
    out = advance([pair], *rows_out(0))
    if SPLIT:
        cut = 2 * pair.other.shape[0] // 3
        f = [Chain(dp_size, pair.total()[:cut], (bits, turned)), Chain(dp_size, pair.total()[cut:], (deep, deep))]
    else:
        f = [Chain(dp_size, pair.total(), (bits, turned))]
    d, t, gqa, gqb, gqv = advance(f, attn_bwd, n, do, qkv, probs)
    pair = Pair(gqa, gqb)
    gin, gs1a = advance(f + [pair], *grad(0))
    q = Chain(dp_size, pair.total(), (bits, turned))
    gin, gs1b = advance(f + [q], *grad(1, gin))
    gin, gs1c = advance(f + [q], *grad(2, gin))
    flight = Flight(f)
    low = Pair(*flight.beside([], small_sums, idx, t, gs2, gs1a, gs1b, gs1c, gb1, gqv))
    out = flight.beside([q, low], *rows_out(1, out))
    flight.land()
    q.late = low.total()
    while len(f[0].steps) > 1:
        advance(f + [q])
    parts = [Slices(c, max(1, len(q.steps) - 1)) for c in f]
    out = advance(parts + [q], *rows_out(2, out))
    while f[0].steps:
        advance(parts + [q])
    g_f = jnp.concatenate([c.own for c in f])
    g_fc2 = g_f[:1024].astype(F32)
    g_fc1 = jnp.concatenate([g_f[1024:1536], g_f[1536:2048]], axis=1).astype(F32)
    g_proj = g_f[2048:].astype(F32)
    while q.steps:
        advance([q])
    g_qkv, g_qv, g_ob, g_gains, g_shifts, g_fc1_bias, g_table = finish(q.own, q.late)
    return out, gin, g_qkv, g_qv, g_proj, g_fc1, g_fc1_bias.reshape(-1), g_fc2, g_ob, g_gains, g_shifts, g_table


def solution(mesh):
    rows = P(("dp", "tp"), None)
    placed = (
        rows, P("dp"), P(), P(None, None, "tp"), P(None, "tp"), P("tp", None), P(None, "tp"), P("tp"),
        P("tp", None), P(), P(), P(), P(None, "tp"), rows,
    )
    results = (
        rows, rows, P(None, None, "tp"), P(None, "tp"), P("tp", None), P(None, "tp"), P("tp"), P("tp", None),
        P(), P(), P(), P(None, "tp"),
    )
    return jax.shard_map(
        functools.partial(per_device, mesh.shape["dp"]), mesh=mesh, in_specs=placed, out_specs=results, check_vma=False
    )
```

```python
import functools

import jax
import jax.numpy as jnp
from jax import lax
from jax.experimental import pallas as pl
from jax.experimental.pallas import tpu as pltpu
from jax.sharding import PartitionSpec as P

HEAD = 32
EPS = 1e-05
WIN = 100
WS = 10
TAB = 361
KEYS = 104
LANES = 128
SLAB = 256
GROUP = 4
ROWS = GROUP * WIN
DENSE = 480
THIRD = 2
CHUNK = 256
LOG2E = 1.4426950408889634
NEG = -1e30
BF = jnp.bfloat16
F32 = jnp.float32
NT = (((1,), (1,)), ((), ()))
TN = (((0,), (0,)), ((), ()))


def dot(a, b):
    return jnp.dot(a, b, preferred_element_type=F32)


def dot_nt(a, b):
    return lax.dot_general(a, b, NT, preferred_element_type=F32)


def dot_tn(a, b):
    return lax.dot_general(a, b, TN, preferred_element_type=F32)


def norm_parts(v):
    mean = jnp.mean(v, axis=-1, keepdims=True)
    centered = v - mean
    var = jnp.mean(centered * centered, axis=-1, keepdims=True)
    r = lax.rsqrt(var + EPS)
    return centered * r, r


def fold_rows(v):
    rows, cols = v.shape
    return jnp.sum(v.reshape(rows // 8, 8, cols), axis=0)


def lane_mask(rows, test):
    lane = lax.broadcasted_iota(jnp.int32, (rows, SLAB), 1)
    return jnp.where(test(lane), 1.0, 0.0).astype(BF)


def attn_fwd_body(
    x_ref, xb_ref, page_ref, rel_ref, ta_ref, tb_ref, wa_ref, wb_ref, qva_ref, qvb_ref, pa_ref, pb_ref, ob_ref, gain_ref,
    shift_ref,
    n_ref, qkv_ref, mixed_ref, att_ref, p_ref, idx_ref,
    scr, cur, nxt, att_scr, att_rows, bias_ref, turn,
):
    scale = (HEAD ** -0.5) * LOG2E

    @pl.when(pl.program_id(0) == 0)
    def _():
        scr[ROWS:, :] = jnp.zeros((scr.shape[0] - ROWS, scr.shape[1]), F32)

    def prepare():
        n, _ = norm_parts(x_ref[...].astype(F32))
        n = (n * gain_ref[0:1] + shift_ref[0:1]).astype(BF)
        n_ref[...] = n
        return n

    def project(n, i):
        for s, (w_ref, b_ref) in enumerate(((wa_ref, qva_ref), (wb_ref, qvb_ref))):
            cols = slice(512 * i + s * SLAB, 512 * i + s * SLAB + SLAB)
            out = dot(n, w_ref[i])
            scr[:ROWS, cols] = out if i == 1 else out + b_ref[i // 2 : i // 2 + 1]
        for w in range(GROUP):
            v = scr[w * WIN : w * WIN + LANES, 512 * i : 512 * i + 512].astype(BF)
            nxt[w, :, 512 * i : 512 * i + 512] = v
            qkv_ref[w, :, 512 * i : 512 * i + 512] = v

    def attend(beside):
        even = lane_mask(LANES, lambda c: (c // HEAD) % 2 == 0)
        odd = lane_mask(LANES, lambda c: (c // HEAD) % 2 == 1)
        low = lane_mask(KEYS, lambda c: c % 128 < 64)[:, :128]
        high = lane_mask(KEYS, lambda c: c % 128 >= 64)[:, :128]
        query_lane = lax.broadcasted_iota(jnp.int32, (1, SLAB), 1) % LANES
        valid = jnp.where(query_lane < WIN, 1.0, 0.0)
        first_head = lax.broadcasted_iota(jnp.int32, (2 * HEAD, LANES), 0) < HEAD
        for w in range(GROUP):
            pages = jnp.broadcast_to(page_ref[w], (LANES, LANES))
            mask = jnp.where(pages == pages.T, 0.0, NEG)[:KEYS]
            mask = jnp.concatenate([mask, mask], axis=1)
            scores, v_ts = [], []
            for s in range(2):
                lo = s * SLAB
                q = cur[w, :, lo : lo + SLAB]
                k = cur[w, :KEYS, 512 + lo : 512 + lo + SLAB]
                v_ts.append(cur[w, :, 1024 + lo : 1024 + lo + SLAB].T)
                q2 = jnp.concatenate([q * even, q * odd], axis=0)
                for p in range(4):
                    cols = slice(128 * (p // 2), 128 * (p // 2) + 128)
                    scores.append(dot_nt(k[:, cols] * (low if p % 2 == 0 else high), q2[:, cols]))
            beside(w)
            for s in range(2):
                outs = []
                for p in range(4):
                    st = scores[4 * s + p] * scale + bias_ref[4 * s + p] + mask
                    e = jnp.exp2(st - jnp.max(st, axis=0, keepdims=True))
                    pt = (e * (valid / jnp.sum(e, axis=0, keepdims=True))).astype(BF)
                    p_ref[w, 4 * s + p] = pt
                    ot = dot(v_ts[s][64 * p : 64 * p + 64, :KEYS], pt)
                    outs.append(jnp.where(first_head, ot[:, :LANES], ot[:, LANES:]))
                att_scr[w, :, s * SLAB : s * SLAB + SLAB] = jnp.concatenate(outs, axis=0).T
        for w in range(GROUP):
            att_rows[w * WIN : w * WIN + WIN, :] = att_scr[w, :WIN, :]
        att = att_rows[...].astype(BF)
        att_ref[...] = att
        mixed_ref[...] = (
            xb_ref[...].astype(F32) + ob_ref[0:1] + dot(att[:, :SLAB], pa_ref[...]) + dot(att[:, SLAB:], pb_ref[...])
        )

    step, end = pl.program_id(0), pl.num_programs(0) - 1

    @pl.when(step == 0)
    def _():
        n = prepare()
        for i in range(3):
            project(n, i)
        cur[...] = nxt[...]
        expand_table(rel_ref, ta_ref, tb_ref, bias_ref, idx_ref, turn)

    @pl.when((step > 0) & (step < end))
    def _():
        n = prepare()
        attend(lambda w: project(n, w) if w < 3 else None)
        cur[...] = nxt[...]

    @pl.when(step == end)
    def _():
        attend(lambda w: None)


def gelu_parts(h):
    phi = 0.5 + 0.5 * lax.erf(h * 0.7071067811865476)
    return phi, jnp.exp2(h * h * (-0.5 * LOG2E)) * 0.3989422804014327


def ffn_body(
    mixed_ref, go_ref, att_ref, w1a_ref, w1b_ref, w2a_ref, w2b_ref, b1a_ref, b1b_ref, pa_ref, pb_ref, gain_ref, shift_ref,
    act_ref, gm_ref, do_ref, gfa_ref, gfb_ref, gb1_ref, gs_ref,
    acc1, acc2, accp, accb, accs,
):
    step = pl.program_id(0)

    @pl.when(step == 0)
    def _():
        acc1[...] = jnp.zeros_like(acc1)
        acc2[...] = jnp.zeros_like(acc2)
        accp[...] = jnp.zeros_like(accp)
        accb[...] = jnp.zeros_like(accb)
        accs[...] = jnp.zeros_like(accs)

    mixed = mixed_ref[...]
    nh, r = norm_parts(mixed)
    n2 = (nh * gain_ref[1:2] + shift_ref[1:2]).astype(BF)
    go = go_ref[...]
    gn = jnp.zeros_like(mixed)
    per_half = 1024 // CHUNK

    def weights(c):
        col = slice(CHUNK * (c % per_half), CHUNK * (c % per_half) + CHUNK)
        return ((w1a_ref, w2a_ref, b1a_ref) if c < per_half else (w1b_ref, w2b_ref, b1b_ref)) + (col,)

    def front(c):
        w1_ref, w2_ref, b1_ref, col = weights(c)
        return dot(n2, w1_ref[:, col]) + b1_ref[0:1, col], dot_nt(go, w2_ref[col, :])

    ready = front(0)
    for c in range(2 * per_half):
        h, ga = ready
        if c + 1 < 2 * per_half:
            ready = front(c + 1)
        w1_ref, _, _, col = weights(c)
        full = slice(CHUNK * c, CHUNK * c + CHUNK)
        phi, density = gelu_parts(h)
        act = (h * phi).astype(BF)
        act_ref[:, full] = act
        ghf = ga * (phi + h * density)
        accb[:, full] += fold_rows(ghf)
        gh = ghf.astype(BF)
        gn += dot_nt(gh, w1_ref[:, col])
        acc2[full, :] += dot_tn(act, go)
        acc1[:, full] += dot_tn(n2, gh)
    gof = go.astype(F32)
    e = gn * gain_ref[1:2]
    gm = gof + r * (
        e - jnp.mean(e, axis=-1, keepdims=True) - nh * jnp.mean(e * nh, axis=-1, keepdims=True)
    )
    gm_ref[...] = gm
    gml = gm.astype(BF)
    accp[...] += dot_tn(att_ref[...], gml)
    do_ref[:, :SLAB] = dot_nt(gml, pa_ref[...]).astype(BF)
    do_ref[:, SLAB:] = dot_nt(gml, pb_ref[...]).astype(BF)
    accs[0] += fold_rows(gm)
    accs[1] += fold_rows(gof)
    accs[2] += fold_rows(gn * nh)
    accs[3] += fold_rows(gn)

    @pl.when(step == pl.num_programs(0) - 1)
    def _():
        for s, gf_ref in enumerate((gfa_ref, gfb_ref)):
            gf_ref[:1024] = acc2[1024 * s : 1024 * s + 1024, :].astype(BF)
            gf_ref[1024:1536] = acc1[:, 1024 * s : 1024 * s + 512].astype(BF)
            gf_ref[1536:2048] = acc1[:, 1024 * s + 512 : 1024 * s + 1024].astype(BF)
            gf_ref[2048:2304] = accp[SLAB * s : SLAB * s + SLAB, :].astype(BF)
        gb1_ref[...] = jnp.sum(accb[...], axis=0, keepdims=True)
        gs_ref[...] = jnp.sum(accs[...], axis=1)


def out_body(mixed_ref, act_ref, w2a_ref, w2b_ref, ob_ref, *refs):
    out_ref = refs[-1]
    out = mixed_ref[...] + ob_ref[1:2] + dot(act_ref[:, :1024], w2a_ref[...]) + dot(act_ref[:, 1024:], w2b_ref[...])
    out_ref[...] = out.astype(BF)


def attn_bwd_body(
    n_ref, do_ref, qkv_ref, p_ref, d_ref, t_ref, gqa_ref, gqb_ref, gqv_ref, scr, prev, acc, accb
):
    scale = HEAD ** -0.5
    step, end = pl.program_id(0), pl.num_programs(0) - 1

    @pl.when(step == 0)
    def _():
        scr[ROWS:, :512] = jnp.zeros((scr.shape[0] - ROWS, 512), F32)
        t_ref[...] = jnp.zeros_like(t_ref)
        prev[...] = jnp.zeros_like(prev)
        acc[...] = jnp.zeros_like(acc)
        accb[...] = jnp.zeros_like(accb)

    def weights(i):
        cols = slice(512 * i, 512 * i + 512)
        d = prev[:, cols]
        acc[:, cols] += dot_tn(n_ref[...], d)
        if i != 1:
            accb[i // 2] += fold_rows(d.astype(F32))

    def windows():
        scr[:ROWS, :512] = do_ref[...].astype(F32)
        row = lax.broadcasted_iota(jnp.int32, (LANES, 512), 0)
        dos = [jnp.where(row < WIN, scr[w * WIN : w * WIN + LANES, :512], 0.0).astype(BF) for w in range(GROUP)]
        even = lane_mask(LANES, lambda c: (c // HEAD) % 2 == 0)
        odd = lane_mask(LANES, lambda c: (c // HEAD) % 2 == 1)
        low = lane_mask(KEYS, lambda c: c % 128 < 64)[:, :128]
        high = lane_mask(KEYS, lambda c: c % 128 >= 64)[:, :128]
        first_head = lax.broadcasted_iota(jnp.int32, (2 * HEAD, LANES), 0) < HEAD
        first_pair = lax.broadcasted_iota(jnp.int32, (KEYS, 128), 1) < 64
        for w in range(GROUP):
            rows = slice(w * WIN, w * WIN + WIN)
            q2s, d2s, k_ts, dps = [], [], [], []
            for s in range(2):
                lo = s * SLAB
                q = qkv_ref[w, :, lo : lo + SLAB]
                v = qkv_ref[w, :KEYS, 1024 + lo : 1024 + lo + SLAB]
                do = dos[w][:, lo : lo + SLAB]
                q2s.append(jnp.concatenate([q * even, q * odd], axis=0))
                d2s.append(jnp.concatenate([do * even, do * odd], axis=0))
                k_ts.append(qkv_ref[w, :, 512 + lo : 512 + lo + SLAB].T)
                for p in range(4):
                    cols = slice(128 * (p // 2), 128 * (p // 2) + 128)
                    dps.append(dot_nt(v[:, cols] * (low if p % 2 == 0 else high), d2s[s][:, cols]))
            if w < 3:
                weights(w)
            for s in range(2):
                lo = s * SLAB
                outs, dks, dvs = [], [], []
                for p in range(4):
                    cols = slice(128 * (p // 2), 128 * (p // 2) + 128)
                    pt = p_ref[w, 4 * s + p]
                    ptf = pt.astype(F32)
                    dp = dps[4 * s + p]
                    ds = ptf * (dp - jnp.sum(dp * ptf, axis=0, keepdims=True))
                    t_ref[4 * s + p] += ds
                    ds = ds.astype(BF)
                    qt = dot(k_ts[s][64 * p : 64 * p + 64, :KEYS], ds)
                    outs.append(jnp.where(first_head, qt[:, :LANES], qt[:, LANES:]))
                    dks.append(dot(ds, q2s[s][:, cols]))
                    dvs.append(dot(pt, d2s[s][:, cols]))
                scr[rows, lo : lo + SLAB] = (jnp.concatenate(outs, axis=0).T * scale)[:WIN]
                for g in range(2):
                    cols = slice(512 + lo + 128 * g, 512 + lo + 128 * g + 128)
                    scr[rows, cols] = (jnp.where(first_pair, dks[2 * g], dks[2 * g + 1]) * scale)[:WIN]
                    cols = slice(1024 + lo + 128 * g, 1024 + lo + 128 * g + 128)
                    scr[rows, cols] = jnp.where(first_pair, dvs[2 * g], dvs[2 * g + 1])[:WIN]
        d = scr[:ROWS, :].astype(BF)
        d_ref[...] = d
        prev[...] = d

    @pl.when(step < end)
    def _():
        windows()

    @pl.when(step == end)
    def _():
        for i in range(3):
            weights(i)
        for s, gq_ref in enumerate((gqa_ref, gqb_ref)):
            for i in range(3):
                cols = slice(512 * i + SLAB * s, 512 * i + SLAB * s + SLAB)
                gq_ref[256 * i : 256 * i + 256, :256] = acc[:256, cols].astype(BF)
                gq_ref[256 * i : 256 * i + 256, 256:] = acc[256:, cols].astype(BF)
        gqv_ref[...] = jnp.sum(accb[...], axis=1)


def input_grad_body(x_ref, gm_ref, d_ref, wa_ref, wb_ref, gain_ref, *refs):
    gin_ref, gs_ref, accs = refs[-3:]
    step = pl.program_id(0)

    @pl.when(step == 0)
    def _():
        accs[...] = jnp.zeros_like(accs)

    gn = jnp.zeros(gm_ref.shape, F32)
    for i in range(3):
        for s, w_ref in enumerate((wa_ref, wb_ref)):
            gn += dot_nt(d_ref[:, 512 * i + SLAB * s : 512 * i + SLAB * s + SLAB], w_ref[i])
    nh, r = norm_parts(x_ref[...].astype(F32))
    e = gn * gain_ref[0:1]
    gin = gm_ref[...] + r * (
        e - jnp.mean(e, axis=-1, keepdims=True) - nh * jnp.mean(e * nh, axis=-1, keepdims=True)
    )
    gin_ref[...] = gin.astype(BF)
    accs[0] += fold_rows(gn * nh)
    accs[1] += fold_rows(gn)

    @pl.when(step == pl.num_programs(0) - 1)
    def _():
        gs_ref[...] = jnp.sum(accs[...], axis=1)


def shaped(shape, dtype):
    return jax.ShapeDtypeStruct(shape, dtype)


def whole(shape):
    return pl.BlockSpec(shape, lambda i: (0,) * len(shape))


def by_rows(*shape, rows=ROWS):
    return pl.BlockSpec((rows,) + shape, lambda i: (i,) + (0,) * len(shape))


def dense_rows(*shape):
    return by_rows(*shape, rows=DENSE)


def by_windows(*shape):
    return pl.BlockSpec((GROUP,) + shape, lambda i: (i,) + (0,) * len(shape))


PARAMS = pltpu.CompilerParams(vmem_limit_bytes=60 << 20, dimension_semantics=("arbitrary",))


def attn_fwd(x, pages, rel_index, ta, tb, wa, wb, qva, qvb, pa, pb, ob, gain, shift):
    rows = x.shape[0]
    windows = rows // WIN
    last = rows // ROWS - 1
    front = lambda *shape: pl.BlockSpec(shape, lambda i: (jnp.minimum(i, last),) + (0,) * (len(shape) - 1))
    back = lambda *shape: pl.BlockSpec(shape, lambda i: (jnp.maximum(i - 1, 0),) + (0,) * (len(shape) - 1))
    return pl.pallas_call(
        attn_fwd_body,
        name="attn_fwd",
        grid=(rows // ROWS + 1,),
        in_specs=[front(ROWS, 512), back(ROWS, 512), back(GROUP, 1, LANES)]
        + [whole(a.shape) for a in (rel_index, ta, tb, wa, wb, qva, qvb, pa, pb, ob, gain, shift)],
        out_specs=[
            front(ROWS, 512), front(GROUP, LANES, 1536), back(ROWS, 512), back(ROWS, 512),
            back(GROUP, 8, KEYS, SLAB), whole((16, SLAB)),
        ],
        out_shape=[
            shaped((rows, 512), BF),
            shaped((windows, LANES, 1536), BF),
            shaped((rows, 512), F32),
            shaped((rows, 512), BF),
            shaped((windows, 8, KEYS, SLAB), BF),
            shaped((16, SLAB), F32),
        ],
        scratch_shapes=[
            pltpu.VMEM((ROWS + 32, 1536), F32),
            pltpu.VMEM((GROUP, LANES, 1536), BF),
            pltpu.VMEM((GROUP, LANES, 1536), BF),
            pltpu.VMEM((GROUP, LANES, 512), F32),
            pltpu.VMEM((ROWS, 512), F32),
            pltpu.VMEM((8, KEYS, SLAB), F32),
            pltpu.VMEM((LANES, LANES), F32),
        ],
        compiler_params=PARAMS,
    )(x, x, pages, rel_index, ta, tb, wa, wb, qva, qvb, pa, pb, ob, gain, shift)


def cost(flops, moved):
    return pl.CostEstimate(flops=int(flops), bytes_accessed=int(moved), transcendentals=0)


def ffn(mixed, go, att, w1a, w1b, w2a, w2b, b1a, b1b, pa, pb, gain, shift):
    rows = mixed.shape[0]
    small = [w1a, w1b, w2a, w2b, b1a, b1b, pa, pb, gain, shift]
    return pl.pallas_call(
        ffn_body,
        name="feed_forward",
        grid=(rows // DENSE,),
        in_specs=[dense_rows(512)] * 3 + [whole(a.shape) for a in small],
        out_specs=[dense_rows(2048), dense_rows(512), dense_rows(512)]
        + [whole((2304, 512)), whole((2304, 512)), whole((1, 2048)), whole((4, 512))],
        out_shape=[
            shaped((rows, 2048), BF),
            shaped((rows, 512), F32),
            shaped((rows, 512), BF),
            shaped((2304, 512), BF),
            shaped((2304, 512), BF),
            shaped((1, 2048), F32),
            shaped((4, 512), F32),
        ],
        scratch_shapes=[
            pltpu.VMEM((512, 2048), F32),
            pltpu.VMEM((2048, 512), F32),
            pltpu.VMEM((512, 512), F32),
            pltpu.VMEM((8, 2048), F32),
            pltpu.VMEM((4, 8, 512), F32),
        ],
        compiler_params=PARAMS,
        cost_estimate=cost(50e9, 40e6),
    )(mixed, go, att, *small)


def third_rows(part):
    return lambda *shape: pl.BlockSpec((ROWS,) + shape, lambda i: (THIRD * part + i,) + (0,) * len(shape))


def out_rows(part, mixed, act, w2a, w2b, ob, *old):
    rows = mixed.shape[0]
    spec = third_rows(part)
    return pl.pallas_call(
        out_body,
        name="block_out",
        grid=(THIRD,),
        in_specs=[spec(512), spec(2048)] + [whole(a.shape) for a in (w2a, w2b, ob)] + [pl.BlockSpec(memory_space=pl.ANY)] * len(old),
        out_specs=spec(512),
        out_shape=shaped((rows, 512), BF),
        input_output_aliases={5: 0} if old else {},
        compiler_params=PARAMS,
        cost_estimate=cost(3e9, 7e6),
    )(mixed, act, w2a, w2b, ob, *old)


def attn_bwd(n, do, qkv, probs):
    rows = n.shape[0]
    last = rows // ROWS - 1
    front = lambda *shape: pl.BlockSpec(shape, lambda i: (jnp.minimum(i, last),) + (0,) * (len(shape) - 1))
    back = lambda *shape: pl.BlockSpec(shape, lambda i: (jnp.maximum(i - 1, 0),) + (0,) * (len(shape) - 1))
    return pl.pallas_call(
        attn_bwd_body,
        name="attn_bwd",
        grid=(rows // ROWS + 1,),
        in_specs=[back(ROWS, 512), front(ROWS, 512), front(GROUP, LANES, 1536), front(GROUP, 8, KEYS, SLAB)],
        out_specs=[
            front(ROWS, 1536), whole((8, KEYS, SLAB)), whole((768, 512)), whole((768, 512)), whole((2, 512)),
        ],
        out_shape=[
            shaped((rows, 1536), BF), shaped((8, KEYS, SLAB), F32), shaped((768, 512), BF), shaped((768, 512), BF),
            shaped((2, 512), F32),
        ],
        scratch_shapes=[
            pltpu.VMEM((ROWS + 32, 1536), F32),
            pltpu.VMEM((ROWS, 1536), BF),
            pltpu.VMEM((512, 1536), F32),
            pltpu.VMEM((2, 8, 512), F32),
        ],
        compiler_params=PARAMS,
        cost_estimate=cost(30e9, 60e6),
    )(n, do, qkv, probs)


def input_grad(part, x, gm, d, wa, wb, gain, *old):
    rows = x.shape[0]
    spec = third_rows(part)
    return pl.pallas_call(
        input_grad_body,
        name="input_grad",
        grid=(THIRD,),
        in_specs=[spec(512), spec(512), spec(1536)] + [whole(a.shape) for a in (wa, wb, gain)] + [pl.BlockSpec(memory_space=pl.ANY)] * len(old),
        out_specs=[spec(512), whole((2, 512))],
        out_shape=[shaped((rows, 512), BF), shaped((2, 512), F32)],
        scratch_shapes=[pltpu.VMEM((2, 8, 512), F32)],
        input_output_aliases={6: 0} if old else {},
        compiler_params=PARAMS,
        cost_estimate=cost(3e9, 7e6),
    )(x, gm, d, wa, wb, gain, *old)


def offset_onehot(index_row):
    slot = lax.broadcasted_iota(jnp.int32, (TAB, SLAB), 0).astype(F32)
    return jnp.where(slot == index_row, 1.0, 0.0).astype(BF)


def expand_table(rel_ref, ta_ref, tb_ref, bias_ref, idx_ref, scr):
    scr[...] = jnp.zeros_like(scr)
    scr[:WIN, :WIN] = rel_ref[...].astype(F32)
    scr[...] = scr[...].T
    lane = lax.broadcasted_iota(jnp.int32, (16, SLAB), 1)
    blank = jnp.zeros((16, SLAB - LANES), F32)

    def place(row, width, at):
        piece = jnp.concatenate([scr[row : row + 16, :], blank], axis=1)
        return pltpu.roll(jnp.where(lane < width, piece, 0.0), at, 1)

    idx = place(0, WIN, WIN - WS)
    for d in range(WS - 1):
        idx += place(WS * (WS - 1 - d), WS, WS * d)
    idx = jnp.where(lane < WIN + WIN - WS, idx, -1.0)
    idx_ref[...] = idx
    table = jnp.concatenate([ta_ref[...], tb_ref[...]], axis=0) * LOG2E
    high = table.astype(BF)
    rest = table - high.astype(F32)
    mid = rest.astype(BF)
    table = jnp.concatenate([high, mid, (rest - mid.astype(F32)).astype(BF)], axis=0)
    row = lax.broadcasted_iota(jnp.int32, (16, 48), 0)
    col = lax.broadcasted_iota(jnp.int32, (16, 48), 1)
    pick = jnp.where(col % 16 == 2 * (row % 8) + row // 8, 1.0, 0.0).astype(BF)
    for jx in range(WS):
        values = dot(pick, dot(table, offset_onehot(idx[jx : jx + 1])).astype(BF))
        for jy in range(WS):
            shift = WS * (WS - 1 - jy)
            moved = pltpu.roll(values, (SLAB - shift) % SLAB, 1) if shift else values
            bias_ref[:, WS * jy + jx, :LANES] = moved[:8, :LANES]
            bias_ref[:, WS * jy + jx, LANES:] = moved[8:, :LANES]
    for key in range(WIN, KEYS):
        bias_ref[:, key, :] = jnp.zeros((8, SLAB), F32)


def small_body(idx_ref, t_ref, gs2_ref, gs1a_ref, gs1b_ref, gs1c_ref, gb1_ref, gqv_ref, own_ref, other_ref, scr):
    total = jnp.zeros((32, TAB), F32)
    blank = jnp.zeros((8, SLAB - LANES), F32)
    for jx in range(WS):
        even = jnp.zeros((8, SLAB), F32)
        odd = jnp.zeros((8, SLAB), F32)
        for jy in range(WS):
            shift = WS * (WS - 1 - jy)
            even += pltpu.roll(jnp.concatenate([t_ref[:, WS * jy + jx, :LANES], blank], axis=1), shift, 1)
            odd += pltpu.roll(jnp.concatenate([t_ref[:, WS * jy + jx, LANES:], blank], axis=1), shift, 1)
        heads = jnp.concatenate([even, odd], axis=0)
        high = heads.astype(BF)
        rest = (heads - high.astype(F32)).astype(BF)
        total += dot_nt(jnp.concatenate([high, rest], axis=0), offset_onehot(idx_ref[jx : jx + 1]))
    total = total[:16] + total[16:]
    for s, out_ref in enumerate((own_ref, other_ref)):
        scr[...] = jnp.zeros_like(scr)
        scr[0:4] = gs2_ref[...]
        scr[4:6] = gs1a_ref[...] + gs1b_ref[...] + gs1c_ref[...]
        scr[6:7] = gb1_ref[:, 1024 * s : 1024 * s + 512]
        scr[7:8] = gb1_ref[:, 1024 * s + 512 : 1024 * s + 1024]
        scr[8:9, :SLAB] = gqv_ref[0:1, SLAB * s : SLAB * s + SLAB]
        scr[8:9, SLAB:] = gqv_ref[1:2, SLAB * s : SLAB * s + SLAB]
        scr[16:20, :TAB] = total[4 * s : 4 * s + 4]
        scr[20:24, :TAB] = total[8 + 4 * s : 12 + 4 * s]
        out_ref[...] = scr[...].astype(BF)


def small_sums(*args):
    return pl.pallas_call(
        small_body,
        name="small_sums",
        out_shape=[shaped((32, 512), BF), shaped((32, 512), BF)],
        scratch_shapes=[pltpu.VMEM((32, 512), F32)],
        compiler_params=pltpu.CompilerParams(vmem_limit_bytes=16 << 20),
        cost_estimate=cost(3e9, 1e6),
    )(*args)


def finish_body(q_ref, late_ref, gq_ref, gqv_ref, gob_ref, gg_ref, gh_ref, gb1_ref, gt_ref, scr):
    for i in range(3):
        q = q_ref[256 * i : 256 * i + 256, :].astype(F32)
        gq_ref[i, :256, :] = q[:, :256]
        gq_ref[i, 256:, :] = q[:, 256:]
    late = late_ref[...].astype(F32)
    gob_ref[...] = late[0:2]
    gg_ref[0:1] = late[4:5]
    gg_ref[1:2] = late[2:3]
    gh_ref[0:1] = late[5:6]
    gh_ref[1:2] = late[3:4]
    gb1_ref[:, :512] = late[6:7]
    gb1_ref[:, 512:] = late[7:8]
    gqv_ref[0:1] = late[8:9, :SLAB]
    gqv_ref[1:2] = late[8:9, SLAB:]
    for h in range(8):
        r = 16 + 4 * (h % 2) + h // 2
        scr[h : h + 1, :] = late[r : r + 1, :]
    gt_ref[...] = scr[:, :TAB]


def finish(q, late):
    return pl.pallas_call(
        finish_body,
        name="finish",
        out_shape=[
            shaped((3, 512, SLAB), F32), shaped((2, SLAB), F32), shaped((2, 512), F32), shaped((2, 512), F32),
            shaped((2, 512), F32), shaped((1, 1024), F32), shaped((8, TAB), F32),
        ],
        scratch_shapes=[pltpu.VMEM((8, 512), F32)],
        compiler_params=pltpu.CompilerParams(vmem_limit_bytes=16 << 20),
        cost_estimate=cost(1e9, 4e6),
    )(q, late)


SWAP = [(0, 1), (1, 0)]
SPLIT = True


def dp_bits(size):
    bits = []
    while 1 << len(bits) < size:
        bits.append(1 << len(bits))
    return bits


class Chain:
    def __init__(self, size, own, orders):
        self.orders, self.size, self.own, self.late = orders, size, own, None
        tp, dp = lax.axis_index("tp"), lax.axis_index("dp")
        self.upper = [jnp.where(tp == 0, dp & p, dp & q) != 0 for p, q in zip(*orders)]
        last = len(orders[0]) - 1
        self.steps = [("half", k) for k in range(last)] + [("full", last)]
        self.steps += [("join", k) for k in range(last - 1, -1, -1)]

    def begin(self):
        kind, k = self.steps[0]
        if kind == "half":
            half = self.own.shape[0] // 2
            up = self.upper[k].astype(jnp.int32)
            send = lax.dynamic_slice_in_dim(self.own, (1 - up) * half, half, 0)
            self.own = lax.dynamic_slice_in_dim(self.own, up * half, half, 0)
            return send
        if self.late is not None:
            return jnp.concatenate([self.own, self.late], axis=0)
        return self.own

    def move(self, send):
        k = self.steps[0][1]
        perm = [(2 * i + t, 2 * (i ^ self.orders[t][k]) + t) for i in range(self.size) for t in range(2)]
        return lax.ppermute(send, ("dp", "tp"), perm)

    def end(self, got):
        kind, k = self.steps.pop(0)
        if kind in ("full", "join") and self.late is not None:
            rows = self.own.shape[0]
            self.late = self.late + got[rows:]
            got = got[:rows]
        if kind == "join":
            up = self.upper[k]
            self.own = jnp.concatenate([jnp.where(up, got, self.own), jnp.where(up, self.own, got)], axis=0)
        else:
            self.own = self.own + got


class Pair:
    def __init__(self, own, other):
        self.own, self.other = own, other

    def begin(self):
        return self.other

    def move(self, send):
        return lax.ppermute(send, "tp", SWAP)

    def end(self, got):
        self.got = got

    def total(self):
        return self.own + self.got


tie = lax.optimization_barrier


def advance(chains, work=None, *inputs):
    sends, inputs = tie(([c.begin() for c in chains], inputs))
    gots = [c.move(v) for c, v in zip(chains, sends)]
    result = None if work is None else work(*inputs)
    gots, result = tie((gots, result))
    for c, got in zip(chains, gots):
        c.end(got)
    return result


class Flight:
    def __init__(self, chains):
        self.chains, self.sends, self.gots = chains, [c.begin() for c in chains], None

    def beside(self, chains, work, *inputs):
        sends = [c.begin() for c in chains]
        self.sends, sends, inputs = tie((self.sends, sends, inputs))
        if self.gots is None:
            self.gots = [c.move(v) for c, v in zip(self.chains, self.sends)]
        gots = [c.move(v) for c, v in zip(chains, sends)]
        gots, result = tie((gots, work(*inputs)))
        self.last = (gots, result)
        for c, got in zip(chains, gots):
            c.end(got)
        return result

    def land(self):
        self.gots, _ = tie((self.gots, self.last))
        for c, got in zip(self.chains, self.gots):
            c.end(got)


class Slices:
    def __init__(self, chain, count):
        self.chain, self.send, self.gots = chain, chain.begin(), []
        rows = self.send.shape[0]
        self.cuts = [rows * i // count // 8 * 8 for i in range(count)] + [rows]

    def begin(self):
        i = len(self.gots)
        return self.send[self.cuts[i] : self.cuts[i + 1]]

    def move(self, send):
        return self.chain.move(send)

    def end(self, got):
        self.gots.append(got)
        if len(self.gots) + 1 == len(self.cuts):
            self.chain.end(jnp.concatenate(self.gots, axis=0))


def forward(x, pages, rel_index, ta, tb, wa, wb, qva, qvb, pa, pb, w1a, w1b, b1a, b1b, w2a, w2b, ob, gain, shift, go):
    n, qkv, mixed, att, probs, idx = attn_fwd(x, pages, rel_index, ta, tb, wa, wb, qva, qvb, pa, pb, ob, gain, shift)
    act, gm, do, gfa, gfb, gb1, gs2 = ffn(mixed, go, att, w1a, w1b, w2a, w2b, b1a, b1b, pa, pb, gain, shift)
    return idx, mixed, n, qkv, probs, act, gm, do, (gfa, gfb), gb1, gs2


def local_block(x, pages, rel_index, wa, wb, qva, qvb, pa, pb, w1a, w1b, b1a, b1b, w2a, w2b, ob, gain, shift, ta, tb, go):
    idx, mixed, n, qkv, probs, act, gm, do, gf, gb1, gs2 = forward(
        x, pages, rel_index, ta.T, tb.T, wa, wb, qva, qvb, pa, pb, w1a, w1b, b1a, b1b, w2a, w2b, ob, gain, shift, go
    )
    d, t, gqa, gqb, gqv = attn_bwd(n, do, qkv, probs)
    gin, out, sums = (), (), []
    for i in range(3):
        *gin, part = input_grad(i, x, gm, d, wa, wb, gain, *gin)
        sums.append(part)
        out = [out_rows(i, mixed, act, w2a, w2b, ob, *out)]
    own, other = small_sums(idx, t, gs2, *sums, gb1, gqv)
    gin, out = gin[0], out[0]
    return out, gin, gf, finish(gqa, own), finish(gqb, other)


def per_device(
    dp_size, inputs, page_of, rel_index, w_qkv, qv_bias, w_proj, w_fc1, fc1_bias, w_fc2, out_biases, norm_gains,
    norm_biases, bias_table, out_grad,
):
    me = lax.axis_index("tp")
    windows = inputs.shape[0] // WIN
    swap = lambda v: lax.ppermute(v, "tp", SWAP)
    pages = lax.dynamic_slice_in_dim(page_of.reshape(2 * windows, WIN), me * windows, windows, 0)
    pages = jnp.pad(pages.astype(F32), ((0, 0), (0, LANES - WIN)), constant_values=-1.0)[:, None, :]
    table = bias_table.T
    w_qkv_b, qv_bias_b, w_proj_b, table_b = (swap(v) for v in (w_qkv, qv_bias, w_proj, table))
    later, w_qkv_b, qv_bias_b, w_proj_b, table_b, pages = tie(
        ((w_fc1, fc1_bias, w_fc2), w_qkv_b, qv_bias_b, w_proj_b, table_b, pages)
    )
    w_fc1_b, fc1_bias_b, w_fc2_b = (swap(v) for v in later)
    idx, mixed, n, qkv, probs, act, gm, do, gf, gb1, gs2 = forward(
        inputs, pages, rel_index, table, table_b, w_qkv, w_qkv_b, qv_bias, qv_bias_b, w_proj, w_proj_b, w_fc1, w_fc1_b,
        fc1_bias[None], fc1_bias_b[None], w_fc2, w_fc2_b, out_biases, norm_gains, norm_biases, out_grad,
    )
    bits = dp_bits(dp_size)
    turned = bits[1:] + bits[:1]
    mid = len(bits) // 2
    deep = bits[mid:-1] + bits[:mid] + bits[-1:]
    grad = lambda i, *old: (functools.partial(input_grad, i), inputs, gm, d, w_qkv, w_qkv_b, norm_gains) + old
    rows_out = lambda i, *old: (functools.partial(out_rows, i), mixed, act, w_fc2, w_fc2_b, out_biases) + old

    pair = Pair(*gf)
    out = advance([pair], *rows_out(0))
    if SPLIT:
        cut = 2 * pair.other.shape[0] // 3
        f = [Chain(dp_size, pair.total()[:cut], (bits, turned)), Chain(dp_size, pair.total()[cut:], (deep, deep))]
    else:
        f = [Chain(dp_size, pair.total(), (bits, turned))]
    d, t, gqa, gqb, gqv = advance(f, attn_bwd, n, do, qkv, probs)
    pair = Pair(gqa, gqb)
    gin, gs1a = advance(f + [pair], *grad(0))
    q = Chain(dp_size, pair.total(), (bits, turned))
    gin, gs1b = advance(f + [q], *grad(1, gin))
    gin, gs1c = advance(f + [q], *grad(2, gin))
    flight = Flight(f)
    low = Pair(*flight.beside([], small_sums, idx, t, gs2, gs1a, gs1b, gs1c, gb1, gqv))
    out = flight.beside([q, low], *rows_out(1, out))
    flight.land()
    q.late = low.total()
    while len(f[0].steps) > 1:
        advance(f + [q])
    parts = [Slices(c, max(1, len(q.steps) - 1)) for c in f]
    out = advance(parts + [q], *rows_out(2, out))
    while f[0].steps:
        advance(parts + [q])
    g_f = jnp.concatenate([c.own for c in f])
    g_fc2 = g_f[:1024].astype(F32)
    g_fc1 = jnp.concatenate([g_f[1024:1536], g_f[1536:2048]], axis=1).astype(F32)
    g_proj = g_f[2048:].astype(F32)
    while q.steps:
        advance([q])
    g_qkv, g_qv, g_ob, g_gains, g_shifts, g_fc1_bias, g_table = finish(q.own, q.late)
    return out, gin, g_qkv, g_qv, g_proj, g_fc1, g_fc1_bias.reshape(-1), g_fc2, g_ob, g_gains, g_shifts, g_table.T


def solution(mesh):
    rows = P(("dp", "tp"), None)
    placed = (
        rows, P("dp"), P(), P(None, None, "tp"), P(None, "tp"), P("tp", None), P(None, "tp"), P("tp"),
        P("tp", None), P(), P(), P(), P(None, "tp"), rows,
    )
    results = (
        rows, rows, P(None, None, "tp"), P(None, "tp"), P("tp", None), P(None, "tp"), P("tp"), P("tp", None),
        P(), P(), P(), P(None, "tp"),
    )
    return jax.shard_map(
        functools.partial(per_device, mesh.shape["dp"]), mesh=mesh, in_specs=placed, out_specs=results, check_vma=False
    )
```

```python
import functools

import jax
import jax.numpy as jnp
from jax import lax
from jax.experimental import pallas as pl
from jax.experimental.pallas import tpu as pltpu
from jax.sharding import PartitionSpec as P

HEAD = 32
EPS = 1e-05
WIN = 100
WS = 10
TAB = 361
KEYS = 104
LANES = 128
SLAB = 256
GROUP = 4
ROWS = GROUP * WIN
DENSE = 480
THIRD = 2
CHUNK = 256
LOG2E = 1.4426950408889634
NEG = -1e30
BF = jnp.bfloat16
F32 = jnp.float32
NT = (((1,), (1,)), ((), ()))
TN = (((0,), (0,)), ((), ()))


def dot(a, b):
    return jnp.dot(a, b, preferred_element_type=F32)


def dot_nt(a, b):
    return lax.dot_general(a, b, NT, preferred_element_type=F32)


def dot_tn(a, b):
    return lax.dot_general(a, b, TN, preferred_element_type=F32)


def norm_parts(v):
    mean = jnp.mean(v, axis=-1, keepdims=True)
    centered = v - mean
    var = jnp.mean(centered * centered, axis=-1, keepdims=True)
    r = lax.rsqrt(var + EPS)
    return centered * r, r


def fold_rows(v):
    rows, cols = v.shape
    return jnp.sum(v.reshape(rows // 8, 8, cols), axis=0)


def lane_mask(rows, test):
    lane = lax.broadcasted_iota(jnp.int32, (rows, SLAB), 1)
    return jnp.where(test(lane), 1.0, 0.0).astype(BF)


def attn_fwd_body(
    x_ref, xb_ref, page_ref, rel_ref, ta_ref, tb_ref, wa_ref, wb_ref, qva_ref, qvb_ref, pa_ref, pb_ref, ob_ref, gain_ref,
    shift_ref,
    n_ref, qkv_ref, mixed_ref, att_ref, p_ref, idx_ref,
    scr, cur, nxt, att_scr, att_rows, bias_ref, turn,
):
    scale = (HEAD ** -0.5) * LOG2E

    @pl.when(pl.program_id(0) == 0)
    def _():
        scr[ROWS:, :] = jnp.zeros((scr.shape[0] - ROWS, scr.shape[1]), F32)

    def prepare():
        n, _ = norm_parts(x_ref[...].astype(F32))
        n = (n * gain_ref[0:1] + shift_ref[0:1]).astype(BF)
        n_ref[...] = n
        return n

    def project(n, i):
        for s, (w_ref, b_ref) in enumerate(((wa_ref, qva_ref), (wb_ref, qvb_ref))):
            cols = slice(512 * i + s * SLAB, 512 * i + s * SLAB + SLAB)
            out = dot(n, w_ref[i])
            scr[:ROWS, cols] = out if i == 1 else out + b_ref[i // 2 : i // 2 + 1]
        for w in range(GROUP):
            v = scr[w * WIN : w * WIN + LANES, 512 * i : 512 * i + 512].astype(BF)
            nxt[w, :, 512 * i : 512 * i + 512] = v
            qkv_ref[w, :, 512 * i : 512 * i + 512] = v

    def attend(beside):
        even = lane_mask(LANES, lambda c: (c // HEAD) % 2 == 0)
        odd = lane_mask(LANES, lambda c: (c // HEAD) % 2 == 1)
        low = lane_mask(KEYS, lambda c: c % 128 < 64)[:, :128]
        high = lane_mask(KEYS, lambda c: c % 128 >= 64)[:, :128]
        query_lane = lax.broadcasted_iota(jnp.int32, (1, SLAB), 1) % LANES
        valid = jnp.where(query_lane < WIN, 1.0, 0.0)
        first_head = lax.broadcasted_iota(jnp.int32, (2 * HEAD, LANES), 0) < HEAD
        for w in range(GROUP):
            pages = jnp.broadcast_to(page_ref[w], (LANES, LANES))
            mask = jnp.where(pages == pages.T, 0.0, NEG)[:KEYS]
            mask = jnp.concatenate([mask, mask], axis=1)
            scores, v_ts = [], []
            for s in range(2):
                lo = s * SLAB
                q = cur[w, :, lo : lo + SLAB]
                k = cur[w, :KEYS, 512 + lo : 512 + lo + SLAB]
                v_ts.append(cur[w, :, 1024 + lo : 1024 + lo + SLAB].T)
                q2 = jnp.concatenate([q * even, q * odd], axis=0)
                for p in range(4):
                    cols = slice(128 * (p // 2), 128 * (p // 2) + 128)
                    scores.append(dot_nt(k[:, cols] * (low if p % 2 == 0 else high), q2[:, cols]))
            beside(w)
            for s in range(2):
                outs = []
                for p in range(4):
                    st = scores[4 * s + p] * scale + bias_ref[4 * s + p] + mask
                    e = jnp.exp2(st - jnp.max(st, axis=0, keepdims=True))
                    pt = (e * (valid / jnp.sum(e, axis=0, keepdims=True))).astype(BF)
                    p_ref[w, 4 * s + p] = pt
                    ot = dot(v_ts[s][64 * p : 64 * p + 64, :KEYS], pt)
                    outs.append(jnp.where(first_head, ot[:, :LANES], ot[:, LANES:]))
                att_scr[w, :, s * SLAB : s * SLAB + SLAB] = jnp.concatenate(outs, axis=0).T
        for w in range(GROUP):
            att_rows[w * WIN : w * WIN + WIN, :] = att_scr[w, :WIN, :]
        att = att_rows[...].astype(BF)
        att_ref[...] = att
        mixed_ref[...] = (
            xb_ref[...].astype(F32) + ob_ref[0:1] + dot(att[:, :SLAB], pa_ref[...]) + dot(att[:, SLAB:], pb_ref[...])
        )

    step, end = pl.program_id(0), pl.num_programs(0) - 1

    @pl.when(step == 0)
    def _():
        n = prepare()
        for i in range(3):
            project(n, i)
        cur[...] = nxt[...]
        expand_table(rel_ref, ta_ref, tb_ref, bias_ref, idx_ref, turn)

    @pl.when((step > 0) & (step < end))
    def _():
        n = prepare()
        attend(lambda w: project(n, w) if w < 3 else None)
        cur[...] = nxt[...]

    @pl.when(step == end)
    def _():
        attend(lambda w: None)


def gelu_parts(h):
    phi = 0.5 + 0.5 * lax.erf(h * 0.7071067811865476)
    return phi, jnp.exp2(h * h * (-0.5 * LOG2E)) * 0.3989422804014327


def ffn_body(
    mixed_ref, go_ref, att_ref, w1a_ref, w1b_ref, w2a_ref, w2b_ref, b1a_ref, b1b_ref, pa_ref, pb_ref, gain_ref, shift_ref,
    act_ref, gm_ref, do_ref, gfa_ref, gfb_ref, gb1_ref, gs_ref,
    acc1, acc2, accp, accb, accs,
):
    step = pl.program_id(0)

    @pl.when(step == 0)
    def _():
        acc1[...] = jnp.zeros_like(acc1)
        acc2[...] = jnp.zeros_like(acc2)
        accp[...] = jnp.zeros_like(accp)
        accb[...] = jnp.zeros_like(accb)
        accs[...] = jnp.zeros_like(accs)

    mixed = mixed_ref[...]
    nh, r = norm_parts(mixed)
    n2 = (nh * gain_ref[1:2] + shift_ref[1:2]).astype(BF)
    go = go_ref[...]
    gn = jnp.zeros_like(mixed)
    per_half = 1024 // CHUNK

    def weights(c):
        col = slice(CHUNK * (c % per_half), CHUNK * (c % per_half) + CHUNK)
        return ((w1a_ref, w2a_ref, b1a_ref) if c < per_half else (w1b_ref, w2b_ref, b1b_ref)) + (col,)

    def front(c):
        w1_ref, w2_ref, b1_ref, col = weights(c)
        return dot(n2, w1_ref[:, col]) + b1_ref[0:1, col], dot_nt(go, w2_ref[col, :])

    ready = front(0)
    for c in range(2 * per_half):
        h, ga = ready
        if c + 1 < 2 * per_half:
            ready = front(c + 1)
        w1_ref, _, _, col = weights(c)
        full = slice(CHUNK * c, CHUNK * c + CHUNK)
        phi, density = gelu_parts(h)
        act = (h * phi).astype(BF)
        act_ref[:, full] = act
        ghf = ga * (phi + h * density)
        accb[:, full] += fold_rows(ghf)
        gh = ghf.astype(BF)
        gn += dot_nt(gh, w1_ref[:, col])
        acc2[full, :] += dot_tn(act, go)
        acc1[:, full] += dot_tn(n2, gh)
    gof = go.astype(F32)
    e = gn * gain_ref[1:2]
    gm = gof + r * (
        e - jnp.mean(e, axis=-1, keepdims=True) - nh * jnp.mean(e * nh, axis=-1, keepdims=True)
    )
    gm_ref[...] = gm
    gml = gm.astype(BF)
    accp[...] += dot_tn(att_ref[...], gml)
    do_ref[:, :SLAB] = dot_nt(gml, pa_ref[...]).astype(BF)
    do_ref[:, SLAB:] = dot_nt(gml, pb_ref[...]).astype(BF)
    accs[0] += fold_rows(gm)
    accs[1] += fold_rows(gof)
    accs[2] += fold_rows(gn * nh)
    accs[3] += fold_rows(gn)

    @pl.when(step == pl.num_programs(0) - 1)
    def _():
        for s, gf_ref in enumerate((gfa_ref, gfb_ref)):
            gf_ref[:1024] = acc2[1024 * s : 1024 * s + 1024, :].astype(BF)
            gf_ref[1024:1536] = acc1[:, 1024 * s : 1024 * s + 512].astype(BF)
            gf_ref[1536:2048] = acc1[:, 1024 * s + 512 : 1024 * s + 1024].astype(BF)
            gf_ref[2048:2304] = accp[SLAB * s : SLAB * s + SLAB, :].astype(BF)
        gb1_ref[...] = jnp.sum(accb[...], axis=0, keepdims=True)
        gs_ref[...] = jnp.sum(accs[...], axis=1)


def out_body(mixed_ref, act_ref, w2a_ref, w2b_ref, ob_ref, *refs):
    out_ref = refs[-1]
    out = mixed_ref[...] + ob_ref[1:2] + dot(act_ref[:, :1024], w2a_ref[...]) + dot(act_ref[:, 1024:], w2b_ref[...])
    out_ref[...] = out.astype(BF)


def attn_bwd_body(
    n_ref, do_ref, qkv_ref, p_ref, d_ref, t_ref, gqa_ref, gqb_ref, gqv_ref, scr, prev, acc, accb
):
    scale = HEAD ** -0.5
    step, end = pl.program_id(0), pl.num_programs(0) - 1

    @pl.when(step == 0)
    def _():
        scr[ROWS:, :512] = jnp.zeros((scr.shape[0] - ROWS, 512), F32)
        t_ref[...] = jnp.zeros_like(t_ref)
        prev[...] = jnp.zeros_like(prev)
        acc[...] = jnp.zeros_like(acc)
        accb[...] = jnp.zeros_like(accb)

    def weights(i):
        cols = slice(512 * i, 512 * i + 512)
        d = prev[:, cols]
        acc[:, cols] += dot_tn(n_ref[...], d)
        if i != 1:
            accb[i // 2] += fold_rows(d.astype(F32))

    def windows():
        scr[:ROWS, :512] = do_ref[...].astype(F32)
        row = lax.broadcasted_iota(jnp.int32, (LANES, 512), 0)
        dos = [jnp.where(row < WIN, scr[w * WIN : w * WIN + LANES, :512], 0.0).astype(BF) for w in range(GROUP)]
        even = lane_mask(LANES, lambda c: (c // HEAD) % 2 == 0)
        odd = lane_mask(LANES, lambda c: (c // HEAD) % 2 == 1)
        low = lane_mask(KEYS, lambda c: c % 128 < 64)[:, :128]
        high = lane_mask(KEYS, lambda c: c % 128 >= 64)[:, :128]
        first_head = lax.broadcasted_iota(jnp.int32, (2 * HEAD, LANES), 0) < HEAD
        first_pair = lax.broadcasted_iota(jnp.int32, (KEYS, 128), 1) < 64
        for w in range(GROUP):
            rows = slice(w * WIN, w * WIN + WIN)
            q2s, d2s, k_ts, dps = [], [], [], []
            for s in range(2):
                lo = s * SLAB
                q = qkv_ref[w, :, lo : lo + SLAB]
                v = qkv_ref[w, :KEYS, 1024 + lo : 1024 + lo + SLAB]
                do = dos[w][:, lo : lo + SLAB]
                q2s.append(jnp.concatenate([q * even, q * odd], axis=0))
                d2s.append(jnp.concatenate([do * even, do * odd], axis=0))
                k_ts.append(qkv_ref[w, :, 512 + lo : 512 + lo + SLAB].T)
                for p in range(4):
                    cols = slice(128 * (p // 2), 128 * (p // 2) + 128)
                    dps.append(dot_nt(v[:, cols] * (low if p % 2 == 0 else high), d2s[s][:, cols]))
            if w < 3:
                weights(w)
            for s in range(2):
                lo = s * SLAB
                outs, dks, dvs = [], [], []
                for p in range(4):
                    cols = slice(128 * (p // 2), 128 * (p // 2) + 128)
                    pt = p_ref[w, 4 * s + p]
                    ptf = pt.astype(F32)
                    dp = dps[4 * s + p]
                    ds = ptf * (dp - jnp.sum(dp * ptf, axis=0, keepdims=True))
                    t_ref[4 * s + p] += ds
                    ds = ds.astype(BF)
                    qt = dot(k_ts[s][64 * p : 64 * p + 64, :KEYS], ds)
                    outs.append(jnp.where(first_head, qt[:, :LANES], qt[:, LANES:]))
                    dks.append(dot(ds, q2s[s][:, cols]))
                    dvs.append(dot(pt, d2s[s][:, cols]))
                scr[rows, lo : lo + SLAB] = (jnp.concatenate(outs, axis=0).T * scale)[:WIN]
                for g in range(2):
                    cols = slice(512 + lo + 128 * g, 512 + lo + 128 * g + 128)
                    scr[rows, cols] = (jnp.where(first_pair, dks[2 * g], dks[2 * g + 1]) * scale)[:WIN]
                    cols = slice(1024 + lo + 128 * g, 1024 + lo + 128 * g + 128)
                    scr[rows, cols] = jnp.where(first_pair, dvs[2 * g], dvs[2 * g + 1])[:WIN]
        d = scr[:ROWS, :].astype(BF)
        d_ref[...] = d
        prev[...] = d

    @pl.when(step < end)
    def _():
        windows()

    @pl.when(step == end)
    def _():
        for i in range(3):
            weights(i)
        for s, gq_ref in enumerate((gqa_ref, gqb_ref)):
            for i in range(3):
                cols = slice(512 * i + SLAB * s, 512 * i + SLAB * s + SLAB)
                gq_ref[256 * i : 256 * i + 256, :256] = acc[:256, cols].astype(BF)
                gq_ref[256 * i : 256 * i + 256, 256:] = acc[256:, cols].astype(BF)
        gqv_ref[...] = jnp.sum(accb[...], axis=1)


def input_grad_body(x_ref, gm_ref, d_ref, wa_ref, wb_ref, gain_ref, *refs):
    gin_ref, gs_ref, accs = refs[-3:]
    step = pl.program_id(0)

    @pl.when(step == 0)
    def _():
        accs[...] = jnp.zeros_like(accs)

    gn = jnp.zeros(gm_ref.shape, F32)
    for i in range(3):
        for s, w_ref in enumerate((wa_ref, wb_ref)):
            gn += dot_nt(d_ref[:, 512 * i + SLAB * s : 512 * i + SLAB * s + SLAB], w_ref[i])
    nh, r = norm_parts(x_ref[...].astype(F32))
    e = gn * gain_ref[0:1]
    gin = gm_ref[...] + r * (
        e - jnp.mean(e, axis=-1, keepdims=True) - nh * jnp.mean(e * nh, axis=-1, keepdims=True)
    )
    gin_ref[...] = gin.astype(BF)
    accs[0] += fold_rows(gn * nh)
    accs[1] += fold_rows(gn)

    @pl.when(step == pl.num_programs(0) - 1)
    def _():
        gs_ref[...] = jnp.sum(accs[...], axis=1)


def shaped(shape, dtype):
    return jax.ShapeDtypeStruct(shape, dtype)


def whole(shape):
    return pl.BlockSpec(shape, lambda i: (0,) * len(shape))


def by_rows(*shape, rows=ROWS):
    return pl.BlockSpec((rows,) + shape, lambda i: (i,) + (0,) * len(shape))


def dense_rows(*shape):
    return by_rows(*shape, rows=DENSE)


def by_windows(*shape):
    return pl.BlockSpec((GROUP,) + shape, lambda i: (i,) + (0,) * len(shape))


def params(mib):
    return pltpu.CompilerParams(vmem_limit_bytes=mib << 20, dimension_semantics=("arbitrary",))


def attn_fwd(x, pages, rel_index, ta, tb, wa, wb, qva, qvb, pa, pb, ob, gain, shift):
    rows = x.shape[0]
    windows = rows // WIN
    last = rows // ROWS - 1
    front = lambda *shape: pl.BlockSpec(shape, lambda i: (jnp.minimum(i, last),) + (0,) * (len(shape) - 1))
    back = lambda *shape: pl.BlockSpec(shape, lambda i: (jnp.maximum(i - 1, 0),) + (0,) * (len(shape) - 1))
    return pl.pallas_call(
        attn_fwd_body,
        name="attn_fwd",
        grid=(rows // ROWS + 1,),
        in_specs=[front(ROWS, 512), back(ROWS, 512), back(GROUP, 1, LANES)]
        + [whole(a.shape) for a in (rel_index, ta, tb, wa, wb, qva, qvb, pa, pb, ob, gain, shift)],
        out_specs=[
            front(ROWS, 512), front(GROUP, LANES, 1536), back(ROWS, 512), back(ROWS, 512),
            back(GROUP, 8, KEYS, SLAB), whole((16, SLAB)),
        ],
        out_shape=[
            shaped((rows, 512), BF),
            shaped((windows, LANES, 1536), BF),
            shaped((rows, 512), F32),
            shaped((rows, 512), BF),
            shaped((windows, 8, KEYS, SLAB), BF),
            shaped((16, SLAB), F32),
        ],
        scratch_shapes=[
            pltpu.VMEM((ROWS + 32, 1536), F32),
            pltpu.VMEM((GROUP, LANES, 1536), BF),
            pltpu.VMEM((GROUP, LANES, 1536), BF),
            pltpu.VMEM((GROUP, LANES, 512), F32),
            pltpu.VMEM((ROWS, 512), F32),
            pltpu.VMEM((8, KEYS, SLAB), F32),
            pltpu.VMEM((LANES, LANES), F32),
        ],
        compiler_params=params(58),
    )(x, x, pages, rel_index, ta, tb, wa, wb, qva, qvb, pa, pb, ob, gain, shift)


def cost(flops, moved):
    return pl.CostEstimate(flops=int(flops), bytes_accessed=int(moved), transcendentals=0)


def ffn(mixed, go, att, w1a, w1b, w2a, w2b, b1a, b1b, pa, pb, gain, shift):
    rows = mixed.shape[0]
    small = [w1a, w1b, w2a, w2b, b1a, b1b, pa, pb, gain, shift]
    return pl.pallas_call(
        ffn_body,
        name="feed_forward",
        grid=(rows // DENSE,),
        in_specs=[dense_rows(512)] * 3 + [whole(a.shape) for a in small],
        out_specs=[dense_rows(2048), dense_rows(512), dense_rows(512)]
        + [whole((2304, 512)), whole((2304, 512)), whole((1, 2048)), whole((4, 512))],
        out_shape=[
            shaped((rows, 2048), BF),
            shaped((rows, 512), F32),
            shaped((rows, 512), BF),
            shaped((2304, 512), BF),
            shaped((2304, 512), BF),
            shaped((1, 2048), F32),
            shaped((4, 512), F32),
        ],
        scratch_shapes=[
            pltpu.VMEM((512, 2048), F32),
            pltpu.VMEM((2048, 512), F32),
            pltpu.VMEM((512, 512), F32),
            pltpu.VMEM((8, 2048), F32),
            pltpu.VMEM((4, 8, 512), F32),
        ],
        compiler_params=params(50),
        cost_estimate=cost(50e9, 40e6),
    )(mixed, go, att, *small)


def third_rows(part):
    return lambda *shape: pl.BlockSpec((ROWS,) + shape, lambda i: (THIRD * part + i,) + (0,) * len(shape))


def out_rows(part, mixed, act, w2a, w2b, ob, *old):
    rows = mixed.shape[0]
    spec = third_rows(part)
    return pl.pallas_call(
        out_body,
        name="block_out",
        grid=(THIRD,),
        in_specs=[spec(512), spec(2048)] + [whole(a.shape) for a in (w2a, w2b, ob)] + [pl.BlockSpec(memory_space=pl.ANY)] * len(old),
        out_specs=spec(512),
        out_shape=shaped((rows, 512), BF),
        input_output_aliases={5: 0} if old else {},
        compiler_params=params(60),
        cost_estimate=cost(3e9, 7e6),
    )(mixed, act, w2a, w2b, ob, *old)


def attn_bwd(n, do, qkv, probs):
    rows = n.shape[0]
    last = rows // ROWS - 1
    front = lambda *shape: pl.BlockSpec(shape, lambda i: (jnp.minimum(i, last),) + (0,) * (len(shape) - 1))
    back = lambda *shape: pl.BlockSpec(shape, lambda i: (jnp.maximum(i - 1, 0),) + (0,) * (len(shape) - 1))
    return pl.pallas_call(
        attn_bwd_body,
        name="attn_bwd",
        grid=(rows // ROWS + 1,),
        in_specs=[back(ROWS, 512), front(ROWS, 512), front(GROUP, LANES, 1536), front(GROUP, 8, KEYS, SLAB)],
        out_specs=[
            front(ROWS, 1536), whole((8, KEYS, SLAB)), whole((768, 512)), whole((768, 512)), whole((2, 512)),
        ],
        out_shape=[
            shaped((rows, 1536), BF), shaped((8, KEYS, SLAB), F32), shaped((768, 512), BF), shaped((768, 512), BF),
            shaped((2, 512), F32),
        ],
        scratch_shapes=[
            pltpu.VMEM((ROWS + 32, 1536), F32),
            pltpu.VMEM((ROWS, 1536), BF),
            pltpu.VMEM((512, 1536), F32),
            pltpu.VMEM((2, 8, 512), F32),
        ],
        compiler_params=params(54),
        cost_estimate=cost(30e9, 60e6),
    )(n, do, qkv, probs)


def input_grad(part, x, gm, d, wa, wb, gain, *old):
    rows = x.shape[0]
    spec = third_rows(part)
    return pl.pallas_call(
        input_grad_body,
        name="input_grad",
        grid=(THIRD,),
        in_specs=[spec(512), spec(512), spec(1536)] + [whole(a.shape) for a in (wa, wb, gain)] + [pl.BlockSpec(memory_space=pl.ANY)] * len(old),
        out_specs=[spec(512), whole((2, 512))],
        out_shape=[shaped((rows, 512), BF), shaped((2, 512), F32)],
        scratch_shapes=[pltpu.VMEM((2, 8, 512), F32)],
        input_output_aliases={6: 0} if old else {},
        compiler_params=params(60),
        cost_estimate=cost(3e9, 7e6),
    )(x, gm, d, wa, wb, gain, *old)


def offset_onehot(index_row):
    slot = lax.broadcasted_iota(jnp.int32, (TAB, SLAB), 0).astype(F32)
    return jnp.where(slot == index_row, 1.0, 0.0).astype(BF)


def expand_table(rel_ref, ta_ref, tb_ref, bias_ref, idx_ref, scr):
    scr[...] = jnp.zeros_like(scr)
    scr[:WIN, :WIN] = rel_ref[...].astype(F32)
    scr[...] = scr[...].T
    lane = lax.broadcasted_iota(jnp.int32, (16, SLAB), 1)
    blank = jnp.zeros((16, SLAB - LANES), F32)

    def place(row, width, at):
        piece = jnp.concatenate([scr[row : row + 16, :], blank], axis=1)
        return pltpu.roll(jnp.where(lane < width, piece, 0.0), at, 1)

    idx = place(0, WIN, WIN - WS)
    for d in range(WS - 1):
        idx += place(WS * (WS - 1 - d), WS, WS * d)
    idx = jnp.where(lane < WIN + WIN - WS, idx, -1.0)
    idx_ref[...] = idx
    table = jnp.concatenate([ta_ref[...], tb_ref[...]], axis=0) * LOG2E
    high = table.astype(BF)
    rest = table - high.astype(F32)
    mid = rest.astype(BF)
    table = jnp.concatenate([high, mid, (rest - mid.astype(F32)).astype(BF)], axis=0)
    row = lax.broadcasted_iota(jnp.int32, (16, 48), 0)
    col = lax.broadcasted_iota(jnp.int32, (16, 48), 1)
    pick = jnp.where(col % 16 == 2 * (row % 8) + row // 8, 1.0, 0.0).astype(BF)
    for jx in range(WS):
        values = dot(pick, dot(table, offset_onehot(idx[jx : jx + 1])).astype(BF))
        for jy in range(WS):
            shift = WS * (WS - 1 - jy)
            moved = pltpu.roll(values, (SLAB - shift) % SLAB, 1) if shift else values
            bias_ref[:, WS * jy + jx, :LANES] = moved[:8, :LANES]
            bias_ref[:, WS * jy + jx, LANES:] = moved[8:, :LANES]
    for key in range(WIN, KEYS):
        bias_ref[:, key, :] = jnp.zeros((8, SLAB), F32)


def small_body(idx_ref, t_ref, gs2_ref, gs1a_ref, gs1b_ref, gs1c_ref, gb1_ref, gqv_ref, own_ref, other_ref, scr):
    total = jnp.zeros((32, TAB), F32)
    blank = jnp.zeros((8, SLAB - LANES), F32)
    for jx in range(WS):
        even = jnp.zeros((8, SLAB), F32)
        odd = jnp.zeros((8, SLAB), F32)
        for jy in range(WS):
            shift = WS * (WS - 1 - jy)
            even += pltpu.roll(jnp.concatenate([t_ref[:, WS * jy + jx, :LANES], blank], axis=1), shift, 1)
            odd += pltpu.roll(jnp.concatenate([t_ref[:, WS * jy + jx, LANES:], blank], axis=1), shift, 1)
        heads = jnp.concatenate([even, odd], axis=0)
        high = heads.astype(BF)
        rest = (heads - high.astype(F32)).astype(BF)
        total += dot_nt(jnp.concatenate([high, rest], axis=0), offset_onehot(idx_ref[jx : jx + 1]))
    total = total[:16] + total[16:]
    for s, out_ref in enumerate((own_ref, other_ref)):
        scr[...] = jnp.zeros_like(scr)
        scr[0:4] = gs2_ref[...]
        scr[4:6] = gs1a_ref[...] + gs1b_ref[...] + gs1c_ref[...]
        scr[6:7] = gb1_ref[:, 1024 * s : 1024 * s + 512]
        scr[7:8] = gb1_ref[:, 1024 * s + 512 : 1024 * s + 1024]
        scr[8:9, :SLAB] = gqv_ref[0:1, SLAB * s : SLAB * s + SLAB]
        scr[8:9, SLAB:] = gqv_ref[1:2, SLAB * s : SLAB * s + SLAB]
        scr[16:20, :TAB] = total[4 * s : 4 * s + 4]
        scr[20:24, :TAB] = total[8 + 4 * s : 12 + 4 * s]
        out_ref[...] = scr[...].astype(BF)


def small_sums(*args):
    return pl.pallas_call(
        small_body,
        name="small_sums",
        out_shape=[shaped((32, 512), BF), shaped((32, 512), BF)],
        scratch_shapes=[pltpu.VMEM((32, 512), F32)],
        compiler_params=pltpu.CompilerParams(vmem_limit_bytes=16 << 20),
        cost_estimate=cost(3e9, 1e6),
    )(*args)


def finish_body(q_ref, late_ref, gq_ref, gqv_ref, gob_ref, gg_ref, gh_ref, gb1_ref, gt_ref, scr):
    for i in range(3):
        q = q_ref[256 * i : 256 * i + 256, :].astype(F32)
        gq_ref[i, :256, :] = q[:, :256]
        gq_ref[i, 256:, :] = q[:, 256:]
    late = late_ref[...].astype(F32)
    gob_ref[...] = late[0:2]
    gg_ref[0:1] = late[4:5]
    gg_ref[1:2] = late[2:3]
    gh_ref[0:1] = late[5:6]
    gh_ref[1:2] = late[3:4]
    gb1_ref[:, :512] = late[6:7]
    gb1_ref[:, 512:] = late[7:8]
    gqv_ref[0:1] = late[8:9, :SLAB]
    gqv_ref[1:2] = late[8:9, SLAB:]
    for h in range(8):
        r = 16 + 4 * (h % 2) + h // 2
        scr[h : h + 1, :] = late[r : r + 1, :]
    gt_ref[...] = scr[:, :TAB]


def finish(q, late):
    return pl.pallas_call(
        finish_body,
        name="finish",
        out_shape=[
            shaped((3, 512, SLAB), F32), shaped((2, SLAB), F32), shaped((2, 512), F32), shaped((2, 512), F32),
            shaped((2, 512), F32), shaped((1, 1024), F32), shaped((8, TAB), F32),
        ],
        scratch_shapes=[pltpu.VMEM((8, 512), F32)],
        compiler_params=pltpu.CompilerParams(vmem_limit_bytes=16 << 20),
        cost_estimate=cost(1e9, 4e6),
    )(q, late)


SWAP = [(0, 1), (1, 0)]
SPLIT = True


def dp_bits(size):
    bits = []
    while 1 << len(bits) < size:
        bits.append(1 << len(bits))
    return bits


class Chain:
    def __init__(self, size, own, orders):
        self.orders, self.size, self.own, self.late = orders, size, own, None
        tp, dp = lax.axis_index("tp"), lax.axis_index("dp")
        self.upper = [jnp.where(tp == 0, dp & p, dp & q) != 0 for p, q in zip(*orders)]
        last = len(orders[0]) - 1
        self.steps = [("half", k) for k in range(last)] + [("full", last)]
        self.steps += [("join", k) for k in range(last - 1, -1, -1)]

    def begin(self):
        kind, k = self.steps[0]
        if kind == "half":
            half = self.own.shape[0] // 2
            up = self.upper[k].astype(jnp.int32)
            send = lax.dynamic_slice_in_dim(self.own, (1 - up) * half, half, 0)
            self.own = lax.dynamic_slice_in_dim(self.own, up * half, half, 0)
            return send
        if self.late is not None:
            return jnp.concatenate([self.own, self.late], axis=0)
        return self.own

    def move(self, send):
        k = self.steps[0][1]
        perm = [(2 * i + t, 2 * (i ^ self.orders[t][k]) + t) for i in range(self.size) for t in range(2)]
        return lax.ppermute(send, ("dp", "tp"), perm)

    def end(self, got):
        kind, k = self.steps.pop(0)
        if kind in ("full", "join") and self.late is not None:
            rows = self.own.shape[0]
            self.late = self.late + got[rows:]
            got = got[:rows]
        if kind == "join":
            up = self.upper[k]
            self.own = jnp.concatenate([jnp.where(up, got, self.own), jnp.where(up, self.own, got)], axis=0)
        else:
            self.own = self.own + got


class Pair:
    def __init__(self, own, other):
        self.own, self.other = own, other

    def begin(self):
        return self.other

    def move(self, send):
        return lax.ppermute(send, "tp", SWAP)

    def end(self, got):
        self.got = got

    def total(self):
        return self.own + self.got


tie = lax.optimization_barrier


def advance(chains, work=None, *inputs):
    sends, inputs = tie(([c.begin() for c in chains], inputs))
    gots = [c.move(v) for c, v in zip(chains, sends)]
    result = None if work is None else work(*inputs)
    gots, result = tie((gots, result))
    for c, got in zip(chains, gots):
        c.end(got)
    return result


class Flight:
    def __init__(self, chains):
        self.chains, self.sends, self.gots = chains, [c.begin() for c in chains], None

    def beside(self, chains, work, *inputs):
        sends = [c.begin() for c in chains]
        self.sends, sends, inputs = tie((self.sends, sends, inputs))
        if self.gots is None:
            self.gots = [c.move(v) for c, v in zip(self.chains, self.sends)]
        gots = [c.move(v) for c, v in zip(chains, sends)]
        gots, result = tie((gots, work(*inputs)))
        self.last = (gots, result)
        for c, got in zip(chains, gots):
            c.end(got)
        return result

    def land(self):
        self.gots, _ = tie((self.gots, self.last))
        for c, got in zip(self.chains, self.gots):
            c.end(got)


class Slices:
    def __init__(self, chain, count):
        self.chain, self.send, self.gots = chain, chain.begin(), []
        rows = self.send.shape[0]
        self.cuts = [rows * i // count // 8 * 8 for i in range(count)] + [rows]

    def begin(self):
        i = len(self.gots)
        return self.send[self.cuts[i] : self.cuts[i + 1]]

    def move(self, send):
        return self.chain.move(send)

    def end(self, got):
        self.gots.append(got)
        if len(self.gots) + 1 == len(self.cuts):
            self.chain.end(jnp.concatenate(self.gots, axis=0))


def forward(x, pages, rel_index, ta, tb, wa, wb, qva, qvb, pa, pb, w1a, w1b, b1a, b1b, w2a, w2b, ob, gain, shift, go):
    n, qkv, mixed, att, probs, idx = attn_fwd(x, pages, rel_index, ta, tb, wa, wb, qva, qvb, pa, pb, ob, gain, shift)
    act, gm, do, gfa, gfb, gb1, gs2 = ffn(mixed, go, att, w1a, w1b, w2a, w2b, b1a, b1b, pa, pb, gain, shift)
    return idx, mixed, n, qkv, probs, act, gm, do, (gfa, gfb), gb1, gs2


def local_block(x, pages, rel_index, wa, wb, qva, qvb, pa, pb, w1a, w1b, b1a, b1b, w2a, w2b, ob, gain, shift, ta, tb, go):
    idx, mixed, n, qkv, probs, act, gm, do, gf, gb1, gs2 = forward(
        x, pages, rel_index, ta.T, tb.T, wa, wb, qva, qvb, pa, pb, w1a, w1b, b1a, b1b, w2a, w2b, ob, gain, shift, go
    )
    d, t, gqa, gqb, gqv = attn_bwd(n, do, qkv, probs)
    gin, out, sums = (), (), []
    for i in range(3):
        *gin, part = input_grad(i, x, gm, d, wa, wb, gain, *gin)
        sums.append(part)
        out = [out_rows(i, mixed, act, w2a, w2b, ob, *out)]
    own, other = small_sums(idx, t, gs2, *sums, gb1, gqv)
    gin, out = gin[0], out[0]
    return out, gin, gf, finish(gqa, own), finish(gqb, other)


def per_device(
    dp_size, inputs, page_of, rel_index, w_qkv, qv_bias, w_proj, w_fc1, fc1_bias, w_fc2, out_biases, norm_gains,
    norm_biases, bias_table, out_grad,
):
    me = lax.axis_index("tp")
    windows = inputs.shape[0] // WIN
    swap = lambda v: lax.ppermute(v, "tp", SWAP)
    pages = lax.dynamic_slice_in_dim(page_of.reshape(2 * windows, WIN), me * windows, windows, 0)
    pages = jnp.pad(pages.astype(F32), ((0, 0), (0, LANES - WIN)), constant_values=-1.0)[:, None, :]
    table = bias_table.T
    w_qkv_b, qv_bias_b, w_proj_b, table_b = (swap(v) for v in (w_qkv, qv_bias, w_proj, table))
    later, w_qkv_b, qv_bias_b, w_proj_b, table_b, pages = tie(
        ((w_fc1, fc1_bias, w_fc2), w_qkv_b, qv_bias_b, w_proj_b, table_b, pages)
    )
    w_fc1_b, fc1_bias_b, w_fc2_b = (swap(v) for v in later)
    idx, mixed, n, qkv, probs, act, gm, do, gf, gb1, gs2 = forward(
        inputs, pages, rel_index, table, table_b, w_qkv, w_qkv_b, qv_bias, qv_bias_b, w_proj, w_proj_b, w_fc1, w_fc1_b,
        fc1_bias[None], fc1_bias_b[None], w_fc2, w_fc2_b, out_biases, norm_gains, norm_biases, out_grad,
    )
    bits = dp_bits(dp_size)
    turned = bits[1:] + bits[:1]
    mid = len(bits) // 2
    deep = bits[mid:-1] + bits[:mid] + bits[-1:]
    grad = lambda i, *old: (functools.partial(input_grad, i), inputs, gm, d, w_qkv, w_qkv_b, norm_gains) + old
    rows_out = lambda i, *old: (functools.partial(out_rows, i), mixed, act, w_fc2, w_fc2_b, out_biases) + old

    pair = Pair(*gf)
    out = advance([pair], *rows_out(0))
    if SPLIT:
        cut = 1664
        f = [Chain(dp_size, pair.total()[:cut], (bits, turned)), Chain(dp_size, pair.total()[cut:], (deep, deep))]
    else:
        f = [Chain(dp_size, pair.total(), (bits, turned))]
    d, t, gqa, gqb, gqv = advance(f, attn_bwd, n, do, qkv, probs)
    pair = Pair(gqa, gqb)
    gin, gs1a = advance(f + [pair], *grad(0))
    q = Chain(dp_size, pair.total(), (bits, turned))
    gin, gs1b = advance(f + [q], *grad(1, gin))
    gin, gs1c = advance(f + [q], *grad(2, gin))
    flight = Flight(f)
    low = Pair(*flight.beside([], small_sums, idx, t, gs2, gs1a, gs1b, gs1c, gb1, gqv))
    out = flight.beside([q, low], *rows_out(1, out))
    flight.land()
    q.late = low.total()
    while len(f[0].steps) > 1:
        advance(f + [q])
    parts = [Slices(c, max(1, len(q.steps) - 1)) for c in f]
    out = advance(parts + [q], *rows_out(2, out))
    while f[0].steps:
        advance(parts + [q])
    g_f = jnp.concatenate([c.own for c in f])
    g_fc2 = g_f[:1024].astype(F32)
    g_fc1 = jnp.concatenate([g_f[1024:1536], g_f[1536:2048]], axis=1).astype(F32)
    g_proj = g_f[2048:].astype(F32)
    while q.steps:
        advance([q])
    g_qkv, g_qv, g_ob, g_gains, g_shifts, g_fc1_bias, g_table = finish(q.own, q.late)
    return out, gin, g_qkv, g_qv, g_proj, g_fc1, g_fc1_bias.reshape(-1), g_fc2, g_ob, g_gains, g_shifts, g_table.T


def solution(mesh):
    rows = P(("dp", "tp"), None)
    placed = (
        rows, P("dp"), P(), P(None, None, "tp"), P(None, "tp"), P("tp", None), P(None, "tp"), P("tp"),
        P("tp", None), P(), P(), P(), P(None, "tp"), rows,
    )
    results = (
        rows, rows, P(None, None, "tp"), P(None, "tp"), P("tp", None), P(None, "tp"), P("tp"), P("tp", None),
        P(), P(), P(), P(None, "tp"),
    )
    return jax.shard_map(
        functools.partial(per_device, mesh.shape["dp"]), mesh=mesh, in_specs=placed, out_specs=results, check_vma=False
    )
```

```python
import functools

import jax
import jax.numpy as jnp
from jax import lax
from jax.experimental import pallas as pl
from jax.experimental.pallas import tpu as pltpu
from jax.sharding import PartitionSpec as P

HEAD = 32
EPS = 1e-05
WIN = 100
WS = 10
TAB = 361
KEYS = 104
LANES = 128
SLAB = 256
GROUP = 4
ROWS = GROUP * WIN
DENSE = 480
THIRD = 2
CHUNK = 256
LOG2E = 1.4426950408889634
NEG = -1e30
BF = jnp.bfloat16
F32 = jnp.float32
NT = (((1,), (1,)), ((), ()))
TN = (((0,), (0,)), ((), ()))


def dot(a, b):
    return jnp.dot(a, b, preferred_element_type=F32)


def dot_nt(a, b):
    return lax.dot_general(a, b, NT, preferred_element_type=F32)


def dot_tn(a, b):
    return lax.dot_general(a, b, TN, preferred_element_type=F32)


def norm_parts(v):
    mean = jnp.mean(v, axis=-1, keepdims=True)
    centered = v - mean
    var = jnp.mean(centered * centered, axis=-1, keepdims=True)
    r = lax.rsqrt(var + EPS)
    return centered * r, r


def fold_rows(v):
    rows, cols = v.shape
    return jnp.sum(v.reshape(rows // 8, 8, cols), axis=0)


def lane_mask(rows, test):
    lane = lax.broadcasted_iota(jnp.int32, (rows, SLAB), 1)
    return jnp.where(test(lane), 1.0, 0.0).astype(BF)


def attn_fwd_body(
    x_ref, xb_ref, page_ref, rel_ref, ta_ref, tb_ref, wa_ref, wb_ref, qva_ref, qvb_ref, pa_ref, pb_ref, ob_ref, gain_ref,
    shift_ref,
    n_ref, qkv_ref, mixed_ref, att_ref, p_ref, idx_ref,
    scr, cur, nxt, att_scr, att_rows, bias_ref, turn,
):
    scale = (HEAD ** -0.5) * LOG2E

    @pl.when(pl.program_id(0) == 0)
    def _():
        scr[ROWS:, :] = jnp.zeros((scr.shape[0] - ROWS, scr.shape[1]), F32)

    def prepare():
        n, _ = norm_parts(x_ref[...].astype(F32))
        n = (n * gain_ref[0:1] + shift_ref[0:1]).astype(BF)
        n_ref[...] = n
        return n

    def project(n, i):
        for s, (w_ref, b_ref) in enumerate(((wa_ref, qva_ref), (wb_ref, qvb_ref))):
            cols = slice(512 * i + s * SLAB, 512 * i + s * SLAB + SLAB)
            out = dot(n, w_ref[i])
            scr[:ROWS, cols] = out if i == 1 else out + b_ref[i // 2 : i // 2 + 1]
        for w in range(GROUP):
            v = scr[w * WIN : w * WIN + LANES, 512 * i : 512 * i + 512].astype(BF)
            nxt[w, :, 512 * i : 512 * i + 512] = v
            qkv_ref[w, :, 512 * i : 512 * i + 512] = v

    def attend(beside):
        even = lane_mask(LANES, lambda c: (c // HEAD) % 2 == 0)
        odd = lane_mask(LANES, lambda c: (c // HEAD) % 2 == 1)
        low = lane_mask(KEYS, lambda c: c % 128 < 64)[:, :128]
        high = lane_mask(KEYS, lambda c: c % 128 >= 64)[:, :128]
        query_lane = lax.broadcasted_iota(jnp.int32, (1, SLAB), 1) % LANES
        valid = jnp.where(query_lane < WIN, 1.0, 0.0)
        first_head = lax.broadcasted_iota(jnp.int32, (2 * HEAD, LANES), 0) < HEAD
        for w in range(GROUP):
            pages = jnp.broadcast_to(page_ref[w], (LANES, LANES))
            mask = jnp.where(pages == pages.T, 0.0, NEG)[:KEYS]
            mask = jnp.concatenate([mask, mask], axis=1)
            scores, v_ts = [], []
            for s in range(2):
                lo = s * SLAB
                q = cur[w, :, lo : lo + SLAB]
                k = cur[w, :KEYS, 512 + lo : 512 + lo + SLAB]
                v_ts.append(cur[w, :, 1024 + lo : 1024 + lo + SLAB].T)
                q2 = jnp.concatenate([q * even, q * odd], axis=0)
                for p in range(4):
                    cols = slice(128 * (p // 2), 128 * (p // 2) + 128)
                    scores.append(dot_nt(k[:, cols] * (low if p % 2 == 0 else high), q2[:, cols]))
            beside(w)
            for s in range(2):
                outs = []
                for p in range(4):
                    st = scores[4 * s + p] * scale + bias_ref[4 * s + p] + mask
                    e = jnp.exp2(st - jnp.max(st, axis=0, keepdims=True))
                    pt = (e * (valid / jnp.sum(e, axis=0, keepdims=True))).astype(BF)
                    p_ref[w, 4 * s + p] = pt
                    ot = dot(v_ts[s][64 * p : 64 * p + 64, :KEYS], pt)
                    outs.append(jnp.where(first_head, ot[:, :LANES], ot[:, LANES:]))
                att_scr[w, :, s * SLAB : s * SLAB + SLAB] = jnp.concatenate(outs, axis=0).T
        for w in range(GROUP):
            att_rows[w * WIN : w * WIN + WIN, :] = att_scr[w, :WIN, :]
        att = att_rows[...].astype(BF)
        att_ref[...] = att
        mixed_ref[...] = (
            xb_ref[...].astype(F32) + ob_ref[0:1] + dot(att[:, :SLAB], pa_ref[...]) + dot(att[:, SLAB:], pb_ref[...])
        )

    step, end = pl.program_id(0), pl.num_programs(0) - 1

    @pl.when(step == 0)
    def _():
        n = prepare()
        for i in range(3):
            project(n, i)
        cur[...] = nxt[...]
        expand_table(rel_ref, ta_ref, tb_ref, bias_ref, idx_ref, turn)

    @pl.when((step > 0) & (step < end))
    def _():
        n = prepare()
        attend(lambda w: project(n, w) if w < 3 else None)
        cur[...] = nxt[...]

    @pl.when(step == end)
    def _():
        attend(lambda w: None)


def gelu_parts(h):
    phi = 0.5 + 0.5 * lax.erf(h * 0.7071067811865476)
    return phi, jnp.exp2(h * h * (-0.5 * LOG2E)) * 0.3989422804014327


def ffn_body(
    mixed_ref, go_ref, att_ref, w1a_ref, w1b_ref, w2a_ref, w2b_ref, b1a_ref, b1b_ref, pa_ref, pb_ref, gain_ref, shift_ref,
    act_ref, gm_ref, do_ref, gfa_ref, gfb_ref, gb1_ref, gs_ref,
    acc1, acc2, accp, accb, accs,
):
    step = pl.program_id(0)

    @pl.when(step == 0)
    def _():
        acc1[...] = jnp.zeros_like(acc1)
        acc2[...] = jnp.zeros_like(acc2)
        accp[...] = jnp.zeros_like(accp)
        accb[...] = jnp.zeros_like(accb)
        accs[...] = jnp.zeros_like(accs)

    mixed = mixed_ref[...]
    nh, r = norm_parts(mixed)
    n2 = (nh * gain_ref[1:2] + shift_ref[1:2]).astype(BF)
    go = go_ref[...]
    gn = jnp.zeros_like(mixed)
    per_half = 1024 // CHUNK

    def weights(c):
        col = slice(CHUNK * (c % per_half), CHUNK * (c % per_half) + CHUNK)
        return ((w1a_ref, w2a_ref, b1a_ref) if c < per_half else (w1b_ref, w2b_ref, b1b_ref)) + (col,)

    def front(c):
        w1_ref, w2_ref, b1_ref, col = weights(c)
        return dot(n2, w1_ref[:, col]) + b1_ref[0:1, col], dot_nt(go, w2_ref[col, :])

    ready = front(0)
    for c in range(2 * per_half):
        h, ga = ready
        if c + 1 < 2 * per_half:
            ready = front(c + 1)
        w1_ref, _, _, col = weights(c)
        full = slice(CHUNK * c, CHUNK * c + CHUNK)
        phi, density = gelu_parts(h)
        act = (h * phi).astype(BF)
        act_ref[:, full] = act
        ghf = ga * (phi + h * density)
        accb[:, full] += fold_rows(ghf)
        gh = ghf.astype(BF)
        gn += dot_nt(gh, w1_ref[:, col])
        acc2[full, :] += dot_tn(act, go)
        acc1[:, full] += dot_tn(n2, gh)
    gof = go.astype(F32)
    e = gn * gain_ref[1:2]
    gm = gof + r * (
        e - jnp.mean(e, axis=-1, keepdims=True) - nh * jnp.mean(e * nh, axis=-1, keepdims=True)
    )
    gm_ref[...] = gm
    gml = gm.astype(BF)
    accp[...] += dot_tn(att_ref[...], gml)
    do_ref[:, :SLAB] = dot_nt(gml, pa_ref[...]).astype(BF)
    do_ref[:, SLAB:] = dot_nt(gml, pb_ref[...]).astype(BF)
    accs[0] += fold_rows(gm)
    accs[1] += fold_rows(gof)
    accs[2] += fold_rows(gn * nh)
    accs[3] += fold_rows(gn)

    @pl.when(step == pl.num_programs(0) - 1)
    def _():
        for s, gf_ref in enumerate((gfa_ref, gfb_ref)):
            gf_ref[:1024] = acc2[1024 * s : 1024 * s + 1024, :].astype(BF)
            gf_ref[1024:1536] = acc1[:, 1024 * s : 1024 * s + 512].astype(BF)
            gf_ref[1536:2048] = acc1[:, 1024 * s + 512 : 1024 * s + 1024].astype(BF)
            gf_ref[2048:2304] = accp[SLAB * s : SLAB * s + SLAB, :].astype(BF)
        gb1_ref[...] = jnp.sum(accb[...], axis=0, keepdims=True)
        gs_ref[...] = jnp.sum(accs[...], axis=1)


def out_body(mixed_ref, act_ref, w2a_ref, w2b_ref, ob_ref, *refs):
    out_ref = refs[-1]
    out = mixed_ref[...] + ob_ref[1:2] + dot(act_ref[:, :1024], w2a_ref[...]) + dot(act_ref[:, 1024:], w2b_ref[...])
    out_ref[...] = out.astype(BF)


def attn_bwd_body(
    n_ref, do_ref, qkv_ref, p_ref, d_ref, t_ref, gqa_ref, gqb_ref, gqv_ref, scr, prev, acc, accb
):
    scale = HEAD ** -0.5
    step, end = pl.program_id(0), pl.num_programs(0) - 1

    @pl.when(step == 0)
    def _():
        scr[ROWS:, :512] = jnp.zeros((scr.shape[0] - ROWS, 512), F32)
        t_ref[...] = jnp.zeros_like(t_ref)
        prev[...] = jnp.zeros_like(prev)
        acc[...] = jnp.zeros_like(acc)
        accb[...] = jnp.zeros_like(accb)

    def weights(i):
        cols = slice(512 * i, 512 * i + 512)
        d = prev[:, cols]
        acc[:, cols] += dot_tn(n_ref[...], d)
        if i != 1:
            accb[i // 2] += fold_rows(d.astype(F32))

    def windows():
        scr[:ROWS, :512] = do_ref[...].astype(F32)
        row = lax.broadcasted_iota(jnp.int32, (LANES, 512), 0)
        dos = [jnp.where(row < WIN, scr[w * WIN : w * WIN + LANES, :512], 0.0).astype(BF) for w in range(GROUP)]
        even = lane_mask(LANES, lambda c: (c // HEAD) % 2 == 0)
        odd = lane_mask(LANES, lambda c: (c // HEAD) % 2 == 1)
        low = lane_mask(KEYS, lambda c: c % 128 < 64)[:, :128]
        high = lane_mask(KEYS, lambda c: c % 128 >= 64)[:, :128]
        first_head = lax.broadcasted_iota(jnp.int32, (2 * HEAD, LANES), 0) < HEAD
        first_pair = lax.broadcasted_iota(jnp.int32, (KEYS, 128), 1) < 64
        for w in range(GROUP):
            rows = slice(w * WIN, w * WIN + WIN)
            q2s, d2s, k_ts, dps = [], [], [], []
            for s in range(2):
                lo = s * SLAB
                q = qkv_ref[w, :, lo : lo + SLAB]
                v = qkv_ref[w, :KEYS, 1024 + lo : 1024 + lo + SLAB]
                do = dos[w][:, lo : lo + SLAB]
                q2s.append(jnp.concatenate([q * even, q * odd], axis=0))
                d2s.append(jnp.concatenate([do * even, do * odd], axis=0))
                k_ts.append(qkv_ref[w, :, 512 + lo : 512 + lo + SLAB].T)
                for p in range(4):
                    cols = slice(128 * (p // 2), 128 * (p // 2) + 128)
                    dps.append(dot_nt(v[:, cols] * (low if p % 2 == 0 else high), d2s[s][:, cols]))
            if w < 3:
                weights(w)
            for s in range(2):
                lo = s * SLAB
                outs, dks, dvs = [], [], []
                for p in range(4):
                    cols = slice(128 * (p // 2), 128 * (p // 2) + 128)
                    pt = p_ref[w, 4 * s + p]
                    ptf = pt.astype(F32)
                    dp = dps[4 * s + p]
                    ds = ptf * (dp - jnp.sum(dp * ptf, axis=0, keepdims=True))
                    t_ref[4 * s + p] += ds
                    ds = ds.astype(BF)
                    qt = dot(k_ts[s][64 * p : 64 * p + 64, :KEYS], ds)
                    outs.append(jnp.where(first_head, qt[:, :LANES], qt[:, LANES:]))
                    dks.append(dot(ds, q2s[s][:, cols]))
                    dvs.append(dot(pt, d2s[s][:, cols]))
                scr[rows, lo : lo + SLAB] = (jnp.concatenate(outs, axis=0).T * scale)[:WIN]
                for g in range(2):
                    cols = slice(512 + lo + 128 * g, 512 + lo + 128 * g + 128)
                    scr[rows, cols] = (jnp.where(first_pair, dks[2 * g], dks[2 * g + 1]) * scale)[:WIN]
                    cols = slice(1024 + lo + 128 * g, 1024 + lo + 128 * g + 128)
                    scr[rows, cols] = jnp.where(first_pair, dvs[2 * g], dvs[2 * g + 1])[:WIN]
        d = scr[:ROWS, :].astype(BF)
        d_ref[...] = d
        prev[...] = d

    @pl.when(step < end)
    def _():
        windows()

    @pl.when(step == end)
    def _():
        for i in range(3):
            weights(i)
        for s, gq_ref in enumerate((gqa_ref, gqb_ref)):
            for i in range(3):
                cols = slice(512 * i + SLAB * s, 512 * i + SLAB * s + SLAB)
                gq_ref[256 * i : 256 * i + 256, :256] = acc[:256, cols].astype(BF)
                gq_ref[256 * i : 256 * i + 256, 256:] = acc[256:, cols].astype(BF)
        gqv_ref[...] = jnp.sum(accb[...], axis=1)


def input_grad_body(x_ref, gm_ref, d_ref, wa_ref, wb_ref, gain_ref, *refs):
    gin_ref, gs_ref, accs = refs[-3:]
    step = pl.program_id(0)

    @pl.when(step == 0)
    def _():
        accs[...] = jnp.zeros_like(accs)

    gn = jnp.zeros(gm_ref.shape, F32)
    for i in range(3):
        for s, w_ref in enumerate((wa_ref, wb_ref)):
            gn += dot_nt(d_ref[:, 512 * i + SLAB * s : 512 * i + SLAB * s + SLAB], w_ref[i])
    nh, r = norm_parts(x_ref[...].astype(F32))
    e = gn * gain_ref[0:1]
    gin = gm_ref[...] + r * (
        e - jnp.mean(e, axis=-1, keepdims=True) - nh * jnp.mean(e * nh, axis=-1, keepdims=True)
    )
    gin_ref[...] = gin.astype(BF)
    accs[0] += fold_rows(gn * nh)
    accs[1] += fold_rows(gn)

    @pl.when(step == pl.num_programs(0) - 1)
    def _():
        gs_ref[...] = jnp.sum(accs[...], axis=1)


def shaped(shape, dtype):
    return jax.ShapeDtypeStruct(shape, dtype)


def whole(shape):
    return pl.BlockSpec(shape, lambda i: (0,) * len(shape))


def by_rows(*shape, rows=ROWS):
    return pl.BlockSpec((rows,) + shape, lambda i: (i,) + (0,) * len(shape))


def dense_rows(*shape):
    return by_rows(*shape, rows=DENSE)


def by_windows(*shape):
    return pl.BlockSpec((GROUP,) + shape, lambda i: (i,) + (0,) * len(shape))


def params(mib):
    return pltpu.CompilerParams(vmem_limit_bytes=mib << 20, dimension_semantics=("arbitrary",))


def attn_fwd(x, pages, rel_index, ta, tb, wa, wb, qva, qvb, pa, pb, ob, gain, shift):
    rows = x.shape[0]
    windows = rows // WIN
    last = rows // ROWS - 1
    front = lambda *shape: pl.BlockSpec(shape, lambda i: (jnp.minimum(i, last),) + (0,) * (len(shape) - 1))
    back = lambda *shape: pl.BlockSpec(shape, lambda i: (jnp.maximum(i - 1, 0),) + (0,) * (len(shape) - 1))
    return pl.pallas_call(
        attn_fwd_body,
        name="attn_fwd",
        grid=(rows // ROWS + 1,),
        in_specs=[front(ROWS, 512), back(ROWS, 512), back(GROUP, 1, LANES)]
        + [whole(a.shape) for a in (rel_index, ta, tb, wa, wb, qva, qvb, pa, pb, ob, gain, shift)],
        out_specs=[
            front(ROWS, 512), front(GROUP, LANES, 1536), back(ROWS, 512), back(ROWS, 512),
            back(GROUP, 8, KEYS, SLAB), whole((16, SLAB)),
        ],
        out_shape=[
            shaped((rows, 512), BF),
            shaped((windows, LANES, 1536), BF),
            shaped((rows, 512), F32),
            shaped((rows, 512), BF),
            shaped((windows, 8, KEYS, SLAB), BF),
            shaped((16, SLAB), F32),
        ],
        scratch_shapes=[
            pltpu.VMEM((ROWS + 32, 1536), F32),
            pltpu.VMEM((GROUP, LANES, 1536), BF),
            pltpu.VMEM((GROUP, LANES, 1536), BF),
            pltpu.VMEM((GROUP, LANES, 512), F32),
            pltpu.VMEM((ROWS, 512), F32),
            pltpu.VMEM((8, KEYS, SLAB), F32),
            pltpu.VMEM((LANES, LANES), F32),
        ],
        compiler_params=params(58),
    )(x, x, pages, rel_index, ta, tb, wa, wb, qva, qvb, pa, pb, ob, gain, shift)


def cost(flops, moved):
    return pl.CostEstimate(flops=int(flops), bytes_accessed=int(moved), transcendentals=0)


def ffn(mixed, go, att, w1a, w1b, w2a, w2b, b1a, b1b, pa, pb, gain, shift):
    rows = mixed.shape[0]
    small = [w1a, w1b, w2a, w2b, b1a, b1b, pa, pb, gain, shift]
    return pl.pallas_call(
        ffn_body,
        name="feed_forward",
        grid=(rows // DENSE,),
        in_specs=[dense_rows(512)] * 3 + [whole(a.shape) for a in small],
        out_specs=[dense_rows(2048), dense_rows(512), dense_rows(512)]
        + [whole((2304, 512)), whole((2304, 512)), whole((1, 2048)), whole((4, 512))],
        out_shape=[
            shaped((rows, 2048), BF),
            shaped((rows, 512), F32),
            shaped((rows, 512), BF),
            shaped((2304, 512), BF),
            shaped((2304, 512), BF),
            shaped((1, 2048), F32),
            shaped((4, 512), F32),
        ],
        scratch_shapes=[
            pltpu.VMEM((512, 2048), F32),
            pltpu.VMEM((2048, 512), F32),
            pltpu.VMEM((512, 512), F32),
            pltpu.VMEM((8, 2048), F32),
            pltpu.VMEM((4, 8, 512), F32),
        ],
        compiler_params=params(48),
        cost_estimate=cost(50e9, 40e6),
    )(mixed, go, att, *small)


def third_rows(part):
    return lambda *shape: pl.BlockSpec((ROWS,) + shape, lambda i: (THIRD * part + i,) + (0,) * len(shape))


def out_rows(part, mixed, act, w2a, w2b, ob, *old):
    rows = mixed.shape[0]
    spec = third_rows(part)
    return pl.pallas_call(
        out_body,
        name="block_out",
        grid=(THIRD,),
        in_specs=[spec(512), spec(2048)] + [whole(a.shape) for a in (w2a, w2b, ob)] + [pl.BlockSpec(memory_space=pl.ANY)] * len(old),
        out_specs=spec(512),
        out_shape=shaped((rows, 512), BF),
        input_output_aliases={5: 0} if old else {},
        compiler_params=params(60),
        cost_estimate=cost(3e9, 7e6),
    )(mixed, act, w2a, w2b, ob, *old)


def attn_bwd(n, do, qkv, probs):
    rows = n.shape[0]
    last = rows // ROWS - 1
    front = lambda *shape: pl.BlockSpec(shape, lambda i: (jnp.minimum(i, last),) + (0,) * (len(shape) - 1))
    back = lambda *shape: pl.BlockSpec(shape, lambda i: (jnp.maximum(i - 1, 0),) + (0,) * (len(shape) - 1))
    return pl.pallas_call(
        attn_bwd_body,
        name="attn_bwd",
        grid=(rows // ROWS + 1,),
        in_specs=[back(ROWS, 512), front(ROWS, 512), front(GROUP, LANES, 1536), front(GROUP, 8, KEYS, SLAB)],
        out_specs=[
            front(ROWS, 1536), whole((8, KEYS, SLAB)), whole((768, 512)), whole((768, 512)), whole((2, 512)),
        ],
        out_shape=[
            shaped((rows, 1536), BF), shaped((8, KEYS, SLAB), F32), shaped((768, 512), BF), shaped((768, 512), BF),
            shaped((2, 512), F32),
        ],
        scratch_shapes=[
            pltpu.VMEM((ROWS + 32, 1536), F32),
            pltpu.VMEM((ROWS, 1536), BF),
            pltpu.VMEM((512, 1536), F32),
            pltpu.VMEM((2, 8, 512), F32),
        ],
        compiler_params=params(54),
        cost_estimate=cost(30e9, 60e6),
    )(n, do, qkv, probs)


def input_grad(part, x, gm, d, wa, wb, gain, *old):
    rows = x.shape[0]
    spec = third_rows(part)
    return pl.pallas_call(
        input_grad_body,
        name="input_grad",
        grid=(THIRD,),
        in_specs=[spec(512), spec(512), spec(1536)] + [whole(a.shape) for a in (wa, wb, gain)] + [pl.BlockSpec(memory_space=pl.ANY)] * len(old),
        out_specs=[spec(512), whole((2, 512))],
        out_shape=[shaped((rows, 512), BF), shaped((2, 512), F32)],
        scratch_shapes=[pltpu.VMEM((2, 8, 512), F32)],
        input_output_aliases={6: 0} if old else {},
        compiler_params=params(60),
        cost_estimate=cost(3e9, 7e6),
    )(x, gm, d, wa, wb, gain, *old)


def offset_onehot(index_row):
    slot = lax.broadcasted_iota(jnp.int32, (TAB, SLAB), 0).astype(F32)
    return jnp.where(slot == index_row, 1.0, 0.0).astype(BF)


def expand_table(rel_ref, ta_ref, tb_ref, bias_ref, idx_ref, scr):
    scr[...] = jnp.zeros_like(scr)
    scr[:WIN, :WIN] = rel_ref[...].astype(F32)
    scr[...] = scr[...].T
    lane = lax.broadcasted_iota(jnp.int32, (16, SLAB), 1)
    blank = jnp.zeros((16, SLAB - LANES), F32)

    def place(row, width, at):
        piece = jnp.concatenate([scr[row : row + 16, :], blank], axis=1)
        return pltpu.roll(jnp.where(lane < width, piece, 0.0), at, 1)

    idx = place(0, WIN, WIN - WS)
    for d in range(WS - 1):
        idx += place(WS * (WS - 1 - d), WS, WS * d)
    idx = jnp.where(lane < WIN + WIN - WS, idx, -1.0)
    idx_ref[...] = idx
    table = jnp.concatenate([ta_ref[...], tb_ref[...]], axis=0) * LOG2E
    high = table.astype(BF)
    rest = table - high.astype(F32)
    mid = rest.astype(BF)
    table = jnp.concatenate([high, mid, (rest - mid.astype(F32)).astype(BF)], axis=0)
    row = lax.broadcasted_iota(jnp.int32, (16, 48), 0)
    col = lax.broadcasted_iota(jnp.int32, (16, 48), 1)
    pick = jnp.where(col % 16 == 2 * (row % 8) + row // 8, 1.0, 0.0).astype(BF)
    for jx in range(WS):
        values = dot(pick, dot(table, offset_onehot(idx[jx : jx + 1])).astype(BF))
        for jy in range(WS):
            shift = WS * (WS - 1 - jy)
            moved = pltpu.roll(values, (SLAB - shift) % SLAB, 1) if shift else values
            bias_ref[:, WS * jy + jx, :LANES] = moved[:8, :LANES]
            bias_ref[:, WS * jy + jx, LANES:] = moved[8:, :LANES]
    for key in range(WIN, KEYS):
        bias_ref[:, key, :] = jnp.zeros((8, SLAB), F32)


def small_body(idx_ref, t_ref, gs2_ref, gs1a_ref, gs1b_ref, gs1c_ref, gb1_ref, gqv_ref, own_ref, other_ref, scr):
    total = jnp.zeros((32, TAB), F32)
    blank = jnp.zeros((8, SLAB - LANES), F32)
    for jx in range(WS):
        even = jnp.zeros((8, SLAB), F32)
        odd = jnp.zeros((8, SLAB), F32)
        for jy in range(WS):
            shift = WS * (WS - 1 - jy)
            even += pltpu.roll(jnp.concatenate([t_ref[:, WS * jy + jx, :LANES], blank], axis=1), shift, 1)
            odd += pltpu.roll(jnp.concatenate([t_ref[:, WS * jy + jx, LANES:], blank], axis=1), shift, 1)
        heads = jnp.concatenate([even, odd], axis=0)
        high = heads.astype(BF)
        rest = (heads - high.astype(F32)).astype(BF)
        total += dot_nt(jnp.concatenate([high, rest], axis=0), offset_onehot(idx_ref[jx : jx + 1]))
    total = total[:16] + total[16:]
    for s, out_ref in enumerate((own_ref, other_ref)):
        scr[...] = jnp.zeros_like(scr)
        scr[0:4] = gs2_ref[...]
        scr[4:6] = gs1a_ref[...] + gs1b_ref[...] + gs1c_ref[...]
        scr[6:7] = gb1_ref[:, 1024 * s : 1024 * s + 512]
        scr[7:8] = gb1_ref[:, 1024 * s + 512 : 1024 * s + 1024]
        scr[8:9, :SLAB] = gqv_ref[0:1, SLAB * s : SLAB * s + SLAB]
        scr[8:9, SLAB:] = gqv_ref[1:2, SLAB * s : SLAB * s + SLAB]
        scr[16:20, :TAB] = total[4 * s : 4 * s + 4]
        scr[20:24, :TAB] = total[8 + 4 * s : 12 + 4 * s]
        out_ref[...] = scr[...].astype(BF)


def small_sums(*args):
    return pl.pallas_call(
        small_body,
        name="small_sums",
        out_shape=[shaped((32, 512), BF), shaped((32, 512), BF)],
        scratch_shapes=[pltpu.VMEM((32, 512), F32)],
        compiler_params=pltpu.CompilerParams(vmem_limit_bytes=16 << 20),
        cost_estimate=cost(3e9, 1e6),
    )(*args)


def finish_body(q_ref, late_ref, gq_ref, gqv_ref, gob_ref, gg_ref, gh_ref, gb1_ref, gt_ref, scr):
    for i in range(3):
        q = q_ref[256 * i : 256 * i + 256, :].astype(F32)
        gq_ref[i, :256, :] = q[:, :256]
        gq_ref[i, 256:, :] = q[:, 256:]
    late = late_ref[...].astype(F32)
    gob_ref[...] = late[0:2]
    gg_ref[0:1] = late[4:5]
    gg_ref[1:2] = late[2:3]
    gh_ref[0:1] = late[5:6]
    gh_ref[1:2] = late[3:4]
    gb1_ref[:, :512] = late[6:7]
    gb1_ref[:, 512:] = late[7:8]
    gqv_ref[0:1] = late[8:9, :SLAB]
    gqv_ref[1:2] = late[8:9, SLAB:]
    for h in range(8):
        r = 16 + 4 * (h % 2) + h // 2
        scr[h : h + 1, :] = late[r : r + 1, :]
    gt_ref[...] = scr[:, :TAB]


def finish(q, late):
    return pl.pallas_call(
        finish_body,
        name="finish",
        out_shape=[
            shaped((3, 512, SLAB), F32), shaped((2, SLAB), F32), shaped((2, 512), F32), shaped((2, 512), F32),
            shaped((2, 512), F32), shaped((1, 1024), F32), shaped((8, TAB), F32),
        ],
        scratch_shapes=[pltpu.VMEM((8, 512), F32)],
        compiler_params=pltpu.CompilerParams(vmem_limit_bytes=16 << 20),
        cost_estimate=cost(1e9, 4e6),
    )(q, late)


SWAP = [(0, 1), (1, 0)]
SPLIT = True


def dp_bits(size):
    bits = []
    while 1 << len(bits) < size:
        bits.append(1 << len(bits))
    return bits


class Chain:
    def __init__(self, size, own, orders):
        self.orders, self.size, self.own, self.late = orders, size, own, None
        tp, dp = lax.axis_index("tp"), lax.axis_index("dp")
        self.upper = [jnp.where(tp == 0, dp & p, dp & q) != 0 for p, q in zip(*orders)]
        last = len(orders[0]) - 1
        self.steps = [("half", k) for k in range(last)] + [("full", last)]
        self.steps += [("join", k) for k in range(last - 1, -1, -1)]

    def begin(self):
        kind, k = self.steps[0]
        if kind == "half":
            half = self.own.shape[0] // 2
            up = self.upper[k].astype(jnp.int32)
            send = lax.dynamic_slice_in_dim(self.own, (1 - up) * half, half, 0)
            self.own = lax.dynamic_slice_in_dim(self.own, up * half, half, 0)
            return send
        if self.late is not None:
            return jnp.concatenate([self.own, self.late], axis=0)
        return self.own

    def move(self, send):
        k = self.steps[0][1]
        perm = [(2 * i + t, 2 * (i ^ self.orders[t][k]) + t) for i in range(self.size) for t in range(2)]
        return lax.ppermute(send, ("dp", "tp"), perm)

    def end(self, got):
        kind, k = self.steps.pop(0)
        if kind in ("full", "join") and self.late is not None:
            rows = self.own.shape[0]
            self.late = self.late + got[rows:]
            got = got[:rows]
        if kind == "join":
            up = self.upper[k]
            self.own = jnp.concatenate([jnp.where(up, got, self.own), jnp.where(up, self.own, got)], axis=0)
        else:
            self.own = self.own + got


class Pair:
    def __init__(self, own, other):
        self.own, self.other = own, other

    def begin(self):
        return self.other

    def move(self, send):
        return lax.ppermute(send, "tp", SWAP)

    def end(self, got):
        self.got = got

    def total(self):
        return self.own + self.got


tie = lax.optimization_barrier


def advance(chains, work=None, *inputs):
    sends, inputs = tie(([c.begin() for c in chains], inputs))
    gots = [c.move(v) for c, v in zip(chains, sends)]
    result = None if work is None else work(*inputs)
    gots, result = tie((gots, result))
    for c, got in zip(chains, gots):
        c.end(got)
    return result


class Flight:
    def __init__(self, chains):
        self.chains, self.sends, self.gots = chains, [c.begin() for c in chains], None

    def beside(self, chains, work, *inputs):
        sends = [c.begin() for c in chains]
        self.sends, sends, inputs = tie((self.sends, sends, inputs))
        if self.gots is None:
            self.gots = [c.move(v) for c, v in zip(self.chains, self.sends)]
        gots = [c.move(v) for c, v in zip(chains, sends)]
        gots, result = tie((gots, work(*inputs)))
        self.last = (gots, result)
        for c, got in zip(chains, gots):
            c.end(got)
        return result

    def land(self):
        self.gots, _ = tie((self.gots, self.last))
        for c, got in zip(self.chains, self.gots):
            c.end(got)


class Slices:
    def __init__(self, chain, count):
        self.chain, self.send, self.gots = chain, chain.begin(), []
        rows = self.send.shape[0]
        self.cuts = [rows * i // count // 8 * 8 for i in range(count)] + [rows]

    def begin(self):
        i = len(self.gots)
        return self.send[self.cuts[i] : self.cuts[i + 1]]

    def move(self, send):
        return self.chain.move(send)

    def end(self, got):
        self.gots.append(got)
        if len(self.gots) + 1 == len(self.cuts):
            self.chain.end(jnp.concatenate(self.gots, axis=0))


def forward(x, pages, rel_index, ta, tb, wa, wb, qva, qvb, pa, pb, w1a, w1b, b1a, b1b, w2a, w2b, ob, gain, shift, go):
    n, qkv, mixed, att, probs, idx = attn_fwd(x, pages, rel_index, ta, tb, wa, wb, qva, qvb, pa, pb, ob, gain, shift)
    act, gm, do, gfa, gfb, gb1, gs2 = ffn(mixed, go, att, w1a, w1b, w2a, w2b, b1a, b1b, pa, pb, gain, shift)
    return idx, mixed, n, qkv, probs, act, gm, do, (gfa, gfb), gb1, gs2


def local_block(x, pages, rel_index, wa, wb, qva, qvb, pa, pb, w1a, w1b, b1a, b1b, w2a, w2b, ob, gain, shift, ta, tb, go):
    idx, mixed, n, qkv, probs, act, gm, do, gf, gb1, gs2 = forward(
        x, pages, rel_index, ta.T, tb.T, wa, wb, qva, qvb, pa, pb, w1a, w1b, b1a, b1b, w2a, w2b, ob, gain, shift, go
    )
    d, t, gqa, gqb, gqv = attn_bwd(n, do, qkv, probs)
    gin, out, sums = (), (), []
    for i in range(3):
        *gin, part = input_grad(i, x, gm, d, wa, wb, gain, *gin)
        sums.append(part)
        out = [out_rows(i, mixed, act, w2a, w2b, ob, *out)]
    own, other = small_sums(idx, t, gs2, *sums, gb1, gqv)
    gin, out = gin[0], out[0]
    return out, gin, gf, finish(gqa, own), finish(gqb, other)


def per_device(
    dp_size, inputs, page_of, rel_index, w_qkv, qv_bias, w_proj, w_fc1, fc1_bias, w_fc2, out_biases, norm_gains,
    norm_biases, bias_table, out_grad,
):
    me = lax.axis_index("tp")
    windows = inputs.shape[0] // WIN
    swap = lambda v: lax.ppermute(v, "tp", SWAP)
    pages = lax.dynamic_slice_in_dim(page_of.reshape(2 * windows, WIN), me * windows, windows, 0)
    pages = jnp.pad(pages.astype(F32), ((0, 0), (0, LANES - WIN)), constant_values=-1.0)[:, None, :]
    table = bias_table.T
    w_qkv_b, qv_bias_b, w_proj_b, table_b = (swap(v) for v in (w_qkv, qv_bias, w_proj, table))
    later, w_qkv_b, qv_bias_b, w_proj_b, table_b, pages = tie(
        ((w_fc1, fc1_bias, w_fc2), w_qkv_b, qv_bias_b, w_proj_b, table_b, pages)
    )
    w_fc1_b, fc1_bias_b, w_fc2_b = (swap(v) for v in later)
    idx, mixed, n, qkv, probs, act, gm, do, gf, gb1, gs2 = forward(
        inputs, pages, rel_index, table, table_b, w_qkv, w_qkv_b, qv_bias, qv_bias_b, w_proj, w_proj_b, w_fc1, w_fc1_b,
        fc1_bias[None], fc1_bias_b[None], w_fc2, w_fc2_b, out_biases, norm_gains, norm_biases, out_grad,
    )
    bits = dp_bits(dp_size)
    turned = bits[1:] + bits[:1]
    mid = len(bits) // 2
    deep = bits[mid:-1] + bits[:mid] + bits[-1:]
    grad = lambda i, *old: (functools.partial(input_grad, i), inputs, gm, d, w_qkv, w_qkv_b, norm_gains) + old
    rows_out = lambda i, *old: (functools.partial(out_rows, i), mixed, act, w_fc2, w_fc2_b, out_biases) + old

    pair = Pair(*gf)
    out = advance([pair], *rows_out(0))
    if SPLIT:
        cut = 1664
        f = [Chain(dp_size, pair.total()[:cut], (bits, turned)), Chain(dp_size, pair.total()[cut:], (deep, deep))]
    else:
        f = [Chain(dp_size, pair.total(), (bits, turned))]
    d, t, gqa, gqb, gqv = advance(f, attn_bwd, n, do, qkv, probs)
    pair = Pair(gqa, gqb)
    gin, gs1a = advance(f + [pair], *grad(0))
    q = Chain(dp_size, pair.total(), (bits, turned))
    gin, gs1b = advance(f + [q], *grad(1, gin))
    gin, gs1c = advance(f + [q], *grad(2, gin))
    flight = Flight(f)
    low = Pair(*flight.beside([], small_sums, idx, t, gs2, gs1a, gs1b, gs1c, gb1, gqv))
    out = flight.beside([q, low], *rows_out(1, out))
    flight.land()
    q.late = low.total()
    while len(f[0].steps) > 1:
        advance(f + [q])
    parts = [Slices(c, max(1, len(q.steps) - 1)) for c in f]
    out = advance(parts + [q], *rows_out(2, out))
    while f[0].steps:
        advance(parts + [q])
    g_f = jnp.concatenate([c.own for c in f])
    g_fc2 = g_f[:1024].astype(F32)
    g_fc1 = jnp.concatenate([g_f[1024:1536], g_f[1536:2048]], axis=1).astype(F32)
    g_proj = g_f[2048:].astype(F32)
    while q.steps:
        advance([q])
    g_qkv, g_qv, g_ob, g_gains, g_shifts, g_fc1_bias, g_table = finish(q.own, q.late)
    return out, gin, g_qkv, g_qv, g_proj, g_fc1, g_fc1_bias.reshape(-1), g_fc2, g_ob, g_gains, g_shifts, g_table.T


def solution(mesh):
    rows = P(("dp", "tp"), None)
    placed = (
        rows, P("dp"), P(), P(None, None, "tp"), P(None, "tp"), P("tp", None), P(None, "tp"), P("tp"),
        P("tp", None), P(), P(), P(), P(None, "tp"), rows,
    )
    results = (
        rows, rows, P(None, None, "tp"), P(None, "tp"), P("tp", None), P(None, "tp"), P("tp"), P("tp", None),
        P(), P(), P(), P(None, "tp"),
    )
    return jax.shard_map(
        functools.partial(per_device, mesh.shape["dp"]), mesh=mesh, in_specs=placed, out_specs=results, check_vma=False
    )
```
